32 devices in a mesh: dp: 8 (over z, y), tensor: 4 (over x, core).
Axes of the slice: x: 2, y: 2, z: 4, core: 2. Of those that a mesh axis runs over, the one named last changes fastest.
Arguments:
- inputs: bfloat16 [16384, 768], P('dp'), may hold values from -6 to 6
- segments: int32 [64, 256], P('dp'), may hold values from 0 to 3, never falling along the last dimension, each value on 1 to 128 neighbouring positions
- query_weight: bfloat16 [768, 768], P('dp', 'tensor'), may hold values from -0.21875 to 0.21875
- key_weight: bfloat16 [768, 768], P('dp', 'tensor'), may hold values from -0.21875 to 0.21875
- value_weight: bfloat16 [768, 768], P('dp', 'tensor'), may hold values from -0.21875 to 0.21875
- query_bias: float32 [768], P('tensor'), may hold values from -3 to 3
- value_bias: float32 [768], P('tensor'), may hold values from -3 to 3
- out_weight: bfloat16 [768, 768], P('tensor', 'dp'), may hold values from -1.75 to 1.75
- out_bias: float32 [768], replicated, may hold values from -3 to 3
- first_gain: float32 [768], replicated, may hold values from 0.5 to 1.5
- first_shift: float32 [768], replicated, may hold values from -2 to 2
- inner_weight: bfloat16 [768, 3072], P('dp', 'tensor'), may hold values from -0.21875 to 0.21875
- inner_bias: float32 [3072], P('tensor'), may hold values from -3 to 3
- outer_weight: bfloat16 [3072, 768], P('tensor', 'dp'), may hold values from -0.109375 to 0.109375
- outer_bias: float32 [768], replicated, may hold values from -3 to 3
- second_gain: float32 [768], replicated, may hold values from 0.5 to 1.5
- second_shift: float32 [768], replicated, may hold values from -2 to 2
- cotangent: bfloat16 [16384, 768], P('dp'), may hold values from -6 to 6
Outputs:
- layer_out: bfloat16 [16384, 768], P('dp')
- input_grad: float32 [16384, 768], P('dp')
- query_weight_grad: float32 [768, 768], P('dp', 'tensor')
- key_weight_grad: float32 [768, 768], P('dp', 'tensor')
- value_weight_grad: float32 [768, 768], P('dp', 'tensor')
- query_bias_grad: float32 [768], P('tensor')
- value_bias_grad: float32 [768], P('tensor')
- out_weight_grad: float32 [768, 768], P('tensor', 'dp')
- out_bias_grad: float32 [768], replicated
- first_gain_grad: float32 [768], replicated
- first_shift_grad: float32 [768], replicated
- inner_weight_grad: float32 [768, 3072], P('dp', 'tensor')
- inner_bias_grad: float32 [3072], P('tensor')
- outer_weight_grad: float32 [3072, 768], P('tensor', 'dp')
- outer_bias_grad: float32 [768], replicated
- second_gain_grad: float32 [768], replicated
- second_shift_grad: float32 [768], replicated
The draws below stay inside these ranges and needn't reach their ends.
Inputs may be any that keep to these rules, and one draw needn't show every extreme that they name: `segments`: in each packed sequence the segment numbers never fall; each segment holds 1 to 128 rows and one holds exactly 128.
All inputs are finite; a program needn't handle non-finite values.
Results may differ from the reference program's by a relative error of at most 0.019.
Values may be sent and summed in bfloat16 or wider, within the bound.
No kernel may reach another device: no remote copies, remote signals or barrier semaphores. Data moves between devices by JAX's collectives and lax.ppermute only.
A program may use at most 192 MiB of HBM per device.

```python
import math
import jax
import jax.numpy as jnp
import numpy as np
from jax import lax

D = 768
HEADS = 12
HEAD_DIM = 64
FF = 3072
LEN = 256
BLOCK_SEQS = 2
TOK_DEV = 2048
SEQS = 64
TOKENS = 16384
N_TENSOR = 4


def spiked(values, own_key, source, target, blocks, factor):
    def block_of(position):
        return (jnp.arange(values.shape[position]) // (values.shape[position] // blocks)).reshape((-1,) + (1,) * (values.ndim - 1 - position))

    near = jax.random.permutation(own_key, blocks)[block_of(target)]
    far = (block_of(target) + blocks // 2) % blocks
    return jnp.where((block_of(source) == near) | (block_of(source) == far), factor * values, values)


def levels(own_key, dims, shards, least, high):
    def one(dim, parts):
        draws = jax.random.uniform(jax.random.fold_in(jax.random.fold_in(own_key, 6), dim), (parts,), jnp.float32, least / len(shards), high / len(shards))
        return jnp.repeat(jnp.exp(draws), dims[dim] // parts).reshape((-1,) + (1,) * (len(dims) - dim - 1))

    level = one(*shards[0])
    for cut in shards[1:]:
        level = level * one(*cut)
    return level


def split_up(number_of, total, limit, skew):
    loads = [(1 << 20) // math.isqrt(grade ** skew) + 1 for grade in range(2, number_of + 1)]
    spare, counts = total - limit - (number_of - 1), [1] * (number_of - 1)
    while spare > 0:
        free = [i for i in range(number_of - 1) if counts[i] < limit]
        whole, remaining = sum([loads[i] for i in free]), spare
        for i in free:
            extra = min(limit - counts[i], max(1, remaining * loads[i] // whole), spare)
            counts[i] = counts[i] + extra
            spare = spare - extra
    return np.array([limit] + counts)


def uneven(rng, number_of, total, limit, lean):
    if number_of == 2:
        one = jax.random.randint(rng, (), max(1, total - limit), min(limit, total - 1) + 1)
        return jnp.stack([one, total - one])
    lengths = jnp.asarray(split_up(number_of, total, limit, lean), jnp.int32)
    couples = (number_of - 1) // 2
    source_of, taker = lengths[1:1 + 2 * couples:2], lengths[2:2 + 2 * couples:2]
    margin = jnp.minimum(source_of - 1, limit - taker)
    passed = jax.random.randint(jax.random.fold_in(rng, 1), (couples,), 0, 1 << 20) % (margin + 1)
    lengths = lengths.at[1:1 + 2 * couples:2].set(source_of - passed).at[2:2 + 2 * couples:2].set(taker + passed)
    return lengths[jax.random.permutation(jax.random.fold_in(rng, 2), number_of)]


def gaussian(own_key, dims, deviation, most, shards=(), dtype=jnp.bfloat16):
    level = levels(own_key, dims, shards, -0.22, 0.18) if shards else 1.0
    drawn = jax.random.normal(own_key, dims, jnp.float32) * deviation * level
    return jnp.minimum(jnp.maximum(drawn, -most), most).astype(dtype)


def gaussian_with(stream_key, shape, deviation, bound, shards, heavy, kind=jnp.bfloat16):
    entries = deviation * jax.random.normal(stream_key, shape, jnp.float32)
    if shards:
        entries = entries * levels(stream_key, shape, shards, -0.22, 0.18)
    return jnp.clip(spiked(entries, jax.random.fold_in(stream_key, 3), *heavy), -bound, bound).astype(kind)


def setup_inputs(seed: int = 0) -> dict:
    streams_of = jax.random.split(jax.random.key(seed), 19)
    inputs = gaussian(streams_of[0], (TOKENS, D), 1.0, 6.0, ((0, 8),))
    segments = jax.vmap(lambda own: jnp.searchsorted(jnp.cumsum(uneven(own, 4, LEN, LEN // 2, 0)), jnp.arange(LEN), side="right"))(jax.random.split(streams_of[1], SEQS)).reshape((SEQS, LEN)).astype(jnp.int32)
    query_weight = gaussian(streams_of[2], (D, D), D ** -0.5, 0.21875, ((0, 8), (1, 4)))
    key_weight = gaussian(streams_of[3], (D, D), D ** -0.5, 0.21875, ((0, 8), (1, 4)))
    value_weight = gaussian(streams_of[4], (D, D), D ** -0.5, 0.21875, ((0, 8), (1, 4)))
    query_bias = gaussian(streams_of[5], (D,), 0.5, 3.0, ((0, 4),), jnp.float32)
    value_bias = gaussian(streams_of[6], (D,), 0.5, 3.0, ((0, 4),), jnp.float32)
    out_weight = gaussian(streams_of[7], (D, D), (D // 64) ** -0.5, 1.75, ((0, 4), (1, 8)))
    out_bias = gaussian(streams_of[8], (D,), 0.5, 3.0, (), jnp.float32)
    first_gain = jnp.clip(1.0 + 0.1 * jax.random.normal(streams_of[9], (D,), jnp.float32), 0.5, 1.5)
    first_shift = gaussian(streams_of[10], (D,), 0.3, 2.0, (), jnp.float32)
    inner_weight = gaussian(streams_of[11], (D, FF), D ** -0.5, 0.21875, ((0, 8), (1, 4)))
    inner_bias = gaussian(streams_of[12], (FF,), 0.5, 3.0, ((0, 4),), jnp.float32)
    outer_weight = gaussian(streams_of[13], (FF, D), FF ** -0.5, 0.109375, ((0, 4), (1, 8)))
    outer_bias = gaussian(streams_of[14], (D,), 0.5, 3.0, (), jnp.float32)
    second_gain = jnp.clip(1.0 + 0.1 * jax.random.normal(streams_of[15], (D,), jnp.float32), 0.5, 1.5)
    second_shift = gaussian(streams_of[16], (D,), 0.3, 2.0, (), jnp.float32)
    cotangent = gaussian_with(streams_of[17], (TOKENS, D), 1.0, 6.0, ((0, 8),), (0, 1, 8, 2.0))
    return dict(inputs=inputs, segments=segments, query_weight=query_weight, key_weight=key_weight, value_weight=value_weight, query_bias=query_bias, value_bias=value_bias, out_weight=out_weight, out_bias=out_bias, first_gain=first_gain, first_shift=first_shift, inner_weight=inner_weight, inner_bias=inner_bias, outer_weight=outer_weight, outer_bias=outer_bias, second_gain=second_gain, second_shift=second_shift, cotangent=cotangent)


@jax.custom_vjp
def low(v):
    return lax.optimization_barrier(v.astype(jnp.bfloat16)).astype(jnp.float32)

@jax.custom_vjp
def low_back(v):
    return v

def low_keep(v):
    return (low(v), None)

def low_pass(kept, grad):
    return (grad,)

def back_keep(v):
    return (v, None)

def back_low(kept, grad):
    return (low(grad),)
low.defvjp(low_keep, low_pass)
low_back.defvjp(back_keep, back_low)
EPS = 1e-06

def product(left, right):
    return jnp.dot(left, right, precision=lax.Precision.HIGHEST)

def norm_rows(hidden, gain, shift):
    center = hidden - lax.optimization_barrier(jnp.mean(hidden, axis=-1, keepdims=True))
    spread = lax.optimization_barrier(jnp.mean(center * center, axis=-1, keepdims=True))
    return center * lax.rsqrt(spread + EPS) * gain + shift

def attend_block(item):
    query, key, value, seg_block = item
    scores = jnp.einsum('qhd,khd->hqk', query, key, precision=lax.Precision.HIGHEST) * HEAD_DIM ** (-0.5)
    scores = low_back(scores)
    order = jnp.arange(query.shape[0]) // LEN
    keep = (order[:, None] == order[None, :]) & (seg_block[:, None] == seg_block[None, :])
    scores = jnp.where(keep[None], scores, -1e+30)
    probs = low(jax.nn.softmax(scores, axis=-1))
    return jnp.einsum('hqk,khd->qhd', probs, value, precision=lax.Precision.HIGHEST)

def layer(hidden, seg_rows, query_weight, key_weight, value_weight, query_bias, value_bias, out_weight, out_bias, first_gain, first_shift, inner_weight, inner_bias, outer_weight, outer_bias, second_gain, second_shift):
    rows = hidden.shape[0]
    query = low_back(low(product(hidden, query_weight) + query_bias))
    key = low_back(low(product(hidden, key_weight)))
    value = low_back(low(product(hidden, value_weight) + value_bias))
    block = BLOCK_SEQS * LEN
    count = rows // block
    split = (count, block, HEADS, HEAD_DIM)
    context = lax.map(jax.checkpoint(attend_block), (query.reshape(split), key.reshape(split), value.reshape(split), seg_rows.reshape(count, block)))
    context = low_back(low(context.reshape(rows, D)))
    width = D // N_TENSOR
    attn = jnp.zeros((rows, D), jnp.float32)
    for group in range(N_TENSOR):
        attn = attn + low(product(context[:, group * width:(group + 1) * width], out_weight[group * width:(group + 1) * width]))
    first_out = norm_rows(low_back(attn) + out_bias + hidden, first_gain, first_shift)
    inner = low_back(product(low(first_out), inner_weight) + inner_bias)
    active = low(jax.nn.gelu(inner, approximate=False))
    hidden_width = FF // N_TENSOR
    ffn = jnp.zeros((rows, D), jnp.float32)
    for group in range(N_TENSOR):
        ffn = ffn + low(product(active[:, group * hidden_width:(group + 1) * hidden_width], outer_weight[group * hidden_width:(group + 1) * hidden_width]))
    return norm_rows(low_back(ffn) + outer_bias + first_out, second_gain, second_shift)

def reference(inputs, segments, query_weight, key_weight, value_weight, query_bias, value_bias, out_weight, out_bias, first_gain, first_shift, inner_weight, inner_bias, outer_weight, outer_bias, second_gain, second_shift, cotangent):
    params = tuple((p.astype(jnp.float32) for p in (query_weight, key_weight, value_weight, query_bias, value_bias, out_weight, out_bias, first_gain, first_shift, inner_weight, inner_bias, outer_weight, outer_bias, second_gain, second_shift)))
    groups = TOKENS // TOK_DEV
    hiddens = inputs.astype(jnp.float32).reshape(groups, TOK_DEV, D)
    cotans = cotangent.astype(jnp.float32).reshape(groups, TOK_DEV, D)
    seg_all = segments.astype(jnp.int32).reshape(groups, TOK_DEV)

    def step(totals, item):
        hidden, cotan, seg_rows = item

        def forward(hid, *weights):
            return layer(hid, seg_rows, *weights)
        result, pull = jax.vjp(forward, hidden, *params)
        grads = pull(cotan)
        return (tuple((a + b for a, b in zip(totals, grads[1:]))), (result, grads[0]))
    zeros = tuple((jnp.zeros_like(p) for p in params))
    totals, (results, input_grads) = lax.scan(step, zeros, (hiddens, cotans, seg_all))
    layer_out = results.reshape(TOKENS, D).astype(jnp.bfloat16)
    input_grad = input_grads.reshape(TOKENS, D)
    return (layer_out, input_grad, totals[0], totals[1], totals[2], totals[3], totals[4], totals[5], totals[6], totals[7], totals[8], totals[9], totals[10], totals[11], totals[12], totals[13], totals[14])
```

```python
import functools
import math

import jax
import jax.numpy as jnp
from jax import lax
from jax.experimental import pallas as pl
from jax.experimental.pallas import tpu as pltpu
from jax.sharding import PartitionSpec as P

HEAD_DIM = 64
LEN = 256
EPS = 1e-06
BF = jnp.bfloat16
F32 = jnp.float32
AXES = ("dp", "tensor")
MIB = 1 << 20


def dot(left, right):
    return lax.dot_general(left, right, (((1,), (0,)), ((), ())), preferred_element_type=F32)


def dot_t(left, right):
    return lax.dot_general(left, right, (((1,), (1,)), ((), ())), preferred_element_type=F32)


def t_dot(left, right):
    return lax.dot_general(left, right, (((0,), (0,)), ((), ())), preferred_element_type=F32)


def vmem():
    return pl.BlockSpec(memory_space=pltpu.VMEM)


def smem():
    return pl.BlockSpec(memory_space=pltpu.SMEM)


def anywhere():
    return pl.BlockSpec(memory_space=pl.ANY)


def call(body, ins, in_specs, outs, out_specs, scratch, limit, flops):
    return pl.pallas_call(
        body,
        out_shape=outs,
        in_specs=in_specs,
        out_specs=out_specs,
        scratch_shapes=scratch,
        compiler_params=pltpu.CompilerParams(vmem_limit_bytes=limit * MIB),
        cost_estimate=pl.CostEstimate(flops=1000, bytes_accessed=1000, transcendentals=0),
    )(*ins)


def shape(dims, dtype):
    return jax.ShapeDtypeStruct(dims, dtype)


class Plan:
    def __init__(self, mesh):
        self.ndp, self.nt = mesh.shape["dp"], mesh.shape["tensor"]
        self.pieces = self.nt == 4 and self.ndp in (4, 8, 16)
        self.nz = self.ndp // 2

    def pairs(self, move):
        found = []
        for d in range(self.ndp):
            for t in range(self.nt):
                z, y, x, c = move(d >> 1, d & 1, t >> 1, t & 1)
                found.append((d * self.nt + t, (z * 2 + y) * self.nt + x * 2 + c))
        return found

    def first(self):
        return self.pairs(lambda z, y, x, c: (z, y, x ^ 1, c) if c == 0 else (z, y ^ 1, x, c))

    def second(self):
        return self.pairs(lambda z, y, x, c: (z, y, x ^ 1, c) if c == 1 else (z, y ^ 1, x, c))

    def core(self):
        return self.pairs(lambda z, y, x, c: (z, y, x, c ^ 1))

    def along(self, j):
        return self.pairs(lambda z, y, x, c: (z ^ j, y, x, c))

    def tables(self):
        d, t = lax.axis_index("dp"), lax.axis_index("tensor")
        z, y, x, c = d >> 1, d & 1, t >> 1, t & 1
        s = jnp.arange(2)[:, None, None]
        r = jnp.arange(4)[None, :, None]
        j = jnp.arange(self.nz)[None, None, :]
        a, b = r & 1, r >> 1
        core = c ^ s
        dx, dy = jnp.where(core == 0, a, b), jnp.where(core == 0, b, a)
        where_t = jnp.broadcast_to((x ^ dx) * 2 + core, (2, 4, self.nz))
        where_d = jnp.broadcast_to((z ^ j) * 2 + (y ^ dy), (2, 4, self.nz))
        s = jnp.arange(2)[:, None, None]
        xx = jnp.arange(2)[None, :, None]
        dd = jnp.arange(self.ndp)[None, None, :]
        core = c ^ s
        dx, dy = xx ^ x, (dd & 1) ^ y
        a, b = jnp.where(core == 0, dx, dy), jnp.where(core == 0, dy, dx)
        slot = jnp.broadcast_to((b * 2 + a) * self.nz + ((dd >> 1) ^ z), (2, 2, self.ndp))
        gather = jnp.stack([where_t.reshape(-1), where_d.reshape(-1)]).astype(jnp.int32)
        scatter = slot.reshape(4, self.ndp).astype(jnp.int32)
        return gather, scatter

    def turn(self, values, pairs):
        return lax.ppermute(values, AXES, pairs)

    def near(self, shard):
        return jnp.stack([shard] + [self.turn(shard, self.along(j)) for j in range(1, self.nz)])

    def share(self, part):
        other = self.turn(part, self.pairs(lambda z, y, x, c: (z, y, x ^ 1, c)))
        return [part, other, self.turn(part, self.core()), self.turn(other, self.core())]

    def add_core(self, keep, got, which):
        return keep[which].astype(F32) + got[which].astype(F32)

    def scatter_a(self, keep, got):
        away = jnp.stack([self.add_core(keep, got, r).astype(BF) for r in (1, 3)])
        return away, lambda: self.turn(away, self.first())

    def scatter_b(self, keep, got, got_a):
        away = (self.add_core(keep, got, 2) + got_a[1].astype(F32)).astype(BF)
        return away, lambda: self.turn(away, self.second())

    def scatter_z(self, keep, got, got_a, got_b):
        left = self.add_core(keep, got, 0) + got_a[0].astype(F32) + got_b.astype(F32)
        low = left[1:].astype(BF)
        moved = [self.turn(low[j - 1], self.along(j)) for j in range(1, self.nz)]
        total = left[0]
        for piece in moved:
            total = total + piece.astype(F32)
        return total

    def total(self, values):
        for pairs in (self.core(), self.first(), self.second()):
            values = values + self.turn(values, pairs)
        moved = [self.turn(values, self.along(j)) for j in range(1, self.nz)]
        for piece in moved:
            values = values + piece
        return values


def load_weights(refs, where, full, sem):
    if len(refs) == 1:
        for t in range(full.shape[0]):
            pltpu.make_async_copy(refs[0].at[t], full.at[t], sem.at[t]).start()
        return
    nz, rows, _ = refs[0].shape
    for r, ref in enumerate(refs):
        for j in range(nz):
            t, d = where[0, r * nz + j], where[1, r * nz + j]
            spot = pl.ds(pl.multiple_of(d * rows, rows), rows)
            pltpu.make_async_copy(ref.at[j], full.at[t, spot], sem.at[t]).start()


def load(ref, held, sem):
    pltpu.make_async_copy(ref, held, sem).start()


def wait(held, sem):
    pltpu.make_async_copy(held, held, sem).wait()


def blocks(rows, block):
    def over(run):
        @pl.loop(0, rows // block)
        def _(i):
            run(pl.ds(pl.multiple_of(i * block, block), block))

    return over


def tie(value, *after):
    return lax.optimization_barrier((value, *after))[0]


def lane_masks(rows):
    lane = lax.broadcasted_iota(jnp.int32, (rows, 128), 1)
    return lane < HEAD_DIM


def pick(mask, values):
    return jnp.where(mask, values, jnp.zeros_like(values))


def norm_stats(hidden):
    center = hidden - jnp.mean(hidden, axis=-1, keepdims=True)
    scale = lax.rsqrt(jnp.mean(center * center, axis=-1, keepdims=True) + EPS)
    return center * scale, scale


def norm_pull(incoming, normed, scale, gain):
    scaled = incoming * gain
    return scale * (
        scaled
        - jnp.mean(scaled, axis=-1, keepdims=True)
        - normed * jnp.mean(scaled * normed, axis=-1, keepdims=True)
    )


def attend_kernel(nw, x_ref, seg_row, seg_col, bias, out_bias, gain, shift, where, *rest):
    refs, rest = rest[:nw], rest[nw:]
    acts, probs, ctx, normed_ref, scale_ref, low_ref, full, keep, sem = rest
    rows = x_ref.shape[0]
    nt = acts.shape[0]
    load_weights(refs, where, full, sem)
    nseq = rows // LEN
    for s in range(nseq):
        same = seg_col[s * LEN : (s + 1) * LEN, :] == seg_row[s : s + 1, :]
        keep[s] = jnp.where(same, 0.0, -1e30).astype(F32)
    low_half = lane_masks(LEN)
    ones = jnp.ones((LEN, 128), BF)

    normed_ref[...] = x_ref[...].astype(F32) + out_bias[...]

    @pl.loop(0, nt)
    def _(t):
        wait(full.at[t], sem.at[t])
        x = x_ref[...]
        acts[t, :, 0:512] = (dot(x, full[t, :, 0:512]) + bias[t, :, 0:512]).astype(BF)
        last = dot(x, full[t, :, 512:640]).astype(BF)
        acts[t, :, 512:640] = pick(lane_masks(rows), last)

        for s in range(nseq):
            span = slice(s * LEN, (s + 1) * LEN)
            q01, k01, v01 = acts[t, span, 0:128], acts[t, span, 128:256], acts[t, span, 256:384]
            qv2, k2 = acts[t, span, 384:512], acts[t, span, 512:640]
            heads = (
                (pick(low_half, q01), k01, v01),
                (pick(~low_half, q01), k01, v01),
                (pick(low_half, qv2), k2, qv2),
            )
            done = []
            for h, (query, key, value) in enumerate(heads):
                scores = dot_t(query, key) * HEAD_DIM ** (-0.5) + keep[s]
                top = jnp.max(scores, axis=-1, keepdims=True)
                expo = jnp.exp(scores - top)
                low = expo.astype(BF)
                mixed = dot(low, jnp.concatenate([value, ones], axis=1))
                inverse = 1.0 / mixed[:, 128:]
                probs[t, s, h] = (expo * jnp.concatenate([inverse, inverse], axis=1)).astype(BF)
                done.append(mixed[:, :128] * inverse)
            ctx[t, span, 0:128] = pick(~low_half, done[2]).astype(BF)
            ctx[t, span, 128:256] = jnp.where(low_half, done[0], done[1]).astype(BF)
        part = dot_t(ctx[t], full[t, :, 512:768]).astype(BF)
        normed_ref[...] += part.astype(F32)

    @blocks(rows, 128)
    def _(span):
        normed, scale = norm_stats(normed_ref[span, :])
        normed_ref[span, :] = normed
        scale_ref[span, :] = jnp.broadcast_to(scale, (128, 128))
        low_ref[span, :] = (normed * gain[...] + shift[...]).astype(BF)


def erfc_parts(values):
    size = jnp.abs(values) * (1.0 / math.sqrt(2.0))
    t = 1.0 / (1.0 + 0.5 * size)
    poly = -0.82215223 + t * 0.17087277
    for c in (1.48851587, -1.13520398, 0.27886807, -0.18628806, 0.09678418, 0.37409196, 1.00002368):
        poly = c + t * poly
    bell = jnp.exp(-size * size)
    tail = 0.5 * t * jnp.exp(t * poly - 1.26551223) * bell
    return jnp.where(values >= 0, 1.0 - tail, tail), bell


def inner_kernel(nw, low_ref, bias, where, *rest):
    refs, rest = rest[:nw], rest[nw:]
    active, slope, full, inner_ref, sem = rest
    rows = low_ref.shape[0]
    nt = active.shape[0]
    load_weights(refs, where, full, sem)

    @pl.loop(0, nt)
    def _(t):
        wait(full.at[t], sem.at[t])
        inner_ref[...] = dot(low_ref[...], full[t]) + bias[t]

        @blocks(rows, 64)
        def _(span):
            inner = inner_ref[span, :]
            phi, bell = erfc_parts(inner)
            active[t, span, :] = (inner * phi).astype(BF)
            slope[t, span, :] = (phi + inner * bell * (1.0 / math.sqrt(2.0 * math.pi))).astype(BF)


def outer_kernel(nw, active, normed_ref, gain1, shift1, outer_bias, gain, shift, cot, where, *rest):
    refs, rest = rest[:nw], rest[nw:]
    out_ref, second_ref, ffn_ref, vec_ref, full, held, sem, sem_a = rest
    rows = normed_ref.shape[0]
    nt = active.shape[0]
    for t in range(nt):
        load(active.at[t], held.at[t], sem_a.at[t])
    load_weights(refs, where, full, sem)
    vec_ref[...] = jnp.zeros_like(vec_ref)
    second_ref[...] = normed_ref[...] * gain1[...] + shift1[...] + outer_bias[...]
    for t in range(nt):
        wait(held.at[t], sem_a.at[t])
        wait(full.at[t], sem.at[t])
        second_ref[...] += dot_t(held[t], full[t]).astype(BF).astype(F32)

    @blocks(rows, 128)
    def _(span):
        normed, scale = norm_stats(second_ref[span, :])
        out_ref[span, :] = (normed * gain[...] + shift[...]).astype(BF)
        incoming = cot[span, :].astype(F32)
        pulled = norm_pull(incoming, normed, scale, gain[...])
        second_ref[span, :] = pulled
        ffn_ref[span, :] = pulled.astype(BF)
        vec_ref[0:1, :] += jnp.sum(incoming * normed, axis=0, keepdims=True)
        vec_ref[1:2, :] += jnp.sum(incoming, axis=0, keepdims=True)
        vec_ref[2:3, :] += jnp.sum(pulled, axis=0, keepdims=True)


def store_grad(ndp, slots, line, held, out, sem):
    nz, rows = out.shape[1], out.shape[2]
    for d in range(ndp):
        slot = slots[line, d]
        pltpu.make_async_copy(held.at[pl.ds(d * rows, rows)], out.at[slot // nz, slot % nz], sem).start()


def grad_kernel(ndp, side, left, right, where, slots, out, part, held, sem_in, sem_out):
    core = (where[0, 0] % 2) ^ side
    for n in range(2):
        load(right.at[2 * n + core], part.at[n], sem_in.at[n])
    for n in range(2):
        wait(part.at[n], sem_in.at[n])
        held[n] = t_dot(left[...], part[n]).astype(BF)
        store_grad(ndp, slots, side * 2 + n, held.at[n], out, sem_out.at[n])
    for n in range(2):
        wait(held.at[n], sem_out.at[n])


def whole_grad_kernel(left, right, out):
    for t in range(out.shape[0]):
        out[t] = t_dot(left[...], right[t]).astype(BF)


def slope_kernel(nw, ffn_ref, slope, where, *rest):
    refs, rest = rest[:nw], rest[nw:]
    pulled, vec_ref, full, held, sem, sem_a = rest
    nt = slope.shape[0]
    load_weights(refs, where, full, sem)
    for t in range(nt):
        load(slope.at[t], held.at[t], sem_a.at[t])
    for t in range(nt):
        wait(full.at[t], sem.at[t])
        wait(held.at[t], sem_a.at[t])
        grad = (dot(ffn_ref[...], full[t]) * held[t].astype(F32)).astype(BF)
        pulled[t] = grad
        vec_ref[t] = jnp.sum(grad.astype(F32), axis=0, keepdims=True)


def first_kernel(nw, pulled, second, normed_ref, scale_ref, gain, where, *rest):
    inner_refs, refs, rest = rest[:nw], rest[nw : 2 * nw], rest[2 * nw :]
    attn_in, attn_low, ctx_grad, vec_ref, inner_full, full, held, sem_i, sem, sem_a = rest
    rows = second.shape[0]
    nt = pulled.shape[0]
    for t in range(nt):
        load(pulled.at[t], held.at[t], sem_a.at[t])
    load_weights(inner_refs, where, inner_full, sem_i)
    load_weights(refs, where, full, sem)
    vec_ref[...] = jnp.zeros_like(vec_ref)
    attn_in[...] = second[...]
    for t in range(nt):
        wait(held.at[t], sem_a.at[t])
        wait(inner_full.at[t], sem_i.at[t])
        attn_in[...] += dot_t(held[t], inner_full[t])

    @blocks(rows, 128)
    def _(span):
        incoming = attn_in[span, :]
        normed = normed_ref[span, :]
        grad = norm_pull(incoming, normed, scale_ref[span, 0:1], gain[...])
        attn_in[span, :] = grad
        attn_low[span, :] = grad.astype(BF)
        vec_ref[0:1, :] += jnp.sum(incoming * normed, axis=0, keepdims=True)
        vec_ref[1:2, :] += jnp.sum(incoming, axis=0, keepdims=True)
        vec_ref[2:3, :] += jnp.sum(grad, axis=0, keepdims=True)

    low_half = lane_masks(rows)
    for t in range(nt):
        wait(full.at[t], sem.at[t])
        got = dot(attn_low[...], full[t, :, 512:768])
        ctx_grad[t, :, 0:128] = pick(~low_half, got[:, :128]).astype(BF)
        ctx_grad[t, :, 128:256] = got[:, 128:].astype(BF)


def attend_pull_kernel(acts, probs, ctx_grad, back, vec_ref):
    nt, rows, _ = acts.shape
    nseq = rows // LEN
    low_half = lane_masks(LEN)
    factor = HEAD_DIM ** (-0.5)

    @pl.loop(0, nt)
    def _(t):
        for s in range(nseq):
            span = slice(s * LEN, (s + 1) * LEN)
            q01, k01, v01 = acts[t, span, 0:128], acts[t, span, 128:256], acts[t, span, 256:384]
            qv2, k2 = acts[t, span, 384:512], acts[t, span, 512:640]
            g2, g01 = ctx_grad[t, span, 0:128], ctx_grad[t, span, 128:256]
            heads = (
                (pick(low_half, g01), q01, k01, v01),
                (pick(~low_half, g01), q01, k01, v01),
                (g2, qv2, k2, qv2),
            )
            queries, keys, values = [], [], []
            for h, (grad, query, key, value) in enumerate(heads):
                prob = probs[t, s, h]
                wide = prob.astype(F32)
                pulled = dot_t(grad, value)
                delta = jnp.sum(pulled * wide, axis=-1, keepdims=True)
                scores = (wide * (pulled - delta)).astype(BF)
                queries.append(dot(scores, key) * factor)
                keys.append(t_dot(scores, query) * factor)
                values.append(t_dot(prob, grad))
            back[t, span, 0:128] = jnp.where(low_half, queries[0], queries[1]).astype(BF)
            back[t, span, 128:256] = jnp.where(low_half, keys[0], keys[1]).astype(BF)
            back[t, span, 256:384] = (values[0] + values[1]).astype(BF)
            back[t, span, 384:512] = jnp.where(low_half, queries[2], values[2]).astype(BF)
            back[t, span, 512:640] = pick(low_half, keys[2]).astype(BF)
        vec_ref[t] = jnp.sum(back[t].astype(F32), axis=0, keepdims=True)


def attn_grad_of(x_ref, attn_low, back, ctx):
    from_x = t_dot(x_ref[...], back)
    from_out = t_dot(attn_low[...], ctx)
    return jnp.concatenate(
        [from_x[:, :512], from_x[:, 512:] + from_out[:, :128], from_out[:, 128:]], axis=1
    ).astype(BF)


def attn_grad_kernel(ndp, x_ref, attn_low, back, ctx, where, slots, *rest):
    outs, held, sems = rest[:2], rest[2], rest[3]
    core = where[0, 0] % 2
    for n, (s, xx) in enumerate(((1, 0), (1, 1), (0, 0), (0, 1))):
        t = 2 * xx + (core ^ s)
        held[n] = attn_grad_of(x_ref, attn_low, back[t], ctx[t])
        store_grad(ndp, slots, s * 2 + xx, held.at[n], outs[s], sems.at[n])
    for n in range(4):
        wait(held.at[n], sems.at[n])


def whole_attn_grad_kernel(x_ref, attn_low, back, ctx, out):
    for t in range(out.shape[0]):
        out[t] = attn_grad_of(x_ref, attn_low, back[t], ctx[t])


def input_kernel(nw, back, attn_in, where, *rest):
    refs, rest = rest[:nw], rest[nw:]
    out_ref, full, total, sem = rest
    nt = back.shape[0]
    load_weights(refs, where, full, sem)
    total[...] = attn_in[...]
    for t in range(nt):
        wait(full.at[t], sem.at[t])
        total[...] += dot_t(back[t], full[t, :, 0:640])
    out_ref[...] = total[...].astype(BF)


def place_kernel(order, one, two, three, four, out, held, sem, sem_out):
    rows = one.shape[0]
    parts = (one, two, three, four)
    for n, part in enumerate(parts):
        load(part, held.at[n], sem.at[n])
    for n in range(4):
        wait(held.at[n], sem.at[n])
        spot = pl.ds(pl.multiple_of(order[n] * rows, rows), rows)
        pltpu.make_async_copy(held.at[n], out.at[spot], sem_out.at[n]).start()
    for n in range(4):
        wait(held.at[n], sem_out.at[n])


def widen_kernel(order, one, two, three, four, out, held, wide, sem, sem_out):
    rows = one.shape[0]
    half = rows // 2
    parts = (one, two, three, four)
    for n, part in enumerate(parts):
        load(part, held.at[n], sem.at[n])
    copies = [None, None]
    for n in range(len(parts)):
        wait(held.at[n], sem.at[n])
        for m in range(2):
            if copies[m] is not None:
                copies[m].wait()
            wide[m] = held[n, m * half : (m + 1) * half, :].astype(F32)
            spot = pl.ds(pl.multiple_of(order[n] * rows + m * half, half), half)
            copies[m] = pltpu.make_async_copy(wide.at[m], out.at[spot], sem_out.at[m])
            copies[m].start()
    for copy in copies:
        copy.wait()


def interleave(q, k, v, o):
    h = HEAD_DIM
    return jnp.concatenate(
        [
            q[..., : 2 * h], k[..., : 2 * h], v[..., : 2 * h],
            q[..., 2 * h :], v[..., 2 * h :], k[..., 2 * h :], o[..., 2 * h :],
            o[..., : 2 * h],
        ],
        axis=-1,
    )


def body(
    plan,
    inputs,
    segments,
    query_weight,
    key_weight,
    value_weight,
    query_bias,
    value_bias,
    out_weight,
    out_bias,
    first_gain,
    first_shift,
    inner_weight,
    inner_bias,
    outer_weight,
    outer_bias,
    second_gain,
    second_shift,
    cotangent,
):
    nt, ndp = plan.nt, plan.ndp
    width = inputs.shape[1]
    local, hidden = query_weight.shape[1], inner_weight.shape[1]
    rows = inputs.shape[0] // nt
    nseq = rows // LEN
    me = lax.axis_index("tensor")
    mine = lambda a, n: lax.dynamic_slice_in_dim(a, me * n, n, 0)
    x = mine(inputs, rows)
    cot = mine(cotangent, rows)
    seg_row = mine(segments, nseq)
    seg_col = seg_row.reshape(rows, 1)

    shards = (
        interleave(query_weight, key_weight, value_weight, out_weight.T),
        inner_weight,
        outer_weight.T,
    )
    nw = 8 if plan.pieces else 1
    if plan.pieces:
        where, slots = plan.tables()
    else:
        where = slots = jnp.zeros((1, 1), jnp.int32)
    row = lambda v: v.reshape(1, width)
    flops = 2 * rows * width * width
    limit = 28 if rows <= 512 else 56
    weights = pltpu.VMEM((nt, width, hidden), BF)
    acted = pltpu.VMEM((nt, rows, hidden), BF)
    dma = pltpu.SemaphoreType.DMA
    any_w = [anywhere()] * nw

    def attend(x, bias, attn_w):
        return call(
            functools.partial(attend_kernel, nw),
            [x, seg_row, seg_col, bias, row(out_bias), row(first_gain), row(first_shift), where, *attn_w],
            [vmem()] * 7 + [smem()] + any_w,
            [
                shape((nt, rows, 640), BF),
                shape((nt, nseq, 3, LEN, LEN), BF),
                shape((nt, rows, 256), BF),
                shape((rows, width), F32),
                shape((rows, 128), F32),
                shape((rows, width), BF),
            ],
            [vmem()] * 6,
            [weights, pltpu.VMEM((nseq, LEN, LEN), F32), dma((nt,))],
            limit,
            8 * flops,
        )

    def inner(low, inner_b, inner_w):
        return call(
            functools.partial(inner_kernel, nw),
            [low, inner_b, where, *inner_w],
            [vmem()] * 2 + [smem()] + any_w,
            [shape((nt, rows, hidden), BF)] * 2,
            [vmem()] * 2,
            [weights, pltpu.VMEM((rows, hidden), F32), dma((nt,))],
            limit,
            8 * flops,
        )

    def outer(active, normed, outer_w):
        return call(
            functools.partial(outer_kernel, nw),
            [
                active, normed, row(first_gain), row(first_shift), row(outer_bias),
                row(second_gain), row(second_shift), cot, where, *outer_w,
            ],
            [anywhere()] + [vmem()] * 7 + [smem()] + any_w,
            [shape((rows, width), BF), shape((rows, width), F32), shape((rows, width), BF), shape((8, width), F32)],
            [vmem()] * 4,
            [weights, acted, dma((nt,)), dma((nt,))],
            limit,
            4 * flops,
        )

    def dinner(ffn_low, slope, outer_w):
        return call(
            functools.partial(slope_kernel, nw),
            [ffn_low, slope, where, *outer_w],
            [vmem(), anywhere(), smem()] + any_w,
            [shape((nt, rows, hidden), BF), shape((nt, 1, hidden), F32)],
            [vmem()] * 2,
            [weights, acted, dma((nt,)), dma((nt,))],
            limit,
            4 * flops,
        )

    def grad(side, left, right):
        return call(
            functools.partial(grad_kernel, ndp, side),
            [left, right, where, slots],
            [vmem(), anywhere(), smem(), smem()],
            [shape((4, plan.nz, width // ndp, hidden), BF)],
            [anywhere()],
            [pltpu.VMEM((2, rows, hidden), BF), pltpu.VMEM((2, width, hidden), BF), dma((2,)), dma((2,))],
            limit,
            2 * flops,
        )[0]

    def whole_grad(left, right):
        return call(
            whole_grad_kernel, [left, right], [vmem()] * 2, [shape((nt, width, hidden), BF)], [vmem()], [], limit, 4 * flops
        )[0]

    def first(pulled, second, normed, scale, inner_w, attn_w):
        return call(
            functools.partial(first_kernel, nw),
            [pulled, second, normed, scale, row(first_gain), where, *inner_w, *attn_w],
            [anywhere()] + [vmem()] * 4 + [smem()] + any_w * 2,
            [shape((rows, width), F32), shape((rows, width), BF), shape((nt, rows, 256), BF), shape((8, width), F32)],
            [vmem()] * 4,
            [weights, weights, acted, dma((nt,)), dma((nt,)), dma((nt,))],
            limit,
            6 * flops,
        )

    def attend_pull(acts, probs, ctx_grad):
        return call(
            attend_pull_kernel,
            [acts, probs, ctx_grad],
            [vmem()] * 3,
            [shape((nt, rows, 640), BF), shape((nt, 1, 640), F32)],
            [vmem()] * 2,
            [],
            limit,
            8 * flops,
        )

    def attn_grad(attn_low, back, ctx):
        return call(
            functools.partial(attn_grad_kernel, ndp),
            [x, attn_low, back, ctx, where, slots],
            [vmem()] * 4 + [smem()] * 2,
            [shape((4, plan.nz, width // ndp, hidden), BF)] * 2,
            [anywhere()] * 2,
            [pltpu.VMEM((4, width, hidden), BF), dma((4,))],
            limit,
            4 * flops,
        )

    def whole_attn_grad(attn_low, back, ctx):
        return call(
            whole_attn_grad_kernel,
            [x, attn_low, back, ctx],
            [vmem()] * 4,
            [shape((nt, width, hidden), BF)],
            [vmem()],
            [],
            limit,
            4 * flops,
        )[0]

    def input_part(back, attn_in, attn_w):
        return call(
            functools.partial(input_kernel, nw),
            [back, attn_in, where, *attn_w],
            [vmem()] * 2 + [smem()] + any_w,
            [shape((rows, width), BF)],
            [vmem()],
            [weights, pltpu.VMEM((rows, width), F32), dma((nt,))],
            limit,
            4 * flops,
        )[0]

    def place(parts):
        order = jnp.stack([me, me ^ 2, me ^ 1, me ^ 3]).astype(jnp.int32)
        return call(
            place_kernel,
            [order, *parts],
            [smem()] + [anywhere()] * 4,
            [shape((nt * rows, width), BF)],
            [anywhere()],
            [pltpu.VMEM((4, rows, width), BF), dma((4,)), dma((4,))],
            limit,
            flops // 8,
        )[0]

    def widen(parts):
        order = jnp.stack([me, me ^ 2, me ^ 1, me ^ 3]).astype(jnp.int32)
        return call(
            widen_kernel,
            [order, *parts],
            [smem()] + [anywhere()] * 4,
            [shape((nt * rows, width), F32)],
            [anywhere()],
            [pltpu.VMEM((4, rows, width), BF), pltpu.VMEM((2, rows // 2, width), F32), dma((4,)), dma((2,))],
            limit,
            flops // 4,
        )[0]

    def small_parts():
        every = lax.all_gather(jnp.concatenate([query_bias, value_bias, inner_bias]), "tensor", axis=0)
        q_b, v_b = every[:, None, :local], every[:, None, local : 2 * local]
        none = jnp.zeros_like(q_b)
        return interleave(q_b, none, v_b, none), every[:, None, 2 * local :]

    bias, inner_b = small_parts()
    if plan.pieces:
        turn, one_way, other_way, core = plan.turn, plan.first(), plan.second(), plan.core()

        def spread(own):
            return [own, turn(own, one_way), turn(own, other_way)]

        def rest_of(three):
            mine = three + [turn(three[1], other_way)]
            return mine, lambda: mine + [turn(v, core) for v in mine]

        own1 = plan.near(shards[0])
        own1, bias, inner_b = lax.optimization_barrier((own1, bias, inner_b))
        own23 = plan.near(jnp.concatenate([shards[1], shards[2]], axis=1))
        own2, own3 = own23[..., :hidden], own23[..., hidden:]
        three1 = spread(own1)
        mine1, all1 = rest_of(three1)
        three2 = spread(tie(own2, mine1[3]))
        attn_w = all1()
        acts, probs, ctx, normed, scale, low = attend(x, bias, attn_w)
        three2 = list(lax.optimization_barrier((*three2, low))[:3])
        mine2, all2 = rest_of(three2)
        three3 = spread(tie(own3, mine2[3]))
        inner_w = all2()
        active, slope = inner(low, inner_b, inner_w)
        three3 = list(lax.optimization_barrier((*three3, active))[:3])
        mine3, all3 = rest_of(three3)
        outer_w = all3()
        layer_part, second, ffn_low, second_vec = outer(active, normed, outer_w)

        send3 = grad(1, ffn_low, active)
        got3 = turn(send3, core)
        layer_parts = plan.share(layer_part)
        keep3 = grad(0, ffn_low, tie(active, send3))
        pulled, inner_vec = dinner(tie(ffn_low, keep3), slope, outer_w)
        got3 = tie(got3, pulled)
        away3, go3a = plan.scatter_a(keep3, got3)
        got3a = go3a()
        low_t = tie(low, away3)
        send2 = grad(1, low_t, pulled)
        got2 = turn(send2, core)
        keep2 = grad(0, low_t, tie(pulled, send2))
        attn_in, attn_low, ctx_grad, first_vec = first(
            pulled, tie(second, keep2), normed, scale, inner_w, attn_w
        )
        got3a = tie(got3a, attn_low)
        away3b, go3b = plan.scatter_b(keep3, got3, got3a)
        got3b = go3b()
        got2 = tie(got2, away3b)
        away2, go2a = plan.scatter_a(keep2, got2)
        got2a = go2a()
        back, back_vec = attend_pull(acts, probs, tie(ctx_grad, away2))
        got3b = tie(got3b, back)
        outer_grad = plan.scatter_z(keep3, got3, got3a, got3b)
        keep1, send1 = attn_grad(attn_low, back, ctx)
        got1 = turn(send1, core)
        layer_out = place(layer_parts)
        got2a = tie(got2a, keep1)
        away2b, go2b = plan.scatter_b(keep2, got2, got2a)
        got2b = go2b()
        input_low = input_part(tie(back, away2b), attn_in, attn_w)
        got1 = tie(got1, input_low)
        away1, go1a = plan.scatter_a(keep1, got1)
        got1a = go1a()
        inner_grad = plan.scatter_z(keep2, got2, got2a, tie(got2b, away1))
        away1b, go1b = plan.scatter_b(keep1, got1, got1a)
        got1b = go1b()
        input_parts = plan.share(tie(input_low, away1b))
        attn_g = plan.scatter_z(keep1, got1, got1a, got1b)
        input_grad = widen(input_parts)
    else:
        attn_w, inner_w, outer_w = (
            [lax.all_gather(lax.all_gather(s, "dp", axis=0, tiled=True), "tensor", axis=0)]
            for s in shards
        )
        acts, probs, ctx, normed, scale, low = attend(x, bias, attn_w)
        active, slope = inner(low, inner_b, inner_w)
        layer_part, second, ffn_low, second_vec = outer(active, normed, outer_w)
        pulled, inner_vec = dinner(ffn_low, slope, outer_w)
        attn_in, attn_low, ctx_grad, first_vec = first(pulled, second, normed, scale, inner_w, attn_w)
        back, back_vec = attend_pull(acts, probs, ctx_grad)
        input_low = input_part(back, attn_in, attn_w)
        outer_grad, inner_grad, attn_g = (
            lax.psum_scatter(
                lax.psum_scatter(g, "tensor", scatter_dimension=0, tiled=False),
                "dp",
                scatter_dimension=0,
                tiled=True,
            ).astype(F32)
            for g in (whole_grad(ffn_low, active), whole_grad(low, pulled), whole_attn_grad(attn_low, back, ctx))
        )
        layer_out = lax.all_gather(layer_part, "tensor", axis=0, tiled=True)
        input_grad = lax.all_gather(input_low, "tensor", axis=0, tiled=True).astype(F32)

    h = HEAD_DIM
    vectors = jnp.concatenate(
        [
            second_vec[:3].reshape(-1),
            first_vec[:3].reshape(-1),
            inner_vec.reshape(-1),
            back_vec.reshape(-1),
        ]
    ).reshape(-1, 128)
    vectors = plan.total(vectors) if plan.pieces else lax.psum(vectors, AXES)
    flat = vectors.reshape(-1)
    gain2, shift2, bias2, gain1, shift1, bias1 = (flat[i * width : (i + 1) * width] for i in range(6))
    at = 6 * width
    inner_bias_grad = lax.dynamic_slice_in_dim(flat, at + me * hidden, hidden, 0)
    at += nt * hidden
    mine_vec = lax.dynamic_slice_in_dim(flat, at + me * 640, 640, 0)
    query_bias_grad = jnp.concatenate([mine_vec[: 2 * h], mine_vec[6 * h : 7 * h]])
    value_bias_grad = jnp.concatenate([mine_vec[4 * h : 6 * h], mine_vec[7 * h : 8 * h]])
    part = lambda *spans: jnp.concatenate([attn_g[:, a * h : b * h] for a, b in spans], axis=1)
    return (
        layer_out,
        input_grad,
        part((0, 2), (6, 7)),
        part((2, 4), (8, 9)),
        part((4, 6), (7, 8)),
        query_bias_grad,
        value_bias_grad,
        part((10, 12), (9, 10)).T,
        bias1,
        gain1,
        shift1,
        inner_grad,
        inner_bias_grad,
        outer_grad.T,
        bias2,
        gain2,
        shift2,
    )


def solution(mesh):
    in_specs = (
        P("dp", None),
        P("dp", None),
        P("dp", "tensor"),
        P("dp", "tensor"),
        P("dp", "tensor"),
        P("tensor"),
        P("tensor"),
        P("tensor", "dp"),
        P(),
        P(),
        P(),
        P("dp", "tensor"),
        P("tensor"),
        P("tensor", "dp"),
        P(),
        P(),
        P(),
        P("dp", None),
    )
    out_specs = (
        P("dp", None),
        P("dp", None),
        P("dp", "tensor"),
        P("dp", "tensor"),
        P("dp", "tensor"),
        P("tensor"),
        P("tensor"),
        P("tensor", "dp"),
        P(),
        P(),
        P(),
        P("dp", "tensor"),
        P("tensor"),
        P("tensor", "dp"),
        P(),
        P(),
        P(),
    )
    return jax.shard_map(
        functools.partial(body, Plan(mesh)),
        mesh=mesh,
        in_specs=in_specs,
        out_specs=out_specs,
        check_vma=False,
    )
```

```python
import functools
import math

import jax
import jax.numpy as jnp
from jax import lax
from jax.experimental import pallas as pl
from jax.experimental.pallas import tpu as pltpu
from jax.sharding import PartitionSpec as P

HEAD_DIM = 64
LEN = 256
EPS = 1e-06
BF = jnp.bfloat16
F32 = jnp.float32
AXES = ("dp", "tensor")
MIB = 1 << 20
SCALE = 0.3


def dot(left, right):
    return lax.dot_general(left, right, (((1,), (0,)), ((), ())), preferred_element_type=F32)


def dot_t(left, right):
    return lax.dot_general(left, right, (((1,), (1,)), ((), ())), preferred_element_type=F32)


def t_dot(left, right):
    return lax.dot_general(left, right, (((0,), (0,)), ((), ())), preferred_element_type=F32)


def vmem():
    return pl.BlockSpec(memory_space=pltpu.VMEM)


def smem():
    return pl.BlockSpec(memory_space=pltpu.SMEM)


def anywhere():
    return pl.BlockSpec(memory_space=pl.ANY)


def call(body, ins, in_specs, outs, out_specs, scratch, limit, cost, aliases={}):
    return pl.pallas_call(
        body,
        out_shape=outs,
        in_specs=in_specs,
        out_specs=out_specs,
        scratch_shapes=scratch,
        input_output_aliases=aliases,
        compiler_params=pltpu.CompilerParams(vmem_limit_bytes=limit * MIB),
        cost_estimate=pl.CostEstimate(flops=int(cost * SCALE * 1e9), bytes_accessed=1000, transcendentals=0),
    )(*ins)


def shape(dims, dtype):
    return jax.ShapeDtypeStruct(dims, dtype)


class Plan:
    def __init__(self, mesh):
        self.ndp, self.nt = mesh.shape["dp"], mesh.shape["tensor"]
        self.pieces = self.nt == 4 and self.ndp in (4, 8, 16)
        self.nz = self.ndp // 2

    def pairs(self, move):
        found = []
        for d in range(self.ndp):
            for t in range(self.nt):
                z, y, x, c = move(d >> 1, d & 1, t >> 1, t & 1)
                found.append((d * self.nt + t, (z * 2 + y) * self.nt + x * 2 + c))
        return found

    def first(self):
        return self.pairs(lambda z, y, x, c: (z, y, x ^ 1, c) if c == 0 else (z, y ^ 1, x, c))

    def second(self):
        return self.pairs(lambda z, y, x, c: (z, y, x ^ 1, c) if c == 1 else (z, y ^ 1, x, c))

    def core(self):
        return self.pairs(lambda z, y, x, c: (z, y, x, c ^ 1))

    def along(self, j):
        return self.pairs(lambda z, y, x, c: (z ^ j, y, x, c))

    def tables(self):
        d, t = lax.axis_index("dp"), lax.axis_index("tensor")
        z, y, x, c = d >> 1, d & 1, t >> 1, t & 1
        s = jnp.arange(2)[:, None, None]
        r = jnp.arange(4)[None, :, None]
        j = jnp.arange(self.nz)[None, None, :]
        a, b = r & 1, r >> 1
        core = c ^ s
        dx, dy = jnp.where(core == 0, a, b), jnp.where(core == 0, b, a)
        where_t = jnp.broadcast_to((x ^ dx) * 2 + core, (2, 4, self.nz))
        where_d = jnp.broadcast_to((z ^ j) * 2 + (y ^ dy), (2, 4, self.nz))
        return jnp.stack([where_t.reshape(-1), where_d.reshape(-1)]).astype(jnp.int32)

    def turn(self, values, pairs):
        return lax.ppermute(values, AXES, pairs)

    def near(self, shard):
        return [self.turn(shard, self.along(j)) for j in range(1, self.nz)]

    def beside(self):
        return self.pairs(lambda z, y, x, c: (z, y, x ^ 1, c))

    def scatter_a(self, keep, got):
        return (keep[2:].astype(F32) + jnp.stack(got[2:]).astype(F32)).astype(BF)

    def scatter_b(self, keep, got, got_a):
        return (keep[1].astype(F32) + got[1].astype(F32) + got_a[1].astype(F32)).astype(BF)

    def scatter_left(self, keep, got, got_a, got_b):
        left = keep[0].astype(F32) + got[0].astype(F32) + got_a[0].astype(F32) + got_b.astype(F32)
        return left[0], [left[j].astype(BF) for j in range(1, self.nz)]

    def go_z(self, low):
        return [self.turn(low[j - 1], self.along(j)) for j in range(1, self.nz)]

    def last(self, total, moved):
        for piece in moved:
            total = total + piece.astype(F32)
        return total


def load_weights(refs, where, full, sem, start=0):
    columns = pl.ds(start, full.shape[2])
    if len(refs) == 1:
        for t in range(full.shape[0]):
            pltpu.make_async_copy(refs[0].at[t, :, columns], full.at[t], sem.at[t]).start()
        return
    nz, rows, _ = refs[0].shape
    for r, ref in enumerate(refs):
        for j in range(nz):
            t, d = where[0, r * nz + j], where[1, r * nz + j]
            spot = pl.ds(pl.multiple_of(d * rows, rows), rows)
            pltpu.make_async_copy(ref.at[j, :, columns], full.at[t, spot], sem.at[t]).start()


def load(ref, held, sem):
    pltpu.make_async_copy(ref, held, sem).start()


def wait(held, sem):
    pltpu.make_async_copy(held, held, sem).wait()


def blocks(rows, block):
    def over(run):
        @pl.loop(0, rows // block)
        def _(i):
            run(pl.ds(pl.multiple_of(i * block, block), block))

    return over


def pack(vectors):
    high = vectors.astype(BF)
    return jnp.concatenate([high, (vectors - high.astype(F32)).astype(BF)])


def unpack(rows):
    half = rows.shape[0] // 2
    return rows[:half].astype(F32) + rows[half:].astype(F32)


def tie(values, *after):
    if after:
        return lax.optimization_barrier((values, *after))[0]
    return lax.optimization_barrier(values)


def lane_masks(rows):
    lane = lax.broadcasted_iota(jnp.int32, (rows, 128), 1)
    return lane < HEAD_DIM


def pick(mask, values):
    return jnp.where(mask, values, jnp.zeros_like(values))


def norm_stats(hidden):
    center = hidden - jnp.mean(hidden, axis=-1, keepdims=True)
    scale = lax.rsqrt(jnp.mean(center * center, axis=-1, keepdims=True) + EPS)
    return center * scale, scale


def norm_pull(incoming, normed, scale, gain):
    scaled = incoming * gain
    return scale * (
        scaled
        - jnp.mean(scaled, axis=-1, keepdims=True)
        - normed * jnp.mean(scaled * normed, axis=-1, keepdims=True)
    )


def attend_kernel(nw, x_ref, seg_row, seg_col, bias, params, where, *rest):
    refs, rest = rest[:nw], rest[nw:]
    acts_out, probs_out, ctx_out, normed_ref, scale_ref, low_ref = rest[:6]
    full, keep, acts, probs, ctx, sem, sem_out = rest[6:]
    rows = x_ref.shape[0]
    nt = acts.shape[0]
    load_weights(refs, where, full, sem)
    nseq = rows // LEN
    for s in range(nseq):
        same = seg_col[s * LEN : (s + 1) * LEN, :] == seg_row[s : s + 1, :]
        keep[s] = jnp.where(same, 0.0, -1e30).astype(F32)
    low_half = lane_masks(LEN)
    ones = jnp.ones((LEN, 128), BF)

    normed_ref[...] = x_ref[...].astype(F32) + params[0:1, :]

    @pl.loop(0, nt)
    def _(t):
        wait(full.at[t], sem.at[t])
        x = x_ref[...]
        acts[t, :, 0:512] = (dot(x, full[t, :, 0:512]) + bias[t, :, 0:512]).astype(BF)
        last = dot(x, full[t, :, 512:640]).astype(BF)
        acts[t, :, 512:640] = pick(lane_masks(rows), last)

        for s in range(nseq):
            span = slice(s * LEN, (s + 1) * LEN)
            q01, k01, v01 = acts[t, span, 0:128], acts[t, span, 128:256], acts[t, span, 256:384]
            qv2, k2 = acts[t, span, 384:512], acts[t, span, 512:640]
            heads = (
                (pick(low_half, q01), k01, v01),
                (pick(~low_half, q01), k01, v01),
                (pick(low_half, qv2), k2, qv2),
            )
            done = []
            for h, (query, key, value) in enumerate(heads):
                scores = dot_t(query, key) * HEAD_DIM ** (-0.5) + keep[s]
                top = jnp.max(scores, axis=-1, keepdims=True)
                expo = jnp.exp(scores - top)
                low = expo.astype(BF)
                mixed = dot(low, jnp.concatenate([value, ones], axis=1))
                inverse = 1.0 / mixed[:, 128:]
                probs[t, s, h] = (expo * jnp.concatenate([inverse, inverse], axis=1)).astype(BF)
                done.append(mixed[:, :128] * inverse)
            ctx[t, span, 0:128] = pick(~low_half, done[2]).astype(BF)
            ctx[t, span, 128:256] = jnp.where(low_half, done[0], done[1]).astype(BF)
        pltpu.make_async_copy(acts.at[t], acts_out.at[t], sem_out.at[0]).start()
        pltpu.make_async_copy(probs.at[t], probs_out.at[t], sem_out.at[1]).start()
        pltpu.make_async_copy(ctx.at[t], ctx_out.at[t], sem_out.at[2]).start()
        part = dot_t(ctx[t], full[t, :, 512:768]).astype(BF)
        normed_ref[...] += part.astype(F32)

    @blocks(rows, 128)
    def _(span):
        normed, scale = norm_stats(normed_ref[span, :])
        normed_ref[span, :] = normed
        scale_ref[span, :] = jnp.broadcast_to(scale, (128, 128))
        low_ref[span, :] = (normed * params[1:2, :] + params[2:3, :]).astype(BF)

    wait(acts, sem_out.at[0])
    wait(probs, sem_out.at[1])
    wait(ctx, sem_out.at[2])


TAIL_STEP = 0.43 / math.sqrt(2.0)
TAIL = (
    0.12125730288161489,
    0.12218773837809233,
    0.1024754485844625,
    0.12342253549698744,
    -0.04286343715820851,
    0.19185342214732998,
    -0.15518700012679373,
    0.036854031729008835,
)


def normal_parts(values):
    t = 1.0 / (1.0 + TAIL_STEP * jnp.abs(values))
    bell = jnp.exp2(values * values * (-0.5 * math.log2(math.e)))
    poly = TAIL[-1]
    for c in TAIL[-2::-1]:
        poly = c + t * poly
    tail = t * poly * bell
    return jnp.where(values >= 0, 1.0 - tail, tail), bell


def inner_kernel(nw, low_ref, bias, where, *rest):
    refs, rest = rest[:nw], rest[nw:]
    active_out, slope_out, full, inner_ref, active, slope, sem, sem_out = rest
    rows = low_ref.shape[0]
    nt = active.shape[0]
    load_weights(refs, where, full, sem)

    @pl.loop(0, nt)
    def _(t):
        wait(full.at[t], sem.at[t])
        inner_ref[...] = dot(low_ref[...], full[t]) + bias[t]

        @blocks(rows, 64)
        def _(span):
            inner = inner_ref[span, :]
            phi, bell = normal_parts(inner)
            active[t, span, :] = (inner * phi).astype(BF)
            slope[t, span, :] = (phi + inner * bell * (1.0 / math.sqrt(2.0 * math.pi))).astype(BF)

        pltpu.make_async_copy(active.at[t], active_out.at[t], sem_out.at[0]).start()
        pltpu.make_async_copy(slope.at[t], slope_out.at[t], sem_out.at[1]).start()

    wait(active, sem_out.at[0])
    wait(slope, sem_out.at[1])


def turn_of(where, n):
    return 2 * (n % 2) + ((where[0, 0] % 2) ^ (1 - n // 2))


def store_grads(where, side, held, outs, sem):
    nz, rows = outs[0].shape[0], outs[0].shape[1]
    for r in range(4):
        for j in range(nz):
            n = (side * 4 + r) * nz + j
            t, d = where[0, n], where[1, n]
            spot = pl.ds(pl.multiple_of(d * rows, rows), rows)
            pltpu.make_async_copy(
                held.at[t // 2, spot], outs[(r & 1) * 2 + (r >> 1)].at[j], sem
            ).start()


def each_grad(where, outs, make):
    def over(held, sems):
        nt = held.shape[0]
        if len(outs) == 1:
            for n in range(nt):
                held[n] = make(n)
                load(held.at[n], outs[0].at[n], sems.at[0])
            return lambda: wait(held, sems.at[0])
        keep, send = outs[0], outs[1:]
        for n in range(nt):
            held[n] = make(turn_of(where, n))
            if n == 1:
                store_grads(where, 1, held.at[0:2], send, sems.at[0])
            if n == 3:
                store_grads(where, 0, held.at[2:4], [keep.at[r] for r in range(4)], sems.at[1])
        return lambda: [wait(held.at[2 * n : 2 * n + 2], sems.at[n]) for n in range(2)]

    return over


def outer_kernel(nw, ng, active_in, normed_in, cot_in, rows_in, where, *rest):
    refs, outs, rest = rest[:nw], rest[nw : nw + ng], rest[nw + ng :]
    out_part, second_out, ffn_out, vec_ref, full, active, normed_ref, cot, second, out_v, ffn = rest[:11]
    turned, held, sem, sem_a, sem_b, sem_out = rest[11:]
    rows = cot.shape[0]
    nt = active.shape[0]
    load_weights(refs, where, full, sem)
    for t in range(nt):
        load(active_in.at[t], active.at[t], sem_a.at[t])
    load(normed_in, normed_ref, sem_b.at[0])
    load(cot_in, cot, sem_b.at[1])
    gain1, shift1, outer_bias, gain, shift = (rows_in[n : n + 1, :] for n in range(1, 6))
    vec_ref[...] = jnp.zeros_like(vec_ref)
    for t in range(nt):
        wait(active.at[t], sem_a.at[t])
        wait(full.at[t], sem.at[t])
        part = dot_t(active[t], full[t]).astype(BF).astype(F32)
        second[...] = part if t == 0 else second[...] + part
    wait(normed_ref, sem_b.at[0])
    wait(cot, sem_b.at[1])

    @blocks(rows, 128)
    def _(span):
        first = normed_ref[span, :] * gain1 + shift1
        normed, scale = norm_stats(second[span, :] + outer_bias + first)
        out_v[span, :] = (normed * gain + shift).astype(BF)
        incoming = cot[span, :].astype(F32)
        pull = norm_pull(incoming, normed, scale, gain)
        second[span, :] = pull
        ffn[span, :] = pull.astype(BF)
        vec_ref[0:1, :] += jnp.sum(incoming * normed, axis=0, keepdims=True)
        vec_ref[1:2, :] += jnp.sum(incoming, axis=0, keepdims=True)
        vec_ref[2:3, :] += jnp.sum(pull, axis=0, keepdims=True)

    load(out_v, out_part, sem_out.at[2])
    load(second, second_out, sem_out.at[3])
    load(ffn, ffn_out, sem_out.at[4])
    turned[...] = ffn[...].T
    each_grad(where, outs, lambda t: dot(turned[...], active[t]).astype(BF))(held, sem_out)()
    wait(out_v, sem_out.at[2])
    wait(second, sem_out.at[3])
    wait(ffn, sem_out.at[4])


def middle_kernel(nw, ng, slope_in, second_in, ffn_in, low_in, normed_in, scale_in, rows_in, where, *rest):
    refs, inner_refs, attn_refs, rest = rest[:nw], rest[nw : 2 * nw], rest[2 * nw : 3 * nw], rest[3 * nw :]
    outs, rest = rest[:ng], rest[ng:]
    attn_in_out, attn_low_out, ctx_grad_out, vec_ref, inner_vec = rest[:5]
    full, inner_full, attn_full, slope, normed_ref, scale_ref, low, second, attn_in, ffn = rest[5:15]
    turned, pulled, ctx_grad, held, sem, sem_a, sem_b, sem_out = rest[15:]
    rows = low.shape[0]
    nt = slope.shape[0]
    load(ffn_in, ffn, sem_b.at[0])
    load_weights(refs, where, full, sem.at[0])
    for t in range(nt):
        load(slope_in.at[t], slope.at[t], sem_a.at[t])
    load(low_in, low, sem_b.at[1])
    load_weights(inner_refs, where, inner_full, sem.at[1])
    load(second_in, second, sem_b.at[2])
    load(normed_in, normed_ref, sem_b.at[3])
    load(scale_in, scale_ref, sem_b.at[4])
    load_weights(attn_refs, where, attn_full, sem.at[2], 512)
    gain1 = rows_in[1:2, :]
    vec_ref[...] = jnp.zeros_like(vec_ref)
    wait(ffn, sem_b.at[0])
    for t in range(nt):
        wait(full.at[t], sem.at[0, t])
        wait(slope.at[t], sem_a.at[t])
        grad = (dot(ffn[...], full[t]) * slope[t].astype(F32)).astype(BF)
        pulled[t] = grad
        inner_vec[t] = jnp.sum(grad.astype(F32), axis=0, keepdims=True)
    wait(low, sem_b.at[1])
    turned[...] = low[...].T
    done = each_grad(where, outs, lambda t: dot(turned[...], pulled[t]).astype(BF))(held, sem_out)
    for t in range(nt):
        wait(inner_full.at[t], sem.at[1, t])
        part = dot_t(pulled[t], inner_full[t])
        attn_in[...] = part if t == 0 else attn_in[...] + part
    wait(second, sem_b.at[2])
    wait(normed_ref, sem_b.at[3])
    wait(scale_ref, sem_b.at[4])

    @blocks(rows, 128)
    def _(span):
        incoming = attn_in[span, :] + second[span, :]
        normed = normed_ref[span, :]
        grad = norm_pull(incoming, normed, scale_ref[span, 0:1], gain1)
        attn_in[span, :] = grad
        ffn[span, :] = grad.astype(BF)
        vec_ref[0:1, :] += jnp.sum(incoming * normed, axis=0, keepdims=True)
        vec_ref[1:2, :] += jnp.sum(incoming, axis=0, keepdims=True)
        vec_ref[2:3, :] += jnp.sum(grad, axis=0, keepdims=True)

    load(attn_in, attn_in_out, sem_out.at[2])
    load(ffn, attn_low_out, sem_out.at[3])
    low_half = lane_masks(rows)
    for t in range(nt):
        wait(attn_full.at[t], sem.at[2, t])
        got = dot(ffn[...], attn_full[t])
        ctx_grad[t, :, 0:128] = pick(~low_half, got[:, :128]).astype(BF)
        ctx_grad[t, :, 128:256] = got[:, 128:].astype(BF)
        load(ctx_grad.at[t], ctx_grad_out.at[t], sem_out.at[4])
    done()
    wait(attn_in, sem_out.at[2])
    wait(ffn, sem_out.at[3])
    wait(ctx_grad, sem_out.at[4])


def attend_pull(acts, probs, ctx_grad, back, t):
    rows = acts.shape[1]
    low_half = lane_masks(LEN)
    factor = HEAD_DIM ** (-0.5)
    h = HEAD_DIM
    for s in range(rows // LEN):
        span = slice(s * LEN, (s + 1) * LEN)
        q01, k01, v01 = acts[t, span, 0:128], acts[t, span, 128:256], acts[t, span, 256:384]
        qv2, k2 = acts[t, span, 384:512], acts[t, span, 512:640]
        g2, g01 = ctx_grad[t, span, 0:128], ctx_grad[t, span, 128:256]
        heads = (
            (pick(low_half, g01), k01, v01),
            (pick(~low_half, g01), k01, v01),
            (g2, k2, qv2),
        )
        queries, scores = [], []
        for n, (grad, key, value) in enumerate(heads):
            wide = probs[t, s, n].astype(F32)
            pulled = dot_t(grad, value)
            delta = jnp.sum(pulled * wide, axis=-1, keepdims=True)
            scores.append((wide * (pulled - delta)).astype(BF))
            queries.append(dot(scores[n], key) * factor)
        q01t, g01t, qv2t, g2t = q01.T, g01.T, qv2.T, g2.T
        keys01 = jnp.concatenate([dot(q01t[:h], scores[0]), dot(q01t[h:], scores[1])], axis=0) * factor
        values01 = jnp.concatenate([dot(g01t[:h], probs[t, s, 0]), dot(g01t[h:], probs[t, s, 1])], axis=0)
        both2 = jnp.concatenate([dot(qv2t[:h], scores[2]) * factor, dot(g2t[h:], probs[t, s, 2])], axis=0)
        kv2 = both2.astype(BF).T
        back[t, span, 0:128] = jnp.where(low_half, queries[0], queries[1]).astype(BF)
        back[t, span, 128:256] = keys01.astype(BF).T
        back[t, span, 256:384] = values01.astype(BF).T
        back[t, span, 384:512] = jnp.where(low_half, queries[2].astype(BF), kv2)
        back[t, span, 512:640] = pick(low_half, kv2)


def attend_back_kernel(nw, ng, x_ref, attn_low, acts_in, probs_in, ctx_in, ctx_grad_in, attn_in, *rest):
    second_vec, first_vec, inner_vec, where, *rest = rest
    refs, outs, (input_ref, vectors) = rest[:nw], rest[nw : nw + ng], rest[nw + ng : nw + ng + 2]
    full, total, acts, probs, ctx, ctx_grad, back, turned_x, turned_a, held, vec_ref = rest[nw + ng + 2 : -3]
    sem, sem_in, sem_out = rest[-3:]
    nt = acts.shape[0]
    for n in range(nt):
        t = turn_of(where, n) if ng > 1 else n
        load(acts_in.at[t], acts.at[t], sem_in.at[t])
        load(ctx_grad_in.at[t], ctx_grad.at[t], sem_in.at[t])
        load(probs_in.at[t], probs.at[t], sem_in.at[t])
        load(ctx_in.at[t], ctx.at[t], sem_in.at[t])
    load_weights(refs, where, full, sem)
    load(attn_in, total, sem_in.at[nt])
    turned_x[...] = x_ref[...].T
    turned_a[...] = attn_low[...].T

    def make(t):
        for held_in in (acts, ctx_grad, probs, ctx):
            wait(held_in.at[t], sem_in.at[t])
        attend_pull(acts, probs, ctx_grad, back, t)
        vec_ref[t] = jnp.sum(back[t].astype(F32), axis=0, keepdims=True)
        from_x = dot(turned_x[...], back[t])
        from_out = dot(turned_a[...], ctx[t])
        return jnp.concatenate(
            [from_x[:, :512], from_x[:, 512:] + from_out[:, :128], from_out[:, 128:]], axis=1
        ).astype(BF)

    done = each_grad(where, outs, make)(held, sem_out)
    wait(total, sem_in.at[nt])
    for t in range(nt):
        wait(full.at[t], sem.at[t])
        total[...] += dot_t(back[t], full[t, :, 0:640])
    input_ref[...] = total[...].astype(BF)
    vectors[...] = jnp.zeros_like(vectors)
    for at, ref in ((0, second_vec), (3, first_vec)):
        vectors[at : at + 3, :] = ref[0:3, :]
    for n in range(nt):
        vectors[6 + n : 7 + n, :] = inner_vec[n]
        vectors[6 + nt + n : 7 + nt + n, 0:640] = vec_ref[n]
    done()


def place_kernel(order, one, two, three, four, out, held, sem, sem_out):
    rows = one.shape[0]
    parts = (one, two, three, four)
    for n, part in enumerate(parts):
        load(part, held.at[n], sem.at[n])
    for n in range(4):
        wait(held.at[n], sem.at[n])
        spot = pl.ds(pl.multiple_of(order[n] * rows, rows), rows)
        pltpu.make_async_copy(held.at[n], out.at[spot], sem_out.at[n]).start()
    for n in range(4):
        wait(held.at[n], sem_out.at[n])


def widen_kernel(order, one, two, *rest):
    out, held, wide, sem, sem_out = rest[-5:]
    rows = one.shape[0]
    half = rows // 2
    for n, part in enumerate((one, two)):
        load(part, held.at[n], sem.at[n])
    for n in range(2):
        wait(held.at[n], sem.at[n])
        for m in range(2):
            wide[2 * n + m] = held[n, m * half : (m + 1) * half, :].astype(F32)
            spot = pl.ds(pl.multiple_of(order[n] * rows + m * half, half), half)
            pltpu.make_async_copy(wide.at[2 * n + m], out.at[spot], sem_out.at[2 * n + m]).start()
    for n in range(4):
        wait(wide.at[n], sem_out.at[n])


def interleave(q, k, v, o):
    h = HEAD_DIM
    return jnp.concatenate(
        [
            q[..., : 2 * h], k[..., : 2 * h], v[..., : 2 * h],
            q[..., 2 * h :], v[..., 2 * h :], k[..., 2 * h :], o[..., 2 * h :],
            o[..., : 2 * h],
        ],
        axis=-1,
    )


def interleave_kernel(q_in, k_in, v_in, o_in, out, q, k, v, o, sem):
    for n, (ref, held) in enumerate(((q_in, q), (k_in, k), (v_in, v), (o_in, o))):
        load(ref, held, sem.at[n])
    for n, held in enumerate((q, k, v, o)):
        wait(held, sem.at[n])
    out[...] = interleave(q[...].astype(F32), k[...].astype(F32), v[...].astype(F32), o[...].astype(F32).T).astype(BF)


def part_kernel(total, *rest):
    moved, (q, k, v, o) = rest[:-4], rest[-4:]
    grad = total[...]
    for piece in moved:
        grad = grad + piece[0 : grad.shape[0], :].astype(F32)
    h = HEAD_DIM
    part = lambda *spans: jnp.concatenate([grad[:, a * h : b * h] for a, b in spans], axis=1)
    q[...] = part((0, 2), (6, 7))
    k[...] = part((2, 4), (8, 9))
    v[...] = part((4, 6), (7, 8))
    o[...] = part((10, 12), (9, 10)).T


def body(
    plan,
    inputs,
    segments,
    query_weight,
    key_weight,
    value_weight,
    query_bias,
    value_bias,
    out_weight,
    out_bias,
    first_gain,
    first_shift,
    inner_weight,
    inner_bias,
    outer_weight,
    outer_bias,
    second_gain,
    second_shift,
    cotangent,
):
    nt, ndp = plan.nt, plan.ndp
    width = inputs.shape[1]
    local, hidden = query_weight.shape[1], inner_weight.shape[1]
    rows = inputs.shape[0] // nt
    nseq = rows // LEN
    me = lax.axis_index("tensor")
    mine = lambda a, n: lax.dynamic_slice_in_dim(a, me * n, n, 0)
    x = mine(inputs, rows)
    cot = mine(cotangent, rows)
    seg_row = mine(segments, nseq)
    seg_col = seg_row.reshape(rows, 1)

    nw = 8 if plan.pieces else 1
    if plan.pieces:
        where = plan.tables()
    else:
        where = jnp.zeros((1, 1), jnp.int32)
    params = jnp.concatenate(
        [
            v.reshape(1, width)
            for v in (out_bias, first_gain, first_shift, outer_bias, second_gain, second_shift, out_bias, out_bias)
        ]
    )
    limit = 56
    LOW = 24 if rows <= 512 else 56
    weights = pltpu.VMEM((nt, width, hidden), BF)
    acted = pltpu.VMEM((nt, rows, hidden), BF)
    dma = pltpu.SemaphoreType.DMA
    any_w = [anywhere()] * nw
    shards = (
        call(
            interleave_kernel,
            [query_weight, key_weight, value_weight, out_weight],
            [anywhere()] * 4,
            [shape((query_weight.shape[0], 4 * local), BF)],
            [vmem()],
            [*[pltpu.VMEM(query_weight.shape, BF)] * 3, pltpu.VMEM(out_weight.shape, BF), dma((4,))],
            limit,
            1,
        )[0],
        inner_weight,
        outer_weight.T,
    )

    def attend(x, bias, attn_w):
        return call(
            functools.partial(attend_kernel, nw),
            [x, seg_row, seg_col, bias, params, where, *attn_w],
            [vmem()] * 5 + [smem()] + any_w,
            [
                shape((nt, rows, 640), BF),
                shape((nt, nseq, 3, LEN, LEN), BF),
                shape((nt, rows, 256), BF),
                shape((rows, width), F32),
                shape((rows, 128), F32),
                shape((rows, width), BF),
            ],
            [anywhere()] * 3 + [vmem()] * 3,
            [
                weights,
                pltpu.VMEM((nseq, LEN, LEN), F32),
                pltpu.VMEM((nt, rows, 640), BF),
                pltpu.VMEM((nt, nseq, 3, LEN, LEN), BF),
                pltpu.VMEM((nt, rows, 256), BF),
                dma((nt,)),
                dma((3,)),
            ],
            limit,
            13,
        )

    def inner(low, inner_b, inner_w):
        return call(
            functools.partial(inner_kernel, nw),
            [low, inner_b, where, *inner_w],
            [vmem()] * 2 + [smem()] + any_w,
            [shape((nt, rows, hidden), BF)] * 2,
            [anywhere()] * 2,
            [weights, pltpu.VMEM((rows, hidden), F32), acted, acted, dma((nt,)), dma((2,))],
            limit,
            13,
        )

    if plan.pieces:
        slot = (plan.nz, width // ndp, hidden)
        grads = [shape((4, *slot), BF)] + [shape(slot, BF)] * 4
    else:
        grads = [shape((nt, width, hidden), BF)]
    ng = len(grads)
    wide, thin = pltpu.VMEM((rows, width), F32), pltpu.VMEM((rows, width), BF)

    def outer(active, normed, outer_w):
        return call(
            functools.partial(outer_kernel, nw, ng),
            [active, normed, cot, params, where, *outer_w],
            [anywhere()] * 3 + [vmem()] + [smem()] + any_w,
            [
                *grads,
                shape((rows, width), BF),
                shape((rows, width), F32),
                shape((rows, width), BF),
                shape((8, width), F32),
            ],
            [anywhere()] * (ng + 3) + [vmem()],
            [
                weights, acted, wide, thin, wide, thin, thin, pltpu.VMEM((width, rows), BF), weights,
                dma((nt,)), dma((nt,)), dma((2,)), dma((5,)),
            ],
            limit,
            14,
        )

    def middle(slope, second, ffn, low, normed, scale, outer_w, inner_w, attn_w):
        return call(
            functools.partial(middle_kernel, nw, ng),
            [slope, second, ffn, low, normed, scale, params, where, *outer_w, *inner_w, *attn_w],
            [anywhere()] * 6 + [vmem()] + [smem()] + any_w * 3,
            [
                *grads,
                shape((rows, width), F32),
                shape((rows, width), BF),
                shape((nt, rows, 256), BF),
                shape((8, width), F32),
                shape((nt, 1, hidden), F32),
            ],
            [anywhere()] * (ng + 3) + [vmem()] * 2,
            [
                weights, weights, pltpu.VMEM((nt, width, 256), BF), acted, wide,
                pltpu.VMEM((rows, 128), F32), thin, wide, wide, thin,
                pltpu.VMEM((width, rows), BF), acted, pltpu.VMEM((nt, rows, 256), BF), weights,
                dma((3, nt)), dma((nt,)), dma((5,)), dma((5,)),
            ],
            limit,
            0.1,
        )

    def attend_back(attn_low, acts, probs, ctx, ctx_grad, attn_in, vecs, attn_w):
        return call(
            functools.partial(attend_back_kernel, nw, ng),
            [x, attn_low, acts, probs, ctx, ctx_grad, attn_in, *vecs, where, *attn_w],
            [vmem()] * 2 + [anywhere()] * 5 + [vmem()] * 3 + [smem()] + any_w,
            [*grads, shape((rows, width), BF), shape((16, hidden), F32)],
            [anywhere()] * ng + [vmem()] * 2,
            [
                weights,
                pltpu.VMEM((rows, width), F32),
                pltpu.VMEM((nt, rows, 640), BF),
                pltpu.VMEM((nt, nseq, 3, LEN, LEN), BF),
                pltpu.VMEM((nt, rows, 256), BF),
                pltpu.VMEM((nt, rows, 256), BF),
                pltpu.VMEM((nt, rows, 640), BF),
                pltpu.VMEM((width, rows), BF),
                pltpu.VMEM((width, rows), BF),
                weights,
                pltpu.VMEM((nt, 1, 640), F32),
                dma((nt,)),
                dma((nt + 1,)),
                dma((2,)),
            ],
            limit,
            0.1,
        )

    def place(parts):
        order = jnp.stack([me, me ^ 2, me ^ 1, me ^ 3]).astype(jnp.int32)
        return call(
            place_kernel,
            [order, *parts],
            [smem()] + [anywhere()] * 4,
            [shape((nt * rows, width), BF)],
            [anywhere()],
            [pltpu.VMEM((4, rows, width), BF), dma((4,)), dma((4,))],
            limit,
            4,
        )[0]

    def widen(parts, flip, half=None):
        order = jnp.stack([me ^ flip, me ^ flip ^ 1]).astype(jnp.int32)
        more = [] if half is None else [half]
        return call(
            widen_kernel,
            [order, *parts, *more],
            [smem()] + [anywhere()] * (2 + len(more)),
            [shape((nt * rows, width), F32)],
            [anywhere()],
            [pltpu.VMEM((2, rows, width), BF), pltpu.VMEM((4, rows // 2, width), F32), dma((2,)), dma((4,))],
            limit,
            4,
            {3: 0} if more else {},
        )[0]

    def small_parts():
        every = lax.all_gather(jnp.concatenate([query_bias, value_bias, inner_bias]), "tensor", axis=0)
        q_b, v_b = every[:, None, :local], every[:, None, local : 2 * local]
        none = jnp.zeros_like(q_b)
        return interleave(q_b, none, v_b, none), every[:, None, 2 * local :]

    bias, inner_b = small_parts()
    if plan.pieces:
        turn, one_way, other_way, core = plan.turn, plan.first(), plan.second(), plan.core()

        beside = plan.beside()

        def spread(own):
            return [turn(own, one_way), turn(own, other_way)]

        def cores(parts):
            return [turn(v, core) for v in parts]

        near = plan.near(shards[0])
        near, bias, inner_b, x, cot, seg_row, seg_col, where, params = tie(
            (near, bias, inner_b, x, cot, seg_row, seg_col, where, params)
        )
        own1 = jnp.stack([shards[0], *near])
        two1 = spread(own1)
        near = plan.near(tie(jnp.concatenate(shards[1:], axis=1), own1))
        two1 = tie(two1)
        both1 = turn(two1[0], other_way)
        cores1 = cores([own1, *two1])
        both1, cores1, near = tie((both1, cores1, near))
        own2 = jnp.stack([shards[1], *[v[:, :hidden] for v in near]])
        own3 = jnp.stack([shards[2], *[v[:, hidden:] for v in near]])
        two2 = spread(own2)
        attn_w = [own1, *two1, both1, *cores1, turn(both1, core)]
        acts, probs, ctx, normed, scale, low = attend(x, bias, attn_w)
        two2, low = tie((two2, low))
        both2 = turn(two2[0], other_way)
        cores2 = cores([own2, *two2])
        two3 = spread(own3)
        both2, cores2 = tie((both2, cores2))
        inner_w = [own2, *two2, both2, *cores2, turn(both2, core)]
        active, slope = inner(low, inner_b, inner_w)
        two3, active = tie((two3, active))
        both3 = turn(two3[0], other_way)
        cores3 = cores([own3, *two3])
        both3, cores3 = tie((both3, cores3))
        outer_w = [own3, *two3, both3, *cores3, turn(both3, core)]
        keep3, *send3, layer_part, second, ffn, second_vec = outer(active, normed, outer_w)

        got3 = cores(send3)
        layer_x = turn(layer_part, beside)
        keep2, *send2, attn_in, attn_low, ctx_grad, first_vec, inner_vec = middle(
            slope, second, tie((ffn, send3))[0], low, normed, scale, outer_w, inner_w, attn_w
        )
        got3, layer_x, send2, ctx_grad = tie((got3, layer_x, send2, ctx_grad))
        away3 = plan.scatter_a(keep3, got3)
        got3a = turn(away3, one_way)
        got2 = cores(send2)
        layer_c = cores([layer_part, layer_x])
        got2, layer_c, ctx_grad = tie((got2, layer_c, ctx_grad))
        away2 = plan.scatter_a(keep2, got2)
        got2a = turn(away2, one_way)
        keep1, *send1, input_low, vectors = attend_back(
            attn_low, acts, probs, ctx, tie((ctx_grad, away2))[0], attn_in, (second_vec, first_vec, inner_vec), attn_w
        )
        got1 = cores(send1)
        vector_c = turn(vectors, core)
        packed = 2 * vectors.shape[0]
        got3a, got2a, got1, vector_c, input_low = tie((got3a, got2a, got1, vector_c, input_low))
        away3 = plan.scatter_b(keep3, got3, got3a)
        got3b = turn(away3, other_way)
        away2 = plan.scatter_b(keep2, got2, got2a)
        got2b = turn(away2, other_way)
        vectors = vectors + vector_c
        away1 = plan.scatter_a(keep1, got1)
        flat = (-1, hidden)
        away1 = jnp.concatenate([away1.reshape(flat), pack(vectors)])
        got1a = turn(away1, one_way)
        input_c = turn(input_low, core)
        layer_out = place(tie(([layer_part, layer_x, *layer_c], away1))[0])
        got3b, layer_out = tie((got3b, layer_out))
        z3 = plan.scatter_left(keep3, got3, got3a, got3b)
        moved3 = plan.go_z(z3[1])
        half_grad = widen(tie(([input_low, input_c], z3))[0], 0)
        got2b, half_grad = tie((got2b, half_grad))
        z2 = plan.scatter_left(keep2, got2, got2a, got2b)
        moved2 = plan.go_z(z2[1])
        got1a, z2, moved3 = tie((got1a, z2, moved3))
        vectors = vectors + unpack(got1a[-packed:])
        got1a = got1a[:-packed].reshape(2, *slot)
        away = plan.scatter_b(keep1, got1, got1a)
        away = jnp.concatenate([away.reshape(flat), pack(vectors)])
        got1b = turn(away, other_way)
        got1b, moved2 = tie((got1b, moved2))
        vectors = vectors + unpack(got1b[-packed:])
        got1b = got1b[:-packed].reshape(slot)
        z1 = plan.scatter_left(keep1, got1, got1a, got1b)
        packs = pack(vectors)
        z1 = z1[0], [jnp.concatenate([v, packs]) for v in z1[1]]
        input_low = tie((input_low, z1[0]))[0]
        moved1 = plan.go_z(z1[1])
        input_x = turn(input_low, beside)
        outer_grad = plan.last(z3[0], moved3)
        inner_grad = plan.last(z2[0], moved2)
        input_x, moved1, outer_grad, inner_grad = tie((input_x, moved1, outer_grad, inner_grad))
        input_xc = turn(input_x, core)
        vectors = plan.last(vectors, [unpack(v[-packed:]) for v in moved1])
        attn_grads = call(
            part_kernel,
            [z1[0], *moved1],
            [vmem()] * (1 + len(moved1)),
            [shape((width // ndp, local), F32)] * 3 + [shape((local, width // ndp), F32)],
            [vmem()] * 4,
            [],
            16,
            1,
        )
        input_grad = widen([input_x, input_xc], 2, half_grad)
    else:
        attn_w, inner_w, outer_w = (
            [lax.all_gather(lax.all_gather(s, "dp", axis=0, tiled=True), "tensor", axis=0)]
            for s in shards
        )
        acts, probs, ctx, normed, scale, low = attend(x, bias, attn_w)
        active, slope = inner(low, inner_b, inner_w)
        outer_g, layer_part, second, ffn, second_vec = outer(active, normed, outer_w)
        inner_g, attn_in, attn_low, ctx_grad, first_vec, inner_vec = middle(
            slope, second, ffn, low, normed, scale, outer_w, inner_w, attn_w
        )
        attn_g, input_low, vectors = attend_back(
            attn_low, acts, probs, ctx, ctx_grad, attn_in, (second_vec, first_vec, inner_vec), attn_w
        )
        outer_grad, inner_grad, attn_g = (
            lax.psum_scatter(
                lax.psum_scatter(g, "tensor", scatter_dimension=0, tiled=False),
                "dp",
                scatter_dimension=0,
                tiled=True,
            ).astype(F32)
            for g in (outer_g, inner_g, attn_g)
        )
        layer_out = lax.all_gather(layer_part, "tensor", axis=0, tiled=True)
        input_grad = lax.all_gather(input_low, "tensor", axis=0, tiled=True).astype(F32)

    if not plan.pieces:
        vectors = lax.psum(vectors, AXES)
    gain2, shift2, bias2, gain1, shift1, bias1 = (vectors[n] for n in range(6))
    inner_bias_grad = lax.dynamic_index_in_dim(vectors, 6 + me, 0, keepdims=False)
    mine_vec = lax.dynamic_index_in_dim(vectors, 6 + nt + me, 0, keepdims=False)
    h = HEAD_DIM
    query_bias_grad = jnp.concatenate([mine_vec[: 2 * h], mine_vec[6 * h : 7 * h]])
    value_bias_grad = jnp.concatenate([mine_vec[4 * h : 6 * h], mine_vec[7 * h : 8 * h]])
    if not plan.pieces:
        part = lambda *spans: jnp.concatenate([attn_g[:, a * h : b * h] for a, b in spans], axis=1)
        attn_grads = part((0, 2), (6, 7)), part((2, 4), (8, 9)), part((4, 6), (7, 8)), part((10, 12), (9, 10)).T
    return (
        layer_out,
        input_grad,
        *attn_grads[:3],
        query_bias_grad,
        value_bias_grad,
        attn_grads[3],
        bias1,
        gain1,
        shift1,
        inner_grad,
        inner_bias_grad,
        outer_grad.T,
        bias2,
        gain2,
        shift2,
    )


def solution(mesh):
    in_specs = (
        P("dp", None),
        P("dp", None),
        P("dp", "tensor"),
        P("dp", "tensor"),
        P("dp", "tensor"),
        P("tensor"),
        P("tensor"),
        P("tensor", "dp"),
        P(),
        P(),
        P(),
        P("dp", "tensor"),
        P("tensor"),
        P("tensor", "dp"),
        P(),
        P(),
        P(),
        P("dp", None),
    )
    out_specs = (
        P("dp", None),
        P("dp", None),
        P("dp", "tensor"),
        P("dp", "tensor"),
        P("dp", "tensor"),
        P("tensor"),
        P("tensor"),
        P("tensor", "dp"),
        P(),
        P(),
        P(),
        P("dp", "tensor"),
        P("tensor"),
        P("tensor", "dp"),
        P(),
        P(),
        P(),
    )
    return jax.shard_map(
        functools.partial(body, Plan(mesh)),
        mesh=mesh,
        in_specs=in_specs,
        out_specs=out_specs,
        check_vma=False,
    )
```

```python
import functools
import math

import jax
import jax.numpy as jnp
from jax import lax
from jax.experimental import pallas as pl
from jax.experimental.pallas import tpu as pltpu
from jax.sharding import PartitionSpec as P

HEAD_DIM = 64
LEN = 256
EPS = 1e-06
BF = jnp.bfloat16
F32 = jnp.float32
AXES = ("dp", "tensor")
MIB = 1 << 20
SCALE = 0.3


def dot(left, right):
    return lax.dot_general(left, right, (((1,), (0,)), ((), ())), preferred_element_type=F32)


def dot_t(left, right):
    return lax.dot_general(left, right, (((1,), (1,)), ((), ())), preferred_element_type=F32)


def t_dot(left, right):
    return lax.dot_general(left, right, (((0,), (0,)), ((), ())), preferred_element_type=F32)


def vmem():
    return pl.BlockSpec(memory_space=pltpu.VMEM)


def smem():
    return pl.BlockSpec(memory_space=pltpu.SMEM)


def anywhere():
    return pl.BlockSpec(memory_space=pl.ANY)


def call(body, ins, in_specs, outs, out_specs, scratch, limit, cost, aliases={}):
    return pl.pallas_call(
        body,
        out_shape=outs,
        in_specs=in_specs,
        out_specs=out_specs,
        scratch_shapes=scratch,
        input_output_aliases=aliases,
        compiler_params=pltpu.CompilerParams(vmem_limit_bytes=limit * MIB),
        cost_estimate=pl.CostEstimate(flops=int(cost * SCALE * 1e9), bytes_accessed=1000, transcendentals=0),
    )(*ins)


def shape(dims, dtype):
    return jax.ShapeDtypeStruct(dims, dtype)


class Plan:
    def __init__(self, mesh):
        self.ndp, self.nt = mesh.shape["dp"], mesh.shape["tensor"]
        self.pieces = self.nt == 4 and self.ndp == 8
        self.nz = self.ndp // 2

    def pairs(self, move):
        found = []
        for d in range(self.ndp):
            for t in range(self.nt):
                z, y, x, c = move(d >> 1, d & 1, t >> 1, t & 1)
                found.append((d * self.nt + t, (z * 2 + y) * self.nt + x * 2 + c))
        return found

    def first(self):
        return self.pairs(lambda z, y, x, c: (z, y, x ^ 1, c) if c == 0 else (z, y ^ 1, x, c))

    def second(self):
        return self.pairs(lambda z, y, x, c: (z, y, x ^ 1, c) if c == 1 else (z, y ^ 1, x, c))

    def core(self):
        return self.pairs(lambda z, y, x, c: (z, y, x, c ^ 1))

    def along(self, j):
        return self.pairs(lambda z, y, x, c: (z ^ j, y, x, c))

    def step(self, last):
        return self.pairs(lambda z, y, x, c: (z ^ (1 if (c == 0) != last else 2), y, x, c))

    def tables(self, split):
        d, t = lax.axis_index("dp"), lax.axis_index("tensor")
        z, y, x, c = d >> 1, d & 1, t >> 1, t & 1
        s = jnp.arange(2)[:, None, None]
        r = jnp.arange(4)[None, :, None]
        j = jnp.arange(self.nz)[None, None, :]
        a, b = r & 1, r >> 1
        core = c ^ s
        dx, dy = jnp.where(core == 0, a, b), jnp.where(core == 0, b, a)
        if split:
            j = jnp.where(core == 0, j, (j & 1) * 2 + (j >> 1))
        where_t = jnp.broadcast_to((x ^ dx) * 2 + core, (2, 4, self.nz))
        where_d = jnp.broadcast_to((z ^ j) * 2 + (y ^ dy), (2, 4, self.nz))
        return jnp.stack([where_t.reshape(-1), where_d.reshape(-1)]).astype(jnp.int32)

    def turn(self, values, pairs):
        return lax.ppermute(values, AXES, pairs)

    def near(self, shard):
        return [self.turn(shard, self.along(j)) for j in range(1, self.nz)]

    def beside(self):
        return self.pairs(lambda z, y, x, c: (z, y, x ^ 1, c))

    def scatter_a(self, keep, got):
        return (keep[2:].astype(F32) + jnp.stack(got[2:]).astype(F32)).astype(BF)

    def scatter_b(self, keep, got, got_a):
        return (keep[1].astype(F32) + got[1].astype(F32) + got_a[1].astype(F32)).astype(BF)

    def scatter_left(self, keep, got, got_a, got_b):
        left = keep[0].astype(F32) + got[0].astype(F32) + got_a[0].astype(F32) + got_b.astype(F32)
        return left[0], [left[j].astype(BF) for j in range(1, self.nz)]

    def go_z(self, low):
        return [self.turn(low[j - 1], self.along(j)) for j in range(1, self.nz)]

    def last(self, total, moved):
        for piece in moved:
            total = total + piece.astype(F32)
        return total


def load_weights(refs, where, full, sem, start=0):
    columns = pl.ds(start, full.shape[2])
    if len(refs) == 1:
        for t in range(full.shape[0]):
            pltpu.make_async_copy(refs[0].at[t, :, columns], full.at[t], sem.at[t]).start()
        return
    nz, rows, _ = refs[0].shape
    for r, ref in enumerate(refs):
        for j in range(nz):
            t, d = where[0, r * nz + j], where[1, r * nz + j]
            spot = pl.ds(pl.multiple_of(d * rows, rows), rows)
            pltpu.make_async_copy(ref.at[j, :, columns], full.at[t, spot], sem.at[t]).start()


def load(ref, held, sem):
    pltpu.make_async_copy(ref, held, sem).start()


def wait(held, sem):
    pltpu.make_async_copy(held, held, sem).wait()


def blocks(rows, block):
    def over(run):
        @pl.loop(0, rows // block)
        def _(i):
            run(pl.ds(pl.multiple_of(i * block, block), block))

    return over


def pack(vectors):
    high = vectors.astype(BF)
    return jnp.concatenate([high, (vectors - high.astype(F32)).astype(BF)])


def unpack(rows):
    half = rows.shape[0] // 2
    return rows[:half].astype(F32) + rows[half:].astype(F32)


def tie(values, *after):
    if after:
        return lax.optimization_barrier((values, *after))[0]
    return lax.optimization_barrier(values)


def lane_masks(rows):
    lane = lax.broadcasted_iota(jnp.int32, (rows, 128), 1)
    return lane < HEAD_DIM


def pick(mask, values):
    return jnp.where(mask, values, jnp.zeros_like(values))


def norm_stats(hidden):
    center = hidden - jnp.mean(hidden, axis=-1, keepdims=True)
    scale = lax.rsqrt(jnp.mean(center * center, axis=-1, keepdims=True) + EPS)
    return center * scale, scale


def norm_pull(incoming, normed, scale, gain):
    scaled = incoming * gain
    return scale * (
        scaled
        - jnp.mean(scaled, axis=-1, keepdims=True)
        - normed * jnp.mean(scaled * normed, axis=-1, keepdims=True)
    )


def attend_kernel(nw, x_ref, seg_row, bias, params, where, *rest):
    refs, rest = rest[:nw], rest[nw:]
    acts_out, probs_out, ctx_out, normed_ref, scale_ref, low_ref = rest[:6]
    full, keep, acts, probs, ctx, sem, sem_out = rest[6:]
    rows = x_ref.shape[0]
    nt = acts.shape[0]
    load_weights(refs, where, full, sem)
    nseq = rows // LEN
    for s in range(nseq):
        own = seg_row[s : s + 1, :].astype(F32)
        same = jnp.broadcast_to(own, (8, LEN)).T[:, 0:1] == own
        keep[s] = jnp.where(same, 0.0, -1e30).astype(F32)
    low_half = lane_masks(LEN)
    ones = jnp.ones((LEN, 128), BF)

    normed_ref[...] = x_ref[...].astype(F32) + params[0:1, :]

    @pl.loop(0, nt)
    def _(t):
        wait(full.at[t], sem.at[t])
        x = x_ref[...]
        acts[t, :, 0:512] = (dot(x, full[t, :, 0:512]) + bias[t, :, 0:512]).astype(BF)
        last = dot(x, full[t, :, 512:640]).astype(BF)
        acts[t, :, 512:640] = pick(lane_masks(rows), last)

        for s in range(nseq):
            span = slice(s * LEN, (s + 1) * LEN)
            q01, k01, v01 = acts[t, span, 0:128], acts[t, span, 128:256], acts[t, span, 256:384]
            qv2, k2 = acts[t, span, 384:512], acts[t, span, 512:640]
            heads = (
                (pick(low_half, q01), k01, v01),
                (pick(~low_half, q01), k01, v01),
                (pick(low_half, qv2), k2, qv2),
            )
            done = []
            for h, (query, key, value) in enumerate(heads):
                scores = dot_t(query, key) * HEAD_DIM ** (-0.5) + keep[s]
                top = jnp.max(scores, axis=-1, keepdims=True)
                expo = jnp.exp(scores - top)
                low = expo.astype(BF)
                mixed = dot(low, jnp.concatenate([value, ones], axis=1))
                inverse = 1.0 / mixed[:, 128:]
                probs[t, s, h] = (expo * jnp.concatenate([inverse, inverse], axis=1)).astype(BF)
                done.append(mixed[:, :128] * inverse)
            ctx[t, span, 0:128] = pick(~low_half, done[2]).astype(BF)
            ctx[t, span, 128:256] = jnp.where(low_half, done[0], done[1]).astype(BF)
        pltpu.make_async_copy(acts.at[t], acts_out.at[t], sem_out.at[0]).start()
        pltpu.make_async_copy(probs.at[t], probs_out.at[t], sem_out.at[1]).start()
        pltpu.make_async_copy(ctx.at[t], ctx_out.at[t], sem_out.at[2]).start()
        part = dot_t(ctx[t], full[t, :, 512:768]).astype(BF)
        normed_ref[...] += part.astype(F32)

    @blocks(rows, 128)
    def _(span):
        normed, scale = norm_stats(normed_ref[span, :])
        normed_ref[span, :] = normed
        scale_ref[span, :] = jnp.broadcast_to(scale, (128, 128))
        low_ref[span, :] = (normed * params[1:2, :] + params[2:3, :]).astype(BF)

    wait(acts, sem_out.at[0])
    wait(probs, sem_out.at[1])
    wait(ctx, sem_out.at[2])


TAIL_STEP = 0.43 / math.sqrt(2.0)
TAIL = (
    0.12125730288161489,
    0.12218773837809233,
    0.1024754485844625,
    0.12342253549698744,
    -0.04286343715820851,
    0.19185342214732998,
    -0.15518700012679373,
    0.036854031729008835,
)


def normal_parts(values):
    t = 1.0 / (1.0 + TAIL_STEP * jnp.abs(values))
    bell = jnp.exp2(values * values * (-0.5 * math.log2(math.e)))
    poly = TAIL[-1]
    for c in TAIL[-2::-1]:
        poly = c + t * poly
    tail = t * poly * bell
    return jnp.where(values >= 0, 1.0 - tail, tail), bell


def inner_kernel(nw, low_ref, bias, where, *rest):
    refs, rest = rest[:nw], rest[nw:]
    active_out, slope_out, full, inner_ref, active, slope, sem, sem_out = rest
    rows = low_ref.shape[0]
    nt = active.shape[0]
    load_weights(refs, where, full, sem)

    @pl.loop(0, nt)
    def _(t):
        wait(full.at[t], sem.at[t])
        inner_ref[...] = dot(low_ref[...], full[t]) + bias[t]

        @blocks(rows, 64)
        def _(span):
            inner = inner_ref[span, :]
            phi, bell = normal_parts(inner)
            active[t, span, :] = (inner * phi).astype(BF)
            slope[t, span, :] = (phi + inner * bell * (1.0 / math.sqrt(2.0 * math.pi))).astype(BF)

        pltpu.make_async_copy(active.at[t], active_out.at[t], sem_out.at[0]).start()
        pltpu.make_async_copy(slope.at[t], slope_out.at[t], sem_out.at[1]).start()

    wait(active, sem_out.at[0])
    wait(slope, sem_out.at[1])


def turn_of(where, n):
    return 2 * (n % 2) + ((where[0, 0] % 2) ^ (1 - n // 2))


def store_grads(where, side, held, outs, sem):
    nz, rows = outs[0].shape[0], outs[0].shape[1]
    for r in range(4):
        for j in range(nz):
            n = (side * 4 + r) * nz + j
            t, d = where[0, n], where[1, n]
            spot = pl.ds(pl.multiple_of(d * rows, rows), rows)
            pltpu.make_async_copy(
                held.at[t // 2, spot], outs[(r & 1) * 2 + (r >> 1)].at[j], sem
            ).start()


def each_grad(where, outs, make):
    def over(held, sems):
        nt = held.shape[0]
        if len(outs) == 1:
            for n in range(nt):
                held[n] = make(n)
                load(held.at[n], outs[0].at[n], sems.at[0])
            return lambda: wait(held, sems.at[0])
        keep, send = outs[0], outs[1:]
        for n in range(nt):
            held[n] = make(turn_of(where, n))
            if n == 1:
                store_grads(where, 1, held.at[0:2], send, sems.at[0])
            if n == 3:
                store_grads(where, 0, held.at[2:4], [keep.at[r] for r in range(4)], sems.at[1])
        return lambda: [wait(held.at[2 * n : 2 * n + 2], sems.at[n]) for n in range(2)]

    return over


def outer_kernel(nw, ng, active_in, normed_in, cot_in, rows_in, where, where_split, *rest):
    refs, outs, rest = rest[:nw], rest[nw : nw + ng], rest[nw + ng :]
    out_part, second_out, ffn_out, vec_ref, full, active, normed_ref, cot, second, out_v, ffn = rest[:11]
    turned, held, sem, sem_a, sem_b, sem_out = rest[11:]
    rows = cot.shape[0]
    nt = active.shape[0]
    load_weights(refs, where_split, full, sem)
    for t in range(nt):
        load(active_in.at[t], active.at[t], sem_a.at[t])
    load(normed_in, normed_ref, sem_b.at[0])
    load(cot_in, cot, sem_b.at[1])
    gain1, shift1, outer_bias, gain, shift = (rows_in[n : n + 1, :] for n in range(1, 6))
    vec_ref[...] = jnp.zeros_like(vec_ref)
    for t in range(nt):
        wait(active.at[t], sem_a.at[t])
        wait(full.at[t], sem.at[t])
        part = dot_t(active[t], full[t]).astype(BF).astype(F32)
        second[...] = part if t == 0 else second[...] + part
    wait(normed_ref, sem_b.at[0])
    wait(cot, sem_b.at[1])

    @blocks(rows, 128)
    def _(span):
        first = normed_ref[span, :] * gain1 + shift1
        normed, scale = norm_stats(second[span, :] + outer_bias + first)
        out_v[span, :] = (normed * gain + shift).astype(BF)
        incoming = cot[span, :].astype(F32)
        pull = norm_pull(incoming, normed, scale, gain)
        second[span, :] = pull
        ffn[span, :] = pull.astype(BF)
        vec_ref[0:1, :] += jnp.sum(incoming * normed, axis=0, keepdims=True)
        vec_ref[1:2, :] += jnp.sum(incoming, axis=0, keepdims=True)
        vec_ref[2:3, :] += jnp.sum(pull, axis=0, keepdims=True)

    load(out_v, out_part, sem_out.at[2])
    load(second, second_out, sem_out.at[3])
    load(ffn, ffn_out, sem_out.at[4])
    turned[...] = ffn[...].T
    each_grad(where, outs, lambda t: dot(turned[...], active[t]).astype(BF))(held, sem_out)()
    wait(out_v, sem_out.at[2])
    wait(second, sem_out.at[3])
    wait(ffn, sem_out.at[4])


def middle_kernel(nw, ng, slope_in, second_in, ffn_in, low_in, normed_in, scale_in, rows_in, where, where_split, *rest):
    refs, inner_refs, attn_refs, rest = rest[:nw], rest[nw : 2 * nw], rest[2 * nw : 3 * nw], rest[3 * nw :]
    outs, rest = rest[:ng], rest[ng:]
    attn_in_out, attn_low_out, ctx_grad_out, vec_ref, inner_vec = rest[:5]
    full, inner_full, attn_full, slope, normed_ref, scale_ref, low, second, attn_in, ffn = rest[5:15]
    turned, pulled, ctx_grad, held, sem, sem_a, sem_b, sem_out = rest[15:]
    rows = low.shape[0]
    nt = slope.shape[0]
    load(ffn_in, ffn, sem_b.at[0])
    load_weights(refs, where_split, full, sem.at[0])
    for t in range(nt):
        load(slope_in.at[t], slope.at[t], sem_a.at[t])
    load(low_in, low, sem_b.at[1])
    load_weights(inner_refs, where_split, inner_full, sem.at[1])
    load(second_in, second, sem_b.at[2])
    load(normed_in, normed_ref, sem_b.at[3])
    load(scale_in, scale_ref, sem_b.at[4])
    load_weights(attn_refs, where, attn_full, sem.at[2], 512)
    gain1 = rows_in[1:2, :]
    vec_ref[...] = jnp.zeros_like(vec_ref)
    wait(ffn, sem_b.at[0])
    for t in range(nt):
        wait(full.at[t], sem.at[0, t])
        wait(slope.at[t], sem_a.at[t])
        grad = (dot(ffn[...], full[t]) * slope[t].astype(F32)).astype(BF)
        pulled[t] = grad
        inner_vec[t] = jnp.sum(grad.astype(F32), axis=0, keepdims=True)
    wait(low, sem_b.at[1])
    turned[...] = low[...].T
    done = each_grad(where, outs, lambda t: dot(turned[...], pulled[t]).astype(BF))(held, sem_out)
    for t in range(nt):
        wait(inner_full.at[t], sem.at[1, t])
        part = dot_t(pulled[t], inner_full[t])
        attn_in[...] = part if t == 0 else attn_in[...] + part
    wait(second, sem_b.at[2])
    wait(normed_ref, sem_b.at[3])
    wait(scale_ref, sem_b.at[4])

    @blocks(rows, 128)
    def _(span):
        incoming = attn_in[span, :] + second[span, :]
        normed = normed_ref[span, :]
        grad = norm_pull(incoming, normed, scale_ref[span, 0:1], gain1)
        attn_in[span, :] = grad
        ffn[span, :] = grad.astype(BF)
        vec_ref[0:1, :] += jnp.sum(incoming * normed, axis=0, keepdims=True)
        vec_ref[1:2, :] += jnp.sum(incoming, axis=0, keepdims=True)
        vec_ref[2:3, :] += jnp.sum(grad, axis=0, keepdims=True)

    load(attn_in, attn_in_out, sem_out.at[2])
    load(ffn, attn_low_out, sem_out.at[3])
    low_half = lane_masks(rows)
    for t in range(nt):
        wait(attn_full.at[t], sem.at[2, t])
        got = dot(ffn[...], attn_full[t])
        ctx_grad[t, :, 0:128] = pick(~low_half, got[:, :128]).astype(BF)
        ctx_grad[t, :, 128:256] = got[:, 128:].astype(BF)
        load(ctx_grad.at[t], ctx_grad_out.at[t], sem_out.at[4])
    done()
    wait(attn_in, sem_out.at[2])
    wait(ffn, sem_out.at[3])
    wait(ctx_grad, sem_out.at[4])


def attend_pull(acts, probs, ctx_grad, back, t):
    rows = acts.shape[1]
    low_half = lane_masks(LEN)
    factor = HEAD_DIM ** (-0.5)
    h = HEAD_DIM
    for s in range(rows // LEN):
        span = slice(s * LEN, (s + 1) * LEN)
        q01, k01, v01 = acts[t, span, 0:128], acts[t, span, 128:256], acts[t, span, 256:384]
        qv2, k2 = acts[t, span, 384:512], acts[t, span, 512:640]
        g2, g01 = ctx_grad[t, span, 0:128], ctx_grad[t, span, 128:256]
        heads = (
            (pick(low_half, g01), k01, v01),
            (pick(~low_half, g01), k01, v01),
            (g2, k2, qv2),
        )
        queries, scores = [], []
        for n, (grad, key, value) in enumerate(heads):
            wide = probs[t, s, n].astype(F32)
            pulled = dot_t(grad, value)
            delta = jnp.sum(pulled * wide, axis=-1, keepdims=True)
            scores.append((wide * (pulled - delta)).astype(BF))
            queries.append(dot(scores[n], key) * factor)
        q01t, g01t, qv2t, g2t = q01.T, g01.T, qv2.T, g2.T
        keys01 = jnp.concatenate([dot(q01t[:h], scores[0]), dot(q01t[h:], scores[1])], axis=0) * factor
        values01 = jnp.concatenate([dot(g01t[:h], probs[t, s, 0]), dot(g01t[h:], probs[t, s, 1])], axis=0)
        both2 = jnp.concatenate([dot(qv2t[:h], scores[2]) * factor, dot(g2t[h:], probs[t, s, 2])], axis=0)
        kv2 = both2.astype(BF).T
        back[t, span, 0:128] = jnp.where(low_half, queries[0], queries[1]).astype(BF)
        back[t, span, 128:256] = keys01.astype(BF).T
        back[t, span, 256:384] = values01.astype(BF).T
        back[t, span, 384:512] = jnp.where(low_half, queries[2].astype(BF), kv2)
        back[t, span, 512:640] = pick(low_half, kv2)


def attend_back_kernel(nw, ng, x_ref, attn_low, acts_in, probs_in, ctx_in, ctx_grad_in, attn_in, *rest):
    second_vec, first_vec, inner_vec, where, *rest = rest
    refs, outs, (input_ref, vectors) = rest[:nw], rest[nw : nw + ng], rest[nw + ng : nw + ng + 2]
    full, total, acts, probs, ctx, ctx_grad, back, turned_x, turned_a, held, vec_ref = rest[nw + ng + 2 : -3]
    sem, sem_in, sem_out = rest[-3:]
    nt = acts.shape[0]
    for n in range(nt):
        t = turn_of(where, n) if ng > 1 else n
        load(acts_in.at[t], acts.at[t], sem_in.at[t])
        load(ctx_grad_in.at[t], ctx_grad.at[t], sem_in.at[t])
        load(probs_in.at[t], probs.at[t], sem_in.at[t])
        load(ctx_in.at[t], ctx.at[t], sem_in.at[t])
    load_weights(refs, where, full, sem)
    load(attn_in, total, sem_in.at[nt])
    turned_x[...] = x_ref[...].T
    turned_a[...] = attn_low[...].T

    def make(t):
        for held_in in (acts, ctx_grad, probs, ctx):
            wait(held_in.at[t], sem_in.at[t])
        attend_pull(acts, probs, ctx_grad, back, t)
        vec_ref[t] = jnp.sum(back[t].astype(F32), axis=0, keepdims=True)
        from_x = dot(turned_x[...], back[t])
        from_out = dot(turned_a[...], ctx[t])
        return jnp.concatenate(
            [from_x[:, :512], from_x[:, 512:] + from_out[:, :128], from_out[:, 128:]], axis=1
        ).astype(BF)

    done = each_grad(where, outs, make)(held, sem_out)
    wait(total, sem_in.at[nt])
    for t in range(nt):
        wait(full.at[t], sem.at[t])
        total[...] += dot_t(back[t], full[t, :, 0:640])
    input_ref[...] = total[...].astype(BF)
    vectors[...] = jnp.zeros_like(vectors)
    for at, ref in ((0, second_vec), (3, first_vec)):
        vectors[at : at + 3, :] = ref[0:3, :]
    for n in range(nt):
        vectors[6 + n : 7 + n, :] = inner_vec[n]
        vectors[6 + nt + n : 7 + nt + n, 0:640] = vec_ref[n]
    done()


def place_kernel(order, one, two, three, four, out, held, sem, sem_out):
    rows = one.shape[0]
    parts = (one, two, three, four)
    for n, part in enumerate(parts):
        load(part, held.at[n], sem.at[n])
    for n in range(4):
        wait(held.at[n], sem.at[n])
        spot = pl.ds(pl.multiple_of(order[n] * rows, rows), rows)
        pltpu.make_async_copy(held.at[n], out.at[spot], sem_out.at[n]).start()
    for n in range(4):
        wait(held.at[n], sem_out.at[n])


def widen_kernel(order, one, two, *rest):
    out, held, wide, sem, sem_out = rest[-5:]
    rows = one.shape[0]
    half = rows // 2
    for n, part in enumerate((one, two)):
        load(part, held.at[n], sem.at[n])
    for n in range(2):
        wait(held.at[n], sem.at[n])
        for m in range(2):
            wide[2 * n + m] = held[n, m * half : (m + 1) * half, :].astype(F32)
            spot = pl.ds(pl.multiple_of(order[n] * rows + m * half, half), half)
            pltpu.make_async_copy(wide.at[2 * n + m], out.at[spot], sem_out.at[2 * n + m]).start()
    for n in range(4):
        wait(wide.at[n], sem_out.at[n])


def interleave(q, k, v, o):
    h = HEAD_DIM
    return jnp.concatenate(
        [
            q[..., : 2 * h], k[..., : 2 * h], v[..., : 2 * h],
            q[..., 2 * h :], v[..., 2 * h :], k[..., 2 * h :], o[..., 2 * h :],
            o[..., : 2 * h],
        ],
        axis=-1,
    )


def interleave_kernel(q_in, k_in, v_in, o_in, out, q, k, v, o, sem):
    for n, (ref, held) in enumerate(((q_in, q), (k_in, k), (v_in, v), (o_in, o))):
        load(ref, held, sem.at[n])
    for n, held in enumerate((q, k, v, o)):
        wait(held, sem.at[n])
    out[...] = interleave(q[...].astype(F32), k[...].astype(F32), v[...].astype(F32), o[...].astype(F32).T).astype(BF)


def part_kernel(total, *rest):
    moved, (q, k, v, o) = rest[:-4], rest[-4:]
    grad = total[...]
    for piece in moved:
        grad = grad + piece[0 : grad.shape[0], :].astype(F32)
    h = HEAD_DIM
    part = lambda *spans: jnp.concatenate([grad[:, a * h : b * h] for a, b in spans], axis=1)
    q[...] = part((0, 2), (6, 7))
    k[...] = part((2, 4), (8, 9))
    v[...] = part((4, 6), (7, 8))
    o[...] = part((10, 12), (9, 10)).T


def body(
    plan,
    inputs,
    segments,
    query_weight,
    key_weight,
    value_weight,
    query_bias,
    value_bias,
    out_weight,
    out_bias,
    first_gain,
    first_shift,
    inner_weight,
    inner_bias,
    outer_weight,
    outer_bias,
    second_gain,
    second_shift,
    cotangent,
):
    nt, ndp = plan.nt, plan.ndp
    width = inputs.shape[1]
    local, hidden = query_weight.shape[1], inner_weight.shape[1]
    rows = inputs.shape[0] // nt
    nseq = rows // LEN
    me = lax.axis_index("tensor")
    mine = lambda a, n: lax.dynamic_slice_in_dim(a, me * n, n, 0)
    x = mine(inputs, rows)
    cot = mine(cotangent, rows)
    seg_row = mine(segments, nseq)

    nw = 8 if plan.pieces else 1
    if plan.pieces:
        where, where_split = plan.tables(False), plan.tables(True)
    else:
        where = where_split = jnp.zeros((1, 1), jnp.int32)
    params = jnp.concatenate(
        [
            v.reshape(1, width)
            for v in (out_bias, first_gain, first_shift, outer_bias, second_gain, second_shift, out_bias, out_bias)
        ]
    )
    limit = 56
    LOW = 24 if rows <= 512 else 56
    weights = pltpu.VMEM((nt, width, hidden), BF)
    acted = pltpu.VMEM((nt, rows, hidden), BF)
    dma = pltpu.SemaphoreType.DMA
    any_w = [anywhere()] * nw
    shards = (
        call(
            interleave_kernel,
            [query_weight, key_weight, value_weight, out_weight],
            [anywhere()] * 4,
            [shape((query_weight.shape[0], 4 * local), BF)],
            [vmem()],
            [*[pltpu.VMEM(query_weight.shape, BF)] * 3, pltpu.VMEM(out_weight.shape, BF), dma((4,))],
            limit,
            1,
        )[0],
        inner_weight,
        outer_weight.T,
    )

    def attend(x, bias, attn_w):
        return call(
            functools.partial(attend_kernel, nw),
            [x, seg_row, bias, params, where, *attn_w],
            [vmem()] * 4 + [smem()] + any_w,
            [
                shape((nt, rows, 640), BF),
                shape((nt, nseq, 3, LEN, LEN), BF),
                shape((nt, rows, 256), BF),
                shape((rows, width), F32),
                shape((rows, 128), F32),
                shape((rows, width), BF),
            ],
            [anywhere()] * 3 + [vmem()] * 3,
            [
                weights,
                pltpu.VMEM((nseq, LEN, LEN), F32),
                pltpu.VMEM((nt, rows, 640), BF),
                pltpu.VMEM((nt, nseq, 3, LEN, LEN), BF),
                pltpu.VMEM((nt, rows, 256), BF),
                dma((nt,)),
                dma((3,)),
            ],
            limit,
            13,
        )

    def inner(low, inner_b, inner_w):
        return call(
            functools.partial(inner_kernel, nw),
            [low, inner_b, where_split, *inner_w],
            [vmem()] * 2 + [smem()] + any_w,
            [shape((nt, rows, hidden), BF)] * 2,
            [anywhere()] * 2,
            [weights, pltpu.VMEM((rows, hidden), F32), acted, acted, dma((nt,)), dma((2,))],
            limit,
            13,
        )

    if plan.pieces:
        slot = (plan.nz, width // ndp, hidden)
        grads = [shape((4, *slot), BF)] + [shape(slot, BF)] * 4
    else:
        grads = [shape((nt, width, hidden), BF)]
    ng = len(grads)
    wide, thin = pltpu.VMEM((rows, width), F32), pltpu.VMEM((rows, width), BF)

    def outer(active, normed, outer_w):
        return call(
            functools.partial(outer_kernel, nw, ng),
            [active, normed, cot, params, where, where_split, *outer_w],
            [anywhere()] * 3 + [vmem()] + [smem()] * 2 + any_w,
            [
                *grads,
                shape((rows, width), BF),
                shape((rows, width), F32),
                shape((rows, width), BF),
                shape((8, width), F32),
            ],
            [anywhere()] * (ng + 3) + [vmem()],
            [
                weights, acted, wide, thin, wide, thin, thin, pltpu.VMEM((width, rows), BF), weights,
                dma((nt,)), dma((nt,)), dma((2,)), dma((5,)),
            ],
            limit,
            14,
        )

    def middle(slope, second, ffn, low, normed, scale, outer_w, inner_w, attn_w):
        return call(
            functools.partial(middle_kernel, nw, ng),
            [slope, second, ffn, low, normed, scale, params, where, where_split, *outer_w, *inner_w, *attn_w],
            [anywhere()] * 6 + [vmem()] + [smem()] * 2 + any_w * 3,
            [
                *grads,
                shape((rows, width), F32),
                shape((rows, width), BF),
                shape((nt, rows, 256), BF),
                shape((8, width), F32),
                shape((nt, 1, hidden), F32),
            ],
            [anywhere()] * (ng + 3) + [vmem()] * 2,
            [
                weights, weights, pltpu.VMEM((nt, width, 256), BF), acted, wide,
                pltpu.VMEM((rows, 128), F32), thin, wide, wide, thin,
                pltpu.VMEM((width, rows), BF), acted, pltpu.VMEM((nt, rows, 256), BF), weights,
                dma((3, nt)), dma((nt,)), dma((5,)), dma((5,)),
            ],
            limit,
            0.1,
        )

    def attend_back(attn_low, acts, probs, ctx, ctx_grad, attn_in, vecs, attn_w):
        return call(
            functools.partial(attend_back_kernel, nw, ng),
            [x, attn_low, acts, probs, ctx, ctx_grad, attn_in, *vecs, where, *attn_w],
            [vmem()] * 2 + [anywhere()] * 5 + [vmem()] * 3 + [smem()] + any_w,
            [*grads, shape((rows, width), BF), shape((16, hidden), F32)],
            [anywhere()] * ng + [vmem()] * 2,
            [
                weights,
                pltpu.VMEM((rows, width), F32),
                pltpu.VMEM((nt, rows, 640), BF),
                pltpu.VMEM((nt, nseq, 3, LEN, LEN), BF),
                pltpu.VMEM((nt, rows, 256), BF),
                pltpu.VMEM((nt, rows, 256), BF),
                pltpu.VMEM((nt, rows, 640), BF),
                pltpu.VMEM((width, rows), BF),
                pltpu.VMEM((width, rows), BF),
                weights,
                pltpu.VMEM((nt, 1, 640), F32),
                dma((nt,)),
                dma((nt + 1,)),
                dma((2,)),
            ],
            limit,
            0.1,
        )

    def place(parts):
        order = jnp.stack([me, me ^ 2, me ^ 1, me ^ 3]).astype(jnp.int32)
        return call(
            place_kernel,
            [order, *parts],
            [smem()] + [anywhere()] * 4,
            [shape((nt * rows, width), BF)],
            [anywhere()],
            [pltpu.VMEM((4, rows, width), BF), dma((4,)), dma((4,))],
            limit,
            4,
        )[0]

    def widen(parts, flip, half=None):
        order = jnp.stack([me ^ flip, me ^ flip ^ 1]).astype(jnp.int32)
        more = [] if half is None else [half]
        return call(
            widen_kernel,
            [order, *parts, *more],
            [smem()] + [anywhere()] * (2 + len(more)),
            [shape((nt * rows, width), F32)],
            [anywhere()],
            [pltpu.VMEM((2, rows, width), BF), pltpu.VMEM((4, rows // 2, width), F32), dma((2,)), dma((4,))],
            limit,
            4,
            {3: 0} if more else {},
        )[0]

    def small_parts():
        every = lax.all_gather(jnp.concatenate([query_bias, value_bias, inner_bias]), "tensor", axis=0)
        q_b, v_b = every[:, None, :local], every[:, None, local : 2 * local]
        none = jnp.zeros_like(q_b)
        return interleave(q_b, none, v_b, none), every[:, None, 2 * local :]

    bias, inner_b = small_parts()
    if plan.pieces:
        turn, one_way, other_way, core = plan.turn, plan.first(), plan.second(), plan.core()

        beside = plan.beside()

        def spread(own):
            return [turn(own, one_way), turn(own, other_way)]

        def cores(parts):
            return [turn(v, core) for v in parts]

        near = plan.near(shards[0])
        near, bias, inner_b, x, cot, seg_row, where, where_split, params = tie(
            (near, bias, inner_b, x, cot, seg_row, where, where_split, params)
        )
        own1 = jnp.stack([shards[0], *near])
        two1 = spread(own1)
        a2 = turn(tie(shards[1], own1), plan.step(False))
        two1, a2 = tie((two1, a2))
        both1 = turn(two1[0], other_way)
        cores1 = cores([own1, *two1])
        pair2 = jnp.stack([shards[1], a2])
        b2 = turn(pair2, plan.step(True))
        a3 = turn(tie(shards[2], pair2), plan.step(False))
        both1, cores1, b2, a3 = tie((both1, cores1, b2, a3))
        own2 = jnp.concatenate([pair2, b2])
        two2 = spread(own2)
        pair3 = jnp.stack([shards[2], a3])
        b3 = turn(tie(pair3, own2), plan.step(True))
        attn_w = [own1, *two1, both1, *cores1, turn(both1, core)]
        acts, probs, ctx, normed, scale, low = attend(x, bias, attn_w)
        two2, b3, low = tie((two2, b3, low))
        own3 = jnp.concatenate([pair3, b3])
        both2 = turn(two2[0], other_way)
        cores2 = cores([own2, *two2])
        two3 = spread(own3)
        both2, cores2 = tie((both2, cores2))
        inner_w = [own2, *two2, both2, *cores2, turn(both2, core)]
        active, slope = inner(low, inner_b, inner_w)
        two3, active = tie((two3, active))
        both3 = turn(two3[0], other_way)
        cores3 = cores([own3, *two3])
        both3, cores3 = tie((both3, cores3))
        outer_w = [own3, *two3, both3, *cores3, turn(both3, core)]
        keep3, *send3, layer_part, second, ffn, second_vec = outer(active, normed, outer_w)

        got3 = cores(send3)
        layer_x = turn(layer_part, beside)
        keep2, *send2, attn_in, attn_low, ctx_grad, first_vec, inner_vec = middle(
            slope, second, tie((ffn, send3))[0], low, normed, scale, outer_w, inner_w, attn_w
        )
        got3, layer_x, send2, ctx_grad = tie((got3, layer_x, send2, ctx_grad))
        away3 = plan.scatter_a(keep3, got3)
        got3a = turn(away3, one_way)
        got2 = cores(send2)
        layer_c = cores([layer_part, layer_x])
        got2, layer_c, ctx_grad = tie((got2, layer_c, ctx_grad))
        away2 = plan.scatter_a(keep2, got2)
        got2a = turn(away2, one_way)
        keep1, *send1, input_low, vectors = attend_back(
            attn_low, acts, probs, ctx, tie((ctx_grad, away2))[0], attn_in, (second_vec, first_vec, inner_vec), attn_w
        )
        got1 = cores(send1)
        vector_c = turn(vectors, core)
        packed = 2 * vectors.shape[0]
        got3a, got2a, got1, vector_c, input_low = tie((got3a, got2a, got1, vector_c, input_low))
        away3 = plan.scatter_b(keep3, got3, got3a)
        got3b = turn(away3, other_way)
        away2 = plan.scatter_b(keep2, got2, got2a)
        got2b = turn(away2, other_way)
        vectors = vectors + vector_c
        away1 = plan.scatter_a(keep1, got1)
        flat = (-1, hidden)
        away1 = jnp.concatenate([away1.reshape(flat), pack(vectors)])
        got1a = turn(away1, one_way)
        input_c = turn(input_low, core)
        layer_out = place(tie(([layer_part, layer_x, *layer_c], away1))[0])
        got3b, layer_out = tie((got3b, layer_out))
        z3 = plan.scatter_left(keep3, got3, got3a, got3b)
        moved3 = plan.go_z(z3[1])
        half_grad = widen(tie(([input_low, input_c], z3))[0], 0)
        got2b, half_grad = tie((got2b, half_grad))
        z2 = plan.scatter_left(keep2, got2, got2a, got2b)
        moved2 = plan.go_z(z2[1])
        got1a, z2, moved3 = tie((got1a, z2, moved3))
        vectors = vectors + unpack(got1a[-packed:])
        got1a = got1a[:-packed].reshape(2, *slot)
        away = plan.scatter_b(keep1, got1, got1a)
        away = jnp.concatenate([away.reshape(flat), pack(vectors)])
        got1b = turn(away, other_way)
        got1b, moved2 = tie((got1b, moved2))
        vectors = vectors + unpack(got1b[-packed:])
        got1b = got1b[:-packed].reshape(slot)
        z1 = plan.scatter_left(keep1, got1, got1a, got1b)
        packs = pack(vectors)
        z1 = z1[0], [jnp.concatenate([v, packs]) for v in z1[1]]
        input_low = tie((input_low, z1[0]))[0]
        moved1 = plan.go_z(z1[1])
        input_x = turn(input_low, beside)
        outer_grad = plan.last(z3[0], moved3)
        inner_grad = plan.last(z2[0], moved2)
        input_x, moved1, outer_grad, inner_grad = tie((input_x, moved1, outer_grad, inner_grad))
        input_xc = turn(input_x, core)
        vectors = plan.last(vectors, [unpack(v[-packed:]) for v in moved1])
        attn_grads = call(
            part_kernel,
            [z1[0], *moved1],
            [vmem()] * (1 + len(moved1)),
            [shape((width // ndp, local), F32)] * 3 + [shape((local, width // ndp), F32)],
            [vmem()] * 4,
            [],
            16,
            1,
        )
        input_grad = widen([input_x, input_xc], 2, half_grad)
    else:
        attn_w, inner_w, outer_w = (
            [lax.all_gather(lax.all_gather(s, "dp", axis=0, tiled=True), "tensor", axis=0)]
            for s in shards
        )
        acts, probs, ctx, normed, scale, low = attend(x, bias, attn_w)
        active, slope = inner(low, inner_b, inner_w)
        outer_g, layer_part, second, ffn, second_vec = outer(active, normed, outer_w)
        inner_g, attn_in, attn_low, ctx_grad, first_vec, inner_vec = middle(
            slope, second, ffn, low, normed, scale, outer_w, inner_w, attn_w
        )
        attn_g, input_low, vectors = attend_back(
            attn_low, acts, probs, ctx, ctx_grad, attn_in, (second_vec, first_vec, inner_vec), attn_w
        )
        outer_grad, inner_grad, attn_g = (
            lax.psum_scatter(
                lax.psum_scatter(g, "tensor", scatter_dimension=0, tiled=False),
                "dp",
                scatter_dimension=0,
                tiled=True,
            ).astype(F32)
            for g in (outer_g, inner_g, attn_g)
        )
        layer_out = lax.all_gather(layer_part, "tensor", axis=0, tiled=True)
        input_grad = lax.all_gather(input_low, "tensor", axis=0, tiled=True).astype(F32)

    if not plan.pieces:
        vectors = lax.psum(vectors, AXES)
    gain2, shift2, bias2, gain1, shift1, bias1 = (vectors[n] for n in range(6))
    inner_bias_grad = lax.dynamic_index_in_dim(vectors, 6 + me, 0, keepdims=False)
    mine_vec = lax.dynamic_index_in_dim(vectors, 6 + nt + me, 0, keepdims=False)
    h = HEAD_DIM
    query_bias_grad = jnp.concatenate([mine_vec[: 2 * h], mine_vec[6 * h : 7 * h]])
    value_bias_grad = jnp.concatenate([mine_vec[4 * h : 6 * h], mine_vec[7 * h : 8 * h]])
    if not plan.pieces:
        part = lambda *spans: jnp.concatenate([attn_g[:, a * h : b * h] for a, b in spans], axis=1)
        attn_grads = part((0, 2), (6, 7)), part((2, 4), (8, 9)), part((4, 6), (7, 8)), part((10, 12), (9, 10)).T
    return (
        layer_out,
        input_grad,
        *attn_grads[:3],
        query_bias_grad,
        value_bias_grad,
        attn_grads[3],
        bias1,
        gain1,
        shift1,
        inner_grad,
        inner_bias_grad,
        outer_grad.T,
        bias2,
        gain2,
        shift2,
    )


def solution(mesh):
    in_specs = (
        P("dp", None),
        P("dp", None),
        P("dp", "tensor"),
        P("dp", "tensor"),
        P("dp", "tensor"),
        P("tensor"),
        P("tensor"),
        P("tensor", "dp"),
        P(),
        P(),
        P(),
        P("dp", "tensor"),
        P("tensor"),
        P("tensor", "dp"),
        P(),
        P(),
        P(),
        P("dp", None),
    )
    out_specs = (
        P("dp", None),
        P("dp", None),
        P("dp", "tensor"),
        P("dp", "tensor"),
        P("dp", "tensor"),
        P("tensor"),
        P("tensor"),
        P("tensor", "dp"),
        P(),
        P(),
        P(),
        P("dp", "tensor"),
        P("tensor"),
        P("tensor", "dp"),
        P(),
        P(),
        P(),
    )
    return jax.shard_map(
        functools.partial(body, Plan(mesh)),
        mesh=mesh,
        in_specs=in_specs,
        out_specs=out_specs,
        check_vma=False,
    )
```

```python
import functools
import math

import jax
import jax.numpy as jnp
from jax import lax
from jax.experimental import pallas as pl
from jax.experimental.pallas import tpu as pltpu
from jax.sharding import PartitionSpec as P

HEAD_DIM = 64
LEN = 256
EPS = 1e-06
BF = jnp.bfloat16
F32 = jnp.float32
AXES = ("dp", "tensor")
MIB = 1 << 20
SCALE = 0.3


def dot(left, right):
    return lax.dot_general(left, right, (((1,), (0,)), ((), ())), preferred_element_type=F32)


def dot_t(left, right):
    return lax.dot_general(left, right, (((1,), (1,)), ((), ())), preferred_element_type=F32)


def t_dot(left, right):
    return lax.dot_general(left, right, (((0,), (0,)), ((), ())), preferred_element_type=F32)


def vmem():
    return pl.BlockSpec(memory_space=pltpu.VMEM)


def smem():
    return pl.BlockSpec(memory_space=pltpu.SMEM)


def anywhere():
    return pl.BlockSpec(memory_space=pl.ANY)


def call(body, ins, in_specs, outs, out_specs, scratch, limit, cost, aliases={}):
    return pl.pallas_call(
        body,
        out_shape=outs,
        in_specs=in_specs,
        out_specs=out_specs,
        scratch_shapes=scratch,
        input_output_aliases=aliases,
        compiler_params=pltpu.CompilerParams(vmem_limit_bytes=limit * MIB),
        cost_estimate=pl.CostEstimate(flops=int(cost * SCALE * 1e9), bytes_accessed=1000, transcendentals=0),
    )(*ins)


def shape(dims, dtype):
    return jax.ShapeDtypeStruct(dims, dtype)


class Plan:
    def __init__(self, mesh):
        self.ndp, self.nt = mesh.shape["dp"], mesh.shape["tensor"]
        self.pieces = self.nt == 4 and self.ndp == 8
        self.nz = self.ndp // 2

    def pairs(self, move):
        found = []
        for d in range(self.ndp):
            for t in range(self.nt):
                z, y, x, c = move(d >> 1, d & 1, t >> 1, t & 1)
                found.append((d * self.nt + t, (z * 2 + y) * self.nt + x * 2 + c))
        return found

    def first(self):
        return self.pairs(lambda z, y, x, c: (z, y, x ^ 1, c) if c == 0 else (z, y ^ 1, x, c))

    def second(self):
        return self.pairs(lambda z, y, x, c: (z, y, x ^ 1, c) if c == 1 else (z, y ^ 1, x, c))

    def core(self):
        return self.pairs(lambda z, y, x, c: (z, y, x, c ^ 1))

    def along(self, j):
        return self.pairs(lambda z, y, x, c: (z ^ j, y, x, c))

    def step(self, last):
        return self.pairs(lambda z, y, x, c: (z ^ (1 if (c == 0) != last else 2), y, x, c))

    def tables(self, split):
        d, t = lax.axis_index("dp"), lax.axis_index("tensor")
        z, y, x, c = d >> 1, d & 1, t >> 1, t & 1
        s = jnp.arange(2)[:, None, None]
        r = jnp.arange(4)[None, :, None]
        j = jnp.arange(self.nz)[None, None, :]
        a, b = r & 1, r >> 1
        core = c ^ s
        dx, dy = jnp.where(core == 0, a, b), jnp.where(core == 0, b, a)
        if split:
            j = jnp.where(core == 0, j, (j & 1) * 2 + (j >> 1))
        where_t = jnp.broadcast_to((x ^ dx) * 2 + core, (2, 4, self.nz))
        where_d = jnp.broadcast_to((z ^ j) * 2 + (y ^ dy), (2, 4, self.nz))
        return jnp.stack([where_t.reshape(-1), where_d.reshape(-1)]).astype(jnp.int32)

    def turn(self, values, pairs):
        return lax.ppermute(values, AXES, pairs)

    def near(self, shard):
        return [self.turn(shard, self.along(j)) for j in range(1, self.nz)]

    def beside(self):
        return self.pairs(lambda z, y, x, c: (z, y, x ^ 1, c))

    def scatter_a(self, keep, got):
        return (keep[2:].astype(F32) + jnp.stack(got[2:]).astype(F32)).astype(BF)

    def scatter_b(self, keep, got, got_a):
        return (keep[1].astype(F32) + got[1].astype(F32) + got_a[1].astype(F32)).astype(BF)

    def scatter_left(self, keep, got, got_a, got_b):
        return keep[0].astype(F32) + got[0].astype(F32) + got_a[0].astype(F32) + got_b.astype(F32)

    def half_z(self, left):
        return self.turn(left[2:].astype(BF), self.step(True))

    def last_z(self, values):
        return self.turn(values.astype(BF), self.step(False))


def load_weights(refs, where, full, sem, start=0, before=0):
    columns = pl.ds(start, full.shape[2])
    if not refs:
        return
    if len(refs) == 1:
        for t in range(full.shape[0]):
            pltpu.make_async_copy(refs[0].at[t, :, columns], full.at[t], sem.at[t]).start()
        return
    nz, rows, _ = refs[0].shape
    for r, ref in enumerate(refs):
        for j in range(nz):
            n = (before + r) * nz + j
            t, d = where[0, n], where[1, n]
            spot = pl.ds(pl.multiple_of(d * rows, rows), rows)
            pltpu.make_async_copy(ref.at[j, :, columns], full.at[t, spot], sem.at[t]).start()


def load(ref, held, sem):
    pltpu.make_async_copy(ref, held, sem).start()


def wait(held, sem):
    pltpu.make_async_copy(held, held, sem).wait()


def blocks(rows, block):
    def over(run):
        @pl.loop(0, rows // block)
        def _(i):
            run(pl.ds(pl.multiple_of(i * block, block), block))

    return over


def pack(vectors):
    high = vectors.astype(BF)
    return jnp.concatenate([high, (vectors - high.astype(F32)).astype(BF)])


def unpack(rows):
    half = rows.shape[0] // 2
    return rows[:half].astype(F32) + rows[half:].astype(F32)


def tie(values, *after):
    if after:
        return lax.optimization_barrier((values, *after))[0]
    return lax.optimization_barrier(values)


def lane_masks(rows):
    lane = lax.broadcasted_iota(jnp.int32, (rows, 128), 1)
    return lane < HEAD_DIM


def pick(mask, values):
    return jnp.where(mask, values, jnp.zeros_like(values))


def norm_stats(hidden):
    center = hidden - jnp.mean(hidden, axis=-1, keepdims=True)
    scale = lax.rsqrt(jnp.mean(center * center, axis=-1, keepdims=True) + EPS)
    return center * scale, scale


def norm_pull(incoming, normed, scale, gain):
    scaled = incoming * gain
    return scale * (
        scaled
        - jnp.mean(scaled, axis=-1, keepdims=True)
        - normed * jnp.mean(scaled * normed, axis=-1, keepdims=True)
    )


def attend_kernel(nw, x_ref, seg_row, bias, params, where, *rest):
    refs, rest = rest[:nw], rest[nw:]
    acts_out, probs_out, ctx_out, normed_ref, scale_ref, low_ref = rest[:6]
    full, keep, acts, probs, ctx, sem, sem_out = rest[6:]
    rows = x_ref.shape[0]
    nt = acts.shape[0]
    load_weights(refs, where, full, sem)
    nseq = rows // LEN
    for s in range(nseq):
        own = seg_row[s : s + 1, :].astype(F32)
        same = jnp.broadcast_to(own, (8, LEN)).T[:, 0:1] == own
        keep[s] = jnp.where(same, 0.0, -1e30).astype(F32)
    low_half = lane_masks(LEN)
    ones = jnp.ones((LEN, 128), BF)

    normed_ref[...] = x_ref[...].astype(F32) + params[0:1, :]

    @pl.loop(0, nt)
    def _(t):
        wait(full.at[t], sem.at[t])
        x = x_ref[...]
        acts[t, :, 0:512] = (dot(x, full[t, :, 0:512]) + bias[t, :, 0:512]).astype(BF)
        last = dot(x, full[t, :, 512:640]).astype(BF)
        acts[t, :, 512:640] = pick(lane_masks(rows), last)

        for s in range(nseq):
            span = slice(s * LEN, (s + 1) * LEN)
            q01, k01, v01 = acts[t, span, 0:128], acts[t, span, 128:256], acts[t, span, 256:384]
            qv2, k2 = acts[t, span, 384:512], acts[t, span, 512:640]
            heads = (
                (pick(low_half, q01), k01, v01),
                (pick(~low_half, q01), k01, v01),
                (pick(low_half, qv2), k2, qv2),
            )
            done = []
            for h, (query, key, value) in enumerate(heads):
                scores = dot_t(query, key) * HEAD_DIM ** (-0.5) + keep[s]
                top = jnp.max(scores, axis=-1, keepdims=True)
                expo = jnp.exp(scores - top)
                low = expo.astype(BF)
                mixed = dot(low, jnp.concatenate([value, ones], axis=1))
                inverse = 1.0 / mixed[:, 128:]
                probs[t, s, h] = (expo * jnp.concatenate([inverse, inverse], axis=1)).astype(BF)
                done.append(mixed[:, :128] * inverse)
            ctx[t, span, 0:128] = pick(~low_half, done[2]).astype(BF)
            ctx[t, span, 128:256] = jnp.where(low_half, done[0], done[1]).astype(BF)
        pltpu.make_async_copy(acts.at[t], acts_out.at[t], sem_out.at[0]).start()
        pltpu.make_async_copy(probs.at[t], probs_out.at[t], sem_out.at[1]).start()
        pltpu.make_async_copy(ctx.at[t], ctx_out.at[t], sem_out.at[2]).start()
        part = dot_t(ctx[t], full[t, :, 512:768]).astype(BF)
        normed_ref[...] += part.astype(F32)

    @blocks(rows, 128)
    def _(span):
        normed, scale = norm_stats(normed_ref[span, :])
        normed_ref[span, :] = normed
        scale_ref[span, :] = jnp.broadcast_to(scale, (128, 128))
        low_ref[span, :] = (normed * params[1:2, :] + params[2:3, :]).astype(BF)

    wait(acts, sem_out.at[0])
    wait(probs, sem_out.at[1])
    wait(ctx, sem_out.at[2])


TAIL_STEP = 0.43 / math.sqrt(2.0)
TAIL = (
    0.12125730288161489,
    0.12218773837809233,
    0.1024754485844625,
    0.12342253549698744,
    -0.04286343715820851,
    0.19185342214732998,
    -0.15518700012679373,
    0.036854031729008835,
)


def normal_parts(values):
    t = 1.0 / (1.0 + TAIL_STEP * jnp.abs(values))
    bell = jnp.exp2(values * values * (-0.5 * math.log2(math.e)))
    poly = TAIL[-1]
    for c in TAIL[-2::-1]:
        poly = c + t * poly
    tail = t * poly * bell
    return jnp.where(values >= 0, 1.0 - tail, tail), bell


def inner_kernel(nw, low_ref, bias, where, *rest):
    refs, rest = rest[:nw], rest[nw:]
    active_out, slope_out, full, inner_ref, active, slope, sem, sem_out = rest
    rows = low_ref.shape[0]
    nt = active.shape[0]
    load_weights(refs, where, full, sem)

    @pl.loop(0, nt)
    def _(t):
        wait(full.at[t], sem.at[t])
        inner_ref[...] = dot(low_ref[...], full[t]) + bias[t]

        @blocks(rows, 64)
        def _(span):
            inner = inner_ref[span, :]
            phi, bell = normal_parts(inner)
            active[t, span, :] = (inner * phi).astype(BF)
            slope[t, span, :] = (phi + inner * bell * (1.0 / math.sqrt(2.0 * math.pi))).astype(BF)

        pltpu.make_async_copy(active.at[t], active_out.at[t], sem_out.at[0]).start()
        pltpu.make_async_copy(slope.at[t], slope_out.at[t], sem_out.at[1]).start()

    wait(active, sem_out.at[0])
    wait(slope, sem_out.at[1])


def turn_of(where, n):
    return 2 * (n % 2) + ((where[0, 0] % 2) ^ (1 - n // 2))


def store_grads(where, side, held, outs, sem):
    nz, rows = outs[0].shape[0], outs[0].shape[1]
    for r in range(4):
        for j in range(nz):
            n = (side * 4 + r) * nz + j
            t, d = where[0, n], where[1, n]
            spot = pl.ds(pl.multiple_of(d * rows, rows), rows)
            pltpu.make_async_copy(
                held.at[t // 2, spot], outs[(r & 1) * 2 + (r >> 1)].at[j], sem
            ).start()


def each_grad(where, outs, make):
    def over(held, sems):
        nt = held.shape[0]
        if len(outs) == 1:
            for n in range(nt):
                held[n] = make(n)
                load(held.at[n], outs[0].at[n], sems.at[0])
            return lambda: wait(held, sems.at[0])
        keep, send = outs[0], outs[1:]
        for n in range(nt):
            held[n] = make(turn_of(where, n))
            if n == 1:
                store_grads(where, 1, held.at[0:2], send, sems.at[0])
            if n == 3:
                store_grads(where, 0, held.at[2:4], [keep.at[r] for r in range(4)], sems.at[1])
        return lambda: [wait(held.at[2 * n : 2 * n + 2], sems.at[n]) for n in range(2)]

    return over


def outer_kernel(nw, ng, active_in, normed_in, cot_in, rows_in, where, where_split, *rest):
    refs, outs, rest = rest[:nw], rest[nw : nw + ng], rest[nw + ng :]
    out_part, second_out, ffn_out, vec_ref, full, active, normed_ref, cot, second, out_v, ffn = rest[:11]
    turned, held, sem, sem_a, sem_b, sem_out = rest[11:]
    rows = cot.shape[0]
    nt = active.shape[0]
    load_weights(refs[: nw // 2], where_split, full, sem)
    turns = [turn_of(where, n) for n in (2, 3, 0, 1)]
    for t in turns[:2]:
        load(active_in.at[t], active.at[t], sem_a.at[t])
    load_weights(refs[nw // 2 :], where_split, full, sem, 0, nw // 2)
    for t in turns[2:]:
        load(active_in.at[t], active.at[t], sem_a.at[t])
    load(normed_in, normed_ref, sem_b.at[0])
    load(cot_in, cot, sem_b.at[1])
    gain1, shift1, outer_bias, gain, shift = (rows_in[n : n + 1, :] for n in range(1, 6))
    vec_ref[...] = jnp.zeros_like(vec_ref)
    for n, t in enumerate(turns):
        wait(active.at[t], sem_a.at[t])
        wait(full.at[t], sem.at[t])
        part = dot_t(active[t], full[t]).astype(BF).astype(F32)
        second[...] = part if n == 0 else second[...] + part
    wait(normed_ref, sem_b.at[0])
    wait(cot, sem_b.at[1])

    @blocks(rows, 128)
    def _(span):
        first = normed_ref[span, :] * gain1 + shift1
        normed, scale = norm_stats(second[span, :] + outer_bias + first)
        out_v[span, :] = (normed * gain + shift).astype(BF)
        incoming = cot[span, :].astype(F32)
        pull = norm_pull(incoming, normed, scale, gain)
        second[span, :] = pull
        ffn[span, :] = pull.astype(BF)
        vec_ref[0:1, :] += jnp.sum(incoming * normed, axis=0, keepdims=True)
        vec_ref[1:2, :] += jnp.sum(incoming, axis=0, keepdims=True)
        vec_ref[2:3, :] += jnp.sum(pull, axis=0, keepdims=True)

    load(out_v, out_part, sem_out.at[2])
    load(second, second_out, sem_out.at[3])
    load(ffn, ffn_out, sem_out.at[4])
    turned[...] = ffn[...].T
    each_grad(where_split, outs, lambda t: dot(turned[...], active[t]).astype(BF))(held, sem_out)()
    wait(out_v, sem_out.at[2])
    wait(second, sem_out.at[3])
    wait(ffn, sem_out.at[4])


def middle_kernel(nw, ng, slope_in, second_in, ffn_in, low_in, normed_in, scale_in, rows_in, where, where_split, *rest):
    refs, inner_refs, attn_refs, rest = rest[:nw], rest[nw : 2 * nw], rest[2 * nw : 3 * nw], rest[3 * nw :]
    outs, rest = rest[:ng], rest[ng:]
    attn_in_out, attn_low_out, ctx_grad_out, vec_ref, inner_vec = rest[:5]
    full, inner_full, attn_full, slope, normed_ref, scale_ref, low, second, attn_in, ffn = rest[5:15]
    turned, pulled, ctx_grad, held, sem, sem_a, sem_b, sem_out = rest[15:]
    rows = low.shape[0]
    nt = slope.shape[0]
    load(ffn_in, ffn, sem_b.at[0])
    load_weights(refs, where_split, full, sem.at[0])
    for t in [turn_of(where, n) for n in (2, 3, 0, 1)]:
        load(slope_in.at[t], slope.at[t], sem_a.at[t])
    load(low_in, low, sem_b.at[1])
    load_weights(inner_refs, where_split, inner_full, sem.at[1])
    load(second_in, second, sem_b.at[2])
    load(normed_in, normed_ref, sem_b.at[3])
    load(scale_in, scale_ref, sem_b.at[4])
    load_weights(attn_refs, where, attn_full, sem.at[2], 512)
    gain1 = rows_in[1:2, :]
    vec_ref[...] = jnp.zeros_like(vec_ref)
    wait(ffn, sem_b.at[0])
    for t in [turn_of(where, n) for n in (2, 3, 0, 1)]:
        wait(full.at[t], sem.at[0, t])
        wait(slope.at[t], sem_a.at[t])
        grad = (dot(ffn[...], full[t]) * slope[t].astype(F32)).astype(BF)
        pulled[t] = grad
        inner_vec[t] = jnp.sum(grad.astype(F32), axis=0, keepdims=True)
    wait(low, sem_b.at[1])
    turned[...] = low[...].T
    done = each_grad(where_split, outs, lambda t: dot(turned[...], pulled[t]).astype(BF))(held, sem_out)
    for t in range(nt):
        wait(inner_full.at[t], sem.at[1, t])
        part = dot_t(pulled[t], inner_full[t])
        attn_in[...] = part if t == 0 else attn_in[...] + part
    wait(second, sem_b.at[2])
    wait(normed_ref, sem_b.at[3])
    wait(scale_ref, sem_b.at[4])

    @blocks(rows, 128)
    def _(span):
        incoming = attn_in[span, :] + second[span, :]
        normed = normed_ref[span, :]
        grad = norm_pull(incoming, normed, scale_ref[span, 0:1], gain1)
        attn_in[span, :] = grad
        ffn[span, :] = grad.astype(BF)
        vec_ref[0:1, :] += jnp.sum(incoming * normed, axis=0, keepdims=True)
        vec_ref[1:2, :] += jnp.sum(incoming, axis=0, keepdims=True)
        vec_ref[2:3, :] += jnp.sum(grad, axis=0, keepdims=True)

    load(attn_in, attn_in_out, sem_out.at[2])
    load(ffn, attn_low_out, sem_out.at[3])
    low_half = lane_masks(rows)
    for t in range(nt):
        wait(attn_full.at[t], sem.at[2, t])
        got = dot(ffn[...], attn_full[t])
        ctx_grad[t, :, 0:128] = pick(~low_half, got[:, :128]).astype(BF)
        ctx_grad[t, :, 128:256] = got[:, 128:].astype(BF)
        load(ctx_grad.at[t], ctx_grad_out.at[t], sem_out.at[4])
    done()
    wait(attn_in, sem_out.at[2])
    wait(ffn, sem_out.at[3])
    wait(ctx_grad, sem_out.at[4])


def attend_pull(acts, probs, ctx_grad, back, t):
    rows = acts.shape[1]
    low_half = lane_masks(LEN)
    factor = HEAD_DIM ** (-0.5)
    h = HEAD_DIM
    for s in range(rows // LEN):
        span = slice(s * LEN, (s + 1) * LEN)
        q01, k01, v01 = acts[t, span, 0:128], acts[t, span, 128:256], acts[t, span, 256:384]
        qv2, k2 = acts[t, span, 384:512], acts[t, span, 512:640]
        g2, g01 = ctx_grad[t, span, 0:128], ctx_grad[t, span, 128:256]
        heads = (
            (pick(low_half, g01), k01, v01),
            (pick(~low_half, g01), k01, v01),
            (g2, k2, qv2),
        )
        queries, scores = [], []
        for n, (grad, key, value) in enumerate(heads):
            wide = probs[t, s, n].astype(F32)
            pulled = dot_t(grad, value)
            delta = jnp.sum(pulled * wide, axis=-1, keepdims=True)
            scores.append((wide * (pulled - delta)).astype(BF))
            queries.append(dot(scores[n], key) * factor)
        q01t, g01t, qv2t, g2t = q01.T, g01.T, qv2.T, g2.T
        keys01 = jnp.concatenate([dot(q01t[:h], scores[0]), dot(q01t[h:], scores[1])], axis=0) * factor
        values01 = jnp.concatenate([dot(g01t[:h], probs[t, s, 0]), dot(g01t[h:], probs[t, s, 1])], axis=0)
        both2 = jnp.concatenate([dot(qv2t[:h], scores[2]) * factor, dot(g2t[h:], probs[t, s, 2])], axis=0)
        kv2 = both2.astype(BF).T
        back[t, span, 0:128] = jnp.where(low_half, queries[0], queries[1]).astype(BF)
        back[t, span, 128:256] = keys01.astype(BF).T
        back[t, span, 256:384] = values01.astype(BF).T
        back[t, span, 384:512] = jnp.where(low_half, queries[2].astype(BF), kv2)
        back[t, span, 512:640] = pick(low_half, kv2)


def attend_back_kernel(nw, ng, x_ref, attn_low, acts_in, probs_in, ctx_in, ctx_grad_in, attn_in, *rest):
    second_vec, first_vec, inner_vec, where, where_split, *rest = rest
    refs, outs, (input_a, input_b, vectors, packs) = rest[:nw], rest[nw : nw + ng], rest[nw + ng : nw + ng + 4]
    full, total, acts, probs, ctx, ctx_grad, back, turned_x, turned_a, held, vec_ref = rest[nw + ng + 4 : -3]
    sem, sem_in, sem_out = rest[-3:]
    nt = acts.shape[0]
    for n in range(nt):
        t = turn_of(where, n) if ng > 1 else n
        load(acts_in.at[t], acts.at[t], sem_in.at[t])
        load(ctx_grad_in.at[t], ctx_grad.at[t], sem_in.at[t])
        load(probs_in.at[t], probs.at[t], sem_in.at[t])
        load(ctx_in.at[t], ctx.at[t], sem_in.at[t])
    load_weights(refs, where, full, sem)
    load(attn_in, total, sem_in.at[nt])
    turned_x[...] = x_ref[...].T
    turned_a[...] = attn_low[...].T

    def make(t):
        for held_in in (acts, ctx_grad, probs, ctx):
            wait(held_in.at[t], sem_in.at[t])
        attend_pull(acts, probs, ctx_grad, back, t)
        vec_ref[t] = jnp.sum(back[t].astype(F32), axis=0, keepdims=True)
        from_x = dot(turned_x[...], back[t])
        from_out = dot(turned_a[...], ctx[t])
        return jnp.concatenate(
            [from_x[:, :512], from_x[:, 512:] + from_out[:, :128], from_out[:, 128:]], axis=1
        ).astype(BF)

    done = each_grad(where_split, outs, make)(held, sem_out)
    wait(total, sem_in.at[nt])
    for t in range(nt):
        wait(full.at[t], sem.at[t])
        total[...] += dot_t(back[t], full[t, :, 0:640])
    half = total.shape[0] // 2
    input_a[...] = total[:half, :].astype(BF)
    input_b[...] = total[half:, :].astype(BF)
    vectors[...] = jnp.zeros_like(vectors)
    for at, ref in ((0, second_vec), (3, first_vec)):
        vectors[at : at + 3, :] = ref[0:3, :]
    for n in range(nt):
        vectors[6 + n : 7 + n, :] = inner_vec[n]
        sums, h = vec_ref[n], HEAD_DIM
        vectors[6 + nt + n : 7 + nt + n, 0 : 6 * h] = jnp.concatenate(
            [sums[:, : 2 * h], sums[:, 6 * h : 7 * h], sums[:, 4 * h : 6 * h], sums[:, 7 * h : 8 * h]], axis=1
        )
    sums = vectors[...]
    packs[...] = jnp.concatenate([sums, sums - sums.astype(BF).astype(F32)]).astype(BF)
    done()


def place_kernel(order, one, two, three, four, out, held, sem, sem_out):
    rows = one.shape[0]
    parts = (one, two, three, four)
    for n, part in enumerate(parts):
        load(part, held.at[n], sem.at[n])
    for n in range(4):
        wait(held.at[n], sem.at[n])
        spot = pl.ds(pl.multiple_of(order[n] * rows, rows), rows)
        pltpu.make_async_copy(held.at[n], out.at[spot], sem_out.at[n]).start()
    for n in range(4):
        wait(held.at[n], sem_out.at[n])


def widen_kernel(order, *rest):
    parts, (out, held, wide, sem, sem_out) = rest[:4], rest[-5:]
    half = parts[0].shape[0]
    for n, part in enumerate(parts):
        load(part, held.at[n], sem.at[n])
    for n in range(4):
        wait(held.at[n], sem.at[n])
        wide[n] = held[n].astype(F32)
        spot = pl.ds(pl.multiple_of((order[n // 2] * 2 + n % 2) * half, half), half)
        load(wide.at[n], out.at[spot], sem_out.at[n])
    for n in range(4):
        wait(wide.at[n], sem_out.at[n])


def interleave(q, k, v, o):
    h = HEAD_DIM
    return jnp.concatenate(
        [
            q[..., : 2 * h], k[..., : 2 * h], v[..., : 2 * h],
            q[..., 2 * h :], v[..., 2 * h :], k[..., 2 * h :], o[..., 2 * h :],
            o[..., : 2 * h],
        ],
        axis=-1,
    )


def interleave_kernel(q_in, k_in, v_in, o_in, out, q, k, v, o, sem):
    for n, (ref, held) in enumerate(((q_in, q), (k_in, k), (v_in, v), (o_in, o))):
        load(ref, held, sem.at[n])
    for n, held in enumerate((q, k, v, o)):
        wait(held, sem.at[n])
    out[...] = interleave(q[...].astype(F32), k[...].astype(F32), v[...].astype(F32), o[...].astype(F32).T).astype(BF)


def part_kernel(total, moved, q, k, v, o):
    grad = total[...] + moved[0 : total.shape[0], :].astype(F32)
    h = HEAD_DIM
    part = lambda *spans: jnp.concatenate([grad[:, a * h : b * h] for a, b in spans], axis=1)
    q[...] = part((0, 2), (6, 7))
    k[...] = part((2, 4), (8, 9))
    v[...] = part((4, 6), (7, 8))
    o[...] = part((10, 12), (9, 10)).T


def body(
    plan,
    inputs,
    segments,
    query_weight,
    key_weight,
    value_weight,
    query_bias,
    value_bias,
    out_weight,
    out_bias,
    first_gain,
    first_shift,
    inner_weight,
    inner_bias,
    outer_weight,
    outer_bias,
    second_gain,
    second_shift,
    cotangent,
):
    nt, ndp = plan.nt, plan.ndp
    width = inputs.shape[1]
    local, hidden = query_weight.shape[1], inner_weight.shape[1]
    rows = inputs.shape[0] // nt
    nseq = rows // LEN
    me = lax.axis_index("tensor")
    mine = lambda a, n: lax.dynamic_slice_in_dim(a, me * n, n, 0)
    x = mine(inputs, rows)
    cot = mine(cotangent, rows)
    seg_row = mine(segments, nseq)

    nw = 8 if plan.pieces else 1
    if plan.pieces:
        where, where_split = plan.tables(False), plan.tables(True)
    else:
        where = where_split = jnp.zeros((1, 1), jnp.int32)
    params = jnp.concatenate(
        [
            v.reshape(1, width)
            for v in (out_bias, first_gain, first_shift, outer_bias, second_gain, second_shift, out_bias, out_bias)
        ]
    )
    limit = 56
    LOW = 24 if rows <= 512 else 56
    weights = pltpu.VMEM((nt, width, hidden), BF)
    acted = pltpu.VMEM((nt, rows, hidden), BF)
    dma = pltpu.SemaphoreType.DMA
    any_w = [anywhere()] * nw
    shards = (
        call(
            interleave_kernel,
            [query_weight, key_weight, value_weight, out_weight],
            [anywhere()] * 4,
            [shape((query_weight.shape[0], 4 * local), BF)],
            [vmem()],
            [*[pltpu.VMEM(query_weight.shape, BF)] * 3, pltpu.VMEM(out_weight.shape, BF), dma((4,))],
            limit,
            1,
        )[0],
        inner_weight,
        outer_weight.T,
    )

    def attend(x, bias, attn_w):
        return call(
            functools.partial(attend_kernel, nw),
            [x, seg_row, bias, params, where, *attn_w],
            [vmem()] * 4 + [smem()] + any_w,
            [
                shape((nt, rows, 640), BF),
                shape((nt, nseq, 3, LEN, LEN), BF),
                shape((nt, rows, 256), BF),
                shape((rows, width), F32),
                shape((rows, 128), F32),
                shape((rows, width), BF),
            ],
            [anywhere()] * 3 + [vmem()] * 3,
            [
                weights,
                pltpu.VMEM((nseq, LEN, LEN), F32),
                pltpu.VMEM((nt, rows, 640), BF),
                pltpu.VMEM((nt, nseq, 3, LEN, LEN), BF),
                pltpu.VMEM((nt, rows, 256), BF),
                dma((nt,)),
                dma((3,)),
            ],
            limit,
            13,
        )

    def inner(low, inner_b, inner_w):
        return call(
            functools.partial(inner_kernel, nw),
            [low, inner_b, where_split, *inner_w],
            [vmem()] * 2 + [smem()] + any_w,
            [shape((nt, rows, hidden), BF)] * 2,
            [anywhere()] * 2,
            [weights, pltpu.VMEM((rows, hidden), F32), acted, acted, dma((nt,)), dma((2,))],
            limit,
            13,
        )

    if plan.pieces:
        slot = (plan.nz, width // ndp, hidden)
        grads = [shape((4, *slot), BF)] + [shape(slot, BF)] * 4
    else:
        grads = [shape((nt, width, hidden), BF)]
    ng = len(grads)
    wide, thin = pltpu.VMEM((rows, width), F32), pltpu.VMEM((rows, width), BF)

    def outer(active, normed, outer_w):
        return call(
            functools.partial(outer_kernel, nw, ng),
            [active, normed, cot, params, where, where_split, *outer_w],
            [anywhere()] * 3 + [vmem()] + [smem()] * 2 + any_w,
            [
                *grads,
                shape((rows, width), BF),
                shape((rows, width), F32),
                shape((rows, width), BF),
                shape((8, width), F32),
            ],
            [anywhere()] * (ng + 3) + [vmem()],
            [
                weights, acted, wide, thin, wide, thin, thin, pltpu.VMEM((width, rows), BF), weights,
                dma((nt,)), dma((nt,)), dma((2,)), dma((5,)),
            ],
            limit,
            14,
        )

    def middle(slope, second, ffn, low, normed, scale, outer_w, inner_w, attn_w):
        return call(
            functools.partial(middle_kernel, nw, ng),
            [slope, second, ffn, low, normed, scale, params, where, where_split, *outer_w, *inner_w, *attn_w],
            [anywhere()] * 6 + [vmem()] + [smem()] * 2 + any_w * 3,
            [
                *grads,
                shape((rows, width), F32),
                shape((rows, width), BF),
                shape((nt, rows, 256), BF),
                shape((8, width), F32),
                shape((nt, 1, hidden), F32),
            ],
            [anywhere()] * (ng + 3) + [vmem()] * 2,
            [
                weights, weights, pltpu.VMEM((nt, width, 256), BF), acted, wide,
                pltpu.VMEM((rows, 128), F32), thin, wide, wide, thin,
                pltpu.VMEM((width, rows), BF), acted, pltpu.VMEM((nt, rows, 256), BF), weights,
                dma((3, nt)), dma((nt,)), dma((5,)), dma((5,)),
            ],
            limit,
            0.1,
        )

    def attend_back(attn_low, acts, probs, ctx, ctx_grad, attn_in, vecs, attn_w):
        return call(
            functools.partial(attend_back_kernel, nw, ng),
            [x, attn_low, acts, probs, ctx, ctx_grad, attn_in, *vecs, where, where_split, *attn_w],
            [vmem()] * 2 + [anywhere()] * 5 + [vmem()] * 3 + [smem()] * 2 + any_w,
            [*grads, *[shape((rows // 2, width), BF)] * 2, shape((16, hidden), F32), shape((32, hidden), BF)],
            [anywhere()] * ng + [vmem()] * 4,
            [
                weights,
                pltpu.VMEM((rows, width), F32),
                pltpu.VMEM((nt, rows, 640), BF),
                pltpu.VMEM((nt, nseq, 3, LEN, LEN), BF),
                pltpu.VMEM((nt, rows, 256), BF),
                pltpu.VMEM((nt, rows, 256), BF),
                pltpu.VMEM((nt, rows, 640), BF),
                pltpu.VMEM((width, rows), BF),
                pltpu.VMEM((width, rows), BF),
                weights,
                pltpu.VMEM((nt, 1, 640), F32),
                dma((nt,)),
                dma((nt + 1,)),
                dma((2,)),
            ],
            limit,
            0.1,
        )

    def place(parts):
        order = jnp.stack([me, me ^ 2, me ^ 1, me ^ 3]).astype(jnp.int32)
        return call(
            place_kernel,
            [order, *parts],
            [smem()] + [anywhere()] * 4,
            [shape((nt * rows, width), BF)],
            [anywhere()],
            [pltpu.VMEM((4, rows, width), BF), dma((4,)), dma((4,))],
            limit,
            0.1,
        )[0]

    def widen(parts, flip, half=None):
        order = jnp.stack([me ^ flip, me ^ flip ^ 1]).astype(jnp.int32)
        more = [] if half is None else [half]
        return call(
            widen_kernel,
            [order, *parts, *more],
            [smem()] + [anywhere()] * (4 + len(more)),
            [shape((nt * rows, width), F32)],
            [anywhere()],
            [pltpu.VMEM((4, rows // 2, width), BF), pltpu.VMEM((4, rows // 2, width), F32), dma((4,)), dma((4,))],
            limit,
            0.1,
            {5: 0} if more else {},
        )[0]

    def small_parts():
        every = lax.all_gather(jnp.concatenate([query_bias, value_bias, inner_bias]), "tensor", axis=0)
        q_b, v_b = every[:, None, :local], every[:, None, local : 2 * local]
        none = jnp.zeros_like(q_b)
        return interleave(q_b, none, v_b, none), every[:, None, 2 * local :]

    bias, inner_b = small_parts()
    if plan.pieces:
        turn, one_way, other_way, core = plan.turn, plan.first(), plan.second(), plan.core()

        beside = plan.beside()

        def spread(own):
            return [turn(own, one_way), turn(own, other_way)]

        def cores(parts):
            return [turn(v, core) for v in parts]

        near = plan.near(shards[0])
        near, bias, inner_b, x, cot, seg_row, where, where_split, params = tie(
            (near, bias, inner_b, x, cot, seg_row, where, where_split, params)
        )
        own1 = jnp.stack([shards[0], *near])
        two1 = spread(own1)
        a2 = turn(tie(shards[1], own1), plan.step(False))
        own1_c = turn(own1, core)
        two1, a2, own1_c = tie((two1, a2, own1_c))
        both1 = turn(two1[0], other_way)
        cores1 = cores(two1)
        pair2 = jnp.stack([shards[1], a2])
        b2 = turn(pair2, plan.step(True))
        both1, cores1, b2 = tie((both1, cores1, b2))
        own2 = jnp.concatenate([pair2, b2])
        two2 = spread(own2)
        a3 = turn(tie(shards[2], own2), plan.step(False))
        own2_c = turn(own2, core)
        attn_w = [own1, *two1, both1, own1_c, *cores1, turn(both1, core)]
        acts, probs, ctx, normed, scale, low = attend(x, bias, attn_w)
        two2, a3, own2_c, low = tie((two2, a3, own2_c, low))
        both2 = turn(two2[0], other_way)
        cores2 = cores(two2)
        pair3 = jnp.stack([shards[2], a3])
        b3 = turn(pair3, plan.step(True))
        both2, cores2, b3 = tie((both2, cores2, b3))
        own3 = jnp.concatenate([pair3, b3])
        two3 = spread(own3)
        own3_c = turn(own3, core)
        inner_w = [own2, *two2, both2, own2_c, *cores2, turn(both2, core)]
        active, slope = inner(low, inner_b, inner_w)
        two3, own3_c, active = tie((two3, own3_c, active))
        both3 = turn(two3[0], other_way)
        cores3 = cores(two3)
        both3, cores3 = tie((both3, cores3))
        outer_w = [own3, *two3, both3, own3_c, *cores3, turn(both3, core)]
        keep3, *send3, layer_part, second, ffn, second_vec = outer(active, normed, outer_w)

        got3 = cores(send3)
        layer_x = turn(layer_part, beside)
        keep2, *send2, attn_in, attn_low, ctx_grad, first_vec, inner_vec = middle(
            slope, second, tie((ffn, send3))[0], low, normed, scale, outer_w, inner_w, attn_w
        )
        got3, layer_x, send2, ctx_grad = tie((got3, layer_x, send2, ctx_grad))
        away3 = plan.scatter_a(keep3, got3)
        got3a = turn(away3, one_way)
        got2 = cores(send2)
        layer_c = cores([layer_part, layer_x])
        got2, layer_c, ctx_grad = tie((got2, layer_c, ctx_grad))
        away2 = plan.scatter_a(keep2, got2)
        got2a = turn(away2, one_way)
        keep1, *send1, input_a, input_b, vectors, packs = attend_back(
            attn_low, acts, probs, ctx, tie((ctx_grad, away2))[0], attn_in, (second_vec, first_vec, inner_vec), attn_w
        )
        got1 = cores(send1)
        packed = 2 * vectors.shape[0]
        input_low = [input_a, input_b]
        got3a, got2a, got1, input_low, packs = tie((got3a, got2a, got1, input_low, packs))
        flat = (-1, hidden)
        away1 = plan.scatter_a(keep1, got1)
        away1 = jnp.concatenate([away1.reshape(flat), packs])
        got1a = turn(away1, one_way)
        left3 = tie((keep3, away1))[0][:2].astype(F32) + jnp.stack(got3[:2]).astype(F32) + got3a.astype(F32)
        half3 = turn(left3[:, 2:].astype(BF), plan.step(True))
        left = tie((keep2, left3))[0]
        away2 = plan.scatter_b(left, got2, got2a)
        got2b = turn(away2, other_way)
        input_c = cores(input_low)
        layer_out = place(tie(([layer_part, layer_x, *layer_c], away2))[0])
        half_grad = widen(tie(([*input_low, *input_c], layer_out))[0], 0)
        half3, got2b, half_grad, got1a = tie((half3, got2b, half_grad, got1a))
        vectors = vectors + unpack(got1a[-packed:])
        got1a = got1a[:-packed].reshape(2, *slot)
        away = plan.scatter_b(keep1, got1, got1a)
        away = jnp.concatenate([away.reshape(flat), pack(vectors)])
        got1b = turn(away, other_way)
        input_x = turn(input_low[0], beside)
        half3, got2b, away = tie((half3, got2b, away))
        left3 = left3[:, :2] + half3.astype(F32)
        quarter3 = turn(left3[:, 1].astype(BF), plan.step(False))
        left2 = plan.scatter_left(keep2, got2, got2a, got2b)
        half2 = plan.half_z(left2)
        quarter3, half2, got1b, input_x = tie((quarter3, half2, got1b, input_x))
        left3 = left3[:, 0] + quarter3.astype(F32)
        last3 = turn(left3[1].astype(BF), other_way)
        left2 = left2[:2] + half2.astype(F32)
        quarter2 = plan.last_z(left2[1])
        vectors = vectors + unpack(got1b[-packed:])
        got1b = got1b[:-packed].reshape(slot)
        left1 = plan.scatter_left(keep1, got1, got1a, got1b)
        away = jnp.concatenate([left1[2:].astype(BF).reshape(flat), pack(vectors)])
        half1 = turn(away, plan.step(True))
        input_y = turn(tie((input_low[1], away))[0], beside)
        last3, quarter2, away = tie((last3, quarter2, away))
        outer_grad = left3[0] + last3.astype(F32)
        inner_grad = left2[0] + quarter2.astype(F32)
        half1, outer_grad, inner_grad = tie((half1, outer_grad, inner_grad))
        vectors = vectors + unpack(half1[-packed:])
        half1 = half1[:-packed].reshape(2, -1, hidden)
        away = (left1[1] + half1[1].astype(F32)).astype(BF)
        away = jnp.concatenate([away, pack(vectors)])
        quarter1 = turn(away, plan.step(False))
        input_x = [input_x, input_y]
        input_x[1] = tie((input_x[1], half1))[0]
        input_xc = cores(input_x)
        vectors = vectors + unpack(quarter1[-packed:])
        vectors = vectors + turn(vectors, core)
        attn_grads = call(
            part_kernel,
            [left1[0] + half1[0].astype(F32), quarter1],
            [vmem()] * 2,
            [shape((width // ndp, local), F32)] * 3 + [shape((local, width // ndp), F32)],
            [vmem()] * 4,
            [],
            16,
            1,
        )
        input_grad = widen([*input_x, *input_xc], 2, half_grad)
    else:
        attn_w, inner_w, outer_w = (
            [lax.all_gather(lax.all_gather(s, "dp", axis=0, tiled=True), "tensor", axis=0)]
            for s in shards
        )
        acts, probs, ctx, normed, scale, low = attend(x, bias, attn_w)
        active, slope = inner(low, inner_b, inner_w)
        outer_g, layer_part, second, ffn, second_vec = outer(active, normed, outer_w)
        inner_g, attn_in, attn_low, ctx_grad, first_vec, inner_vec = middle(
            slope, second, ffn, low, normed, scale, outer_w, inner_w, attn_w
        )
        attn_g, input_a, input_b, vectors, _ = attend_back(
            attn_low, acts, probs, ctx, ctx_grad, attn_in, (second_vec, first_vec, inner_vec), attn_w
        )
        outer_grad, inner_grad, attn_g = (
            lax.psum_scatter(
                lax.psum_scatter(g, "tensor", scatter_dimension=0, tiled=False),
                "dp",
                scatter_dimension=0,
                tiled=True,
            ).astype(F32)
            for g in (outer_g, inner_g, attn_g)
        )
        layer_out = lax.all_gather(layer_part, "tensor", axis=0, tiled=True)
        input_low = jnp.concatenate([input_a, input_b])
        input_grad = lax.all_gather(input_low, "tensor", axis=0, tiled=True).astype(F32)

    if not plan.pieces:
        vectors = lax.psum(vectors, AXES)
    gain2, shift2, bias2, gain1, shift1, bias1 = (vectors[n] for n in range(6))
    inner_bias_grad = lax.dynamic_index_in_dim(vectors, 6 + me, 0, keepdims=False)
    mine_vec = lax.dynamic_index_in_dim(vectors, 6 + nt + me, 0, keepdims=False)
    query_bias_grad, value_bias_grad = mine_vec[:local], mine_vec[local : 2 * local]
    h = HEAD_DIM
    if not plan.pieces:
        part = lambda *spans: jnp.concatenate([attn_g[:, a * h : b * h] for a, b in spans], axis=1)
        attn_grads = part((0, 2), (6, 7)), part((2, 4), (8, 9)), part((4, 6), (7, 8)), part((10, 12), (9, 10)).T
    return (
        layer_out,
        input_grad,
        *attn_grads[:3],
        query_bias_grad,
        value_bias_grad,
        attn_grads[3],
        bias1,
        gain1,
        shift1,
        inner_grad,
        inner_bias_grad,
        outer_grad.T,
        bias2,
        gain2,
        shift2,
    )


def solution(mesh):
    in_specs = (
        P("dp", None),
        P("dp", None),
        P("dp", "tensor"),
        P("dp", "tensor"),
        P("dp", "tensor"),
        P("tensor"),
        P("tensor"),
        P("tensor", "dp"),
        P(),
        P(),
        P(),
        P("dp", "tensor"),
        P("tensor"),
        P("tensor", "dp"),
        P(),
        P(),
        P(),
        P("dp", None),
    )
    out_specs = (
        P("dp", None),
        P("dp", None),
        P("dp", "tensor"),
        P("dp", "tensor"),
        P("dp", "tensor"),
        P("tensor"),
        P("tensor"),
        P("tensor", "dp"),
        P(),
        P(),
        P(),
        P("dp", "tensor"),
        P("tensor"),
        P("tensor", "dp"),
        P(),
        P(),
        P(),
    )
    return jax.shard_map(
        functools.partial(body, Plan(mesh)),
        mesh=mesh,
        in_specs=in_specs,
        out_specs=out_specs,
        check_vma=False,
    )
```

```python
import functools
import math

import jax
import jax.numpy as jnp
from jax import lax
from jax.experimental import pallas as pl
from jax.experimental.pallas import tpu as pltpu
from jax.sharding import PartitionSpec as P

HEAD_DIM = 64
LEN = 256
EPS = 1e-06
BF = jnp.bfloat16
F32 = jnp.float32
AXES = ("dp", "tensor")
MIB = 1 << 20
SCALE = 0.3


def dot(left, right):
    return lax.dot_general(left, right, (((1,), (0,)), ((), ())), preferred_element_type=F32)


def dot_t(left, right):
    return lax.dot_general(left, right, (((1,), (1,)), ((), ())), preferred_element_type=F32)


def t_dot(left, right):
    return lax.dot_general(left, right, (((0,), (0,)), ((), ())), preferred_element_type=F32)


def vmem():
    return pl.BlockSpec(memory_space=pltpu.VMEM)


def smem():
    return pl.BlockSpec(memory_space=pltpu.SMEM)


def anywhere():
    return pl.BlockSpec(memory_space=pl.ANY)


def call(body, ins, in_specs, outs, out_specs, scratch, limit, cost, aliases={}):
    return pl.pallas_call(
        body,
        out_shape=outs,
        in_specs=in_specs,
        out_specs=out_specs,
        scratch_shapes=scratch,
        input_output_aliases=aliases,
        compiler_params=pltpu.CompilerParams(vmem_limit_bytes=limit * MIB),
        cost_estimate=pl.CostEstimate(flops=int(cost * SCALE * 1e9), bytes_accessed=1000, transcendentals=0),
    )(*ins)


def shape(dims, dtype):
    return jax.ShapeDtypeStruct(dims, dtype)


class Plan:
    def __init__(self, mesh):
        self.ndp, self.nt = mesh.shape["dp"], mesh.shape["tensor"]
        self.pieces = self.nt == 4 and self.ndp == 8
        self.nz = self.ndp // 2

    def pairs(self, move):
        found = []
        for d in range(self.ndp):
            for t in range(self.nt):
                z, y, x, c = move(d >> 1, d & 1, t >> 1, t & 1)
                found.append((d * self.nt + t, (z * 2 + y) * self.nt + x * 2 + c))
        return found

    def first(self):
        return self.pairs(lambda z, y, x, c: (z, y, x ^ 1, c) if c == 0 else (z, y ^ 1, x, c))

    def second(self):
        return self.pairs(lambda z, y, x, c: (z, y, x ^ 1, c) if c == 1 else (z, y ^ 1, x, c))

    def core(self):
        return self.pairs(lambda z, y, x, c: (z, y, x, c ^ 1))

    def along(self, j):
        return self.pairs(lambda z, y, x, c: (z ^ j, y, x, c))

    def step(self, last):
        return self.pairs(lambda z, y, x, c: (z ^ (1 if (c == 0) != last else 2), y, x, c))

    def tables(self, split):
        d, t = lax.axis_index("dp"), lax.axis_index("tensor")
        z, y, x, c = d >> 1, d & 1, t >> 1, t & 1
        s = jnp.arange(2)[:, None, None]
        r = jnp.arange(4)[None, :, None]
        j = jnp.arange(self.nz)[None, None, :]
        a, b = r & 1, r >> 1
        core = c ^ s
        dx, dy = jnp.where(core == 0, a, b), jnp.where(core == 0, b, a)
        if split:
            j = jnp.where(core == 0, j, (j & 1) * 2 + (j >> 1))
        where_t = jnp.broadcast_to((x ^ dx) * 2 + core, (2, 4, self.nz))
        where_d = jnp.broadcast_to((z ^ j) * 2 + (y ^ dy), (2, 4, self.nz))
        return jnp.stack([where_t.reshape(-1), where_d.reshape(-1)]).astype(jnp.int32)

    def turn(self, values, pairs):
        return lax.ppermute(values, AXES, pairs)

    def near(self, shard):
        return [self.turn(shard, self.along(j)) for j in range(1, self.nz)]

    def beside(self):
        return self.pairs(lambda z, y, x, c: (z, y, x ^ 1, c))

    def scatter_a(self, keep, got):
        return (keep[2:].astype(F32) + jnp.stack(got[2:]).astype(F32)).astype(BF)

    def scatter_b(self, keep, got, got_a):
        return (keep[1].astype(F32) + got[1].astype(F32) + got_a[1].astype(F32)).astype(BF)

    def scatter_left(self, keep, got, got_a, got_b):
        return keep[0].astype(F32) + got[0].astype(F32) + got_a[0].astype(F32) + got_b.astype(F32)

    def half_z(self, left):
        return self.turn(left[2:].astype(BF), self.step(True))

    def last_z(self, values):
        return self.turn(values.astype(BF), self.step(False))


def load_weights(refs, where, full, sem, start=0, before=0):
    columns = pl.ds(start, full.shape[2])
    if not refs:
        return
    if len(refs) == 1:
        for t in range(full.shape[0]):
            pltpu.make_async_copy(refs[0].at[t, :, columns], full.at[t], sem.at[t]).start()
        return
    nz, rows, _ = refs[0].shape
    for r, ref in enumerate(refs):
        for j in range(nz):
            n = (before + r) * nz + j
            t, d = where[0, n], where[1, n]
            spot = pl.ds(pl.multiple_of(d * rows, rows), rows)
            pltpu.make_async_copy(ref.at[j, :, columns], full.at[t, spot], sem.at[t]).start()


def load(ref, held, sem):
    pltpu.make_async_copy(ref, held, sem).start()


def wait(held, sem):
    pltpu.make_async_copy(held, held, sem).wait()


def blocks(rows, block):
    def over(run):
        @pl.loop(0, rows // block)
        def _(i):
            run(pl.ds(pl.multiple_of(i * block, block), block))

    return over


def pack(vectors):
    high = vectors.astype(BF)
    return jnp.concatenate([high, (vectors - high.astype(F32)).astype(BF)])


def unpack(rows):
    half = rows.shape[0] // 2
    return rows[:half].astype(F32) + rows[half:].astype(F32)


def tie(values, *after):
    if after:
        return lax.optimization_barrier((values, *after))[0]
    return lax.optimization_barrier(values)


def lane_masks(rows):
    lane = lax.broadcasted_iota(jnp.int32, (rows, 128), 1)
    return lane < HEAD_DIM


def pick(mask, values):
    return jnp.where(mask, values, jnp.zeros_like(values))


def norm_stats(hidden):
    center = hidden - jnp.mean(hidden, axis=-1, keepdims=True)
    scale = lax.rsqrt(jnp.mean(center * center, axis=-1, keepdims=True) + EPS)
    return center * scale, scale


def norm_pull(incoming, normed, scale, gain):
    scaled = incoming * gain
    return scale * (
        scaled
        - jnp.mean(scaled, axis=-1, keepdims=True)
        - normed * jnp.mean(scaled * normed, axis=-1, keepdims=True)
    )


def attend_kernel(nw, x_ref, seg_row, bias, params, where, *rest):
    refs, rest = rest[:nw], rest[nw:]
    acts_out, probs_out, ctx_out, normed_ref, scale_ref, low_ref = rest[:6]
    full, keep, acts, probs, ctx, sem, sem_out = rest[6:]
    rows = x_ref.shape[0]
    nt = acts.shape[0]
    load_weights(refs, where, full, sem)
    nseq = rows // LEN
    for s in range(nseq):
        own = seg_row[s : s + 1, :].astype(F32)
        same = jnp.broadcast_to(own, (8, LEN)).T[:, 0:1] == own
        keep[s] = jnp.where(same, 0.0, -1e30).astype(F32)
    low_half = lane_masks(LEN)
    ones = jnp.ones((LEN, 128), BF)

    normed_ref[...] = x_ref[...].astype(F32) + params[0:1, :]

    @pl.loop(0, nt)
    def _(t):
        wait(full.at[t], sem.at[t])
        x = x_ref[...]
        acts[t, :, 0:512] = (dot(x, full[t, :, 0:512]) + bias[t, :, 0:512]).astype(BF)
        last = dot(x, full[t, :, 512:640]).astype(BF)
        acts[t, :, 512:640] = pick(lane_masks(rows), last)

        for s in range(nseq):
            span = slice(s * LEN, (s + 1) * LEN)
            q01, k01, v01 = acts[t, span, 0:128], acts[t, span, 128:256], acts[t, span, 256:384]
            qv2, k2 = acts[t, span, 384:512], acts[t, span, 512:640]
            heads = (
                (pick(low_half, q01), k01, v01),
                (pick(~low_half, q01), k01, v01),
                (pick(low_half, qv2), k2, qv2),
            )
            done = []
            for h, (query, key, value) in enumerate(heads):
                scores = dot_t(query, key) * HEAD_DIM ** (-0.5) + keep[s]
                top = jnp.max(scores, axis=-1, keepdims=True)
                expo = jnp.exp(scores - top)
                low = expo.astype(BF)
                mixed = dot(low, jnp.concatenate([value, ones], axis=1))
                inverse = 1.0 / mixed[:, 128:]
                probs[t, s, h] = (expo * jnp.concatenate([inverse, inverse], axis=1)).astype(BF)
                done.append(mixed[:, :128] * inverse)
            ctx[t, span, 0:128] = pick(~low_half, done[2]).astype(BF)
            ctx[t, span, 128:256] = jnp.where(low_half, done[0], done[1]).astype(BF)
        pltpu.make_async_copy(acts.at[t], acts_out.at[t], sem_out.at[0]).start()
        pltpu.make_async_copy(probs.at[t], probs_out.at[t], sem_out.at[1]).start()
        pltpu.make_async_copy(ctx.at[t], ctx_out.at[t], sem_out.at[2]).start()
        part = dot_t(ctx[t], full[t, :, 512:768]).astype(BF)
        normed_ref[...] += part.astype(F32)

    @blocks(rows, 128)
    def _(span):
        normed, scale = norm_stats(normed_ref[span, :])
        normed_ref[span, :] = normed
        scale_ref[span, :] = jnp.broadcast_to(scale, (128, 128))
        low_ref[span, :] = (normed * params[1:2, :] + params[2:3, :]).astype(BF)

    wait(acts, sem_out.at[0])
    wait(probs, sem_out.at[1])
    wait(ctx, sem_out.at[2])


TAIL_STEP = 0.43 / math.sqrt(2.0)
TAIL = (
    0.12125730288161489,
    0.12218773837809233,
    0.1024754485844625,
    0.12342253549698744,
    -0.04286343715820851,
    0.19185342214732998,
    -0.15518700012679373,
    0.036854031729008835,
)


def normal_parts(values):
    t = 1.0 / (1.0 + TAIL_STEP * jnp.abs(values))
    bell = jnp.exp2(values * values * (-0.5 * math.log2(math.e)))
    poly = TAIL[-1]
    for c in TAIL[-2::-1]:
        poly = c + t * poly
    tail = t * poly * bell
    return jnp.where(values >= 0, 1.0 - tail, tail), bell


def inner_kernel(nw, low_ref, bias, where, *rest):
    refs, rest = rest[:nw], rest[nw:]
    active_out, slope_out, full, inner_ref, active, slope, sem, sem_out = rest
    rows = low_ref.shape[0]
    nt = active.shape[0]
    load_weights(refs, where, full, sem)

    @pl.loop(0, nt)
    def _(t):
        wait(full.at[t], sem.at[t])
        inner_ref[...] = dot(low_ref[...], full[t]) + bias[t]

        @blocks(rows, 64)
        def _(span):
            inner = inner_ref[span, :]
            phi, bell = normal_parts(inner)
            active[t, span, :] = (inner * phi).astype(BF)
            slope[t, span, :] = (phi + inner * bell * (1.0 / math.sqrt(2.0 * math.pi))).astype(BF)

        pltpu.make_async_copy(active.at[t], active_out.at[t], sem_out.at[0]).start()
        pltpu.make_async_copy(slope.at[t], slope_out.at[t], sem_out.at[1]).start()

    wait(active, sem_out.at[0])
    wait(slope, sem_out.at[1])


def turn_of(where, n):
    return 2 * (n % 2) + ((where[0, 0] % 2) ^ (1 - n // 2))


def store_grads(where, side, held, outs, sem):
    nz, rows = outs[0].shape[0], outs[0].shape[1]
    for r in range(4):
        for j in range(nz):
            n = (side * 4 + r) * nz + j
            t, d = where[0, n], where[1, n]
            spot = pl.ds(pl.multiple_of(d * rows, rows), rows)
            pltpu.make_async_copy(
                held.at[t // 2, spot], outs[(r & 1) * 2 + (r >> 1)].at[j], sem
            ).start()


def each_grad(where, outs, make):
    def over(held, sems):
        nt = held.shape[0]
        if len(outs) == 1:
            for n in range(nt):
                held[n] = make(n)
                load(held.at[n], outs[0].at[n], sems.at[0])
            return lambda: wait(held, sems.at[0])
        keep, send = outs[0], outs[1:]
        for n in range(nt):
            held[n] = make(turn_of(where, n))
            if n == 1:
                store_grads(where, 1, held.at[0:2], send, sems.at[0])
            if n == 3:
                store_grads(where, 0, held.at[2:4], [keep.at[r] for r in range(4)], sems.at[1])
        return lambda: [wait(held.at[2 * n : 2 * n + 2], sems.at[n]) for n in range(2)]

    return over


def outer_kernel(nw, ng, active_in, normed_in, cot_in, rows_in, where, where_split, *rest):
    refs, outs, rest = rest[:nw], rest[nw : nw + ng], rest[nw + ng :]
    out_part, second_out, ffn_out, vec_ref, full, active, normed_ref, cot, second, out_v, ffn = rest[:11]
    turned, held, sem, sem_a, sem_b, sem_out = rest[11:]
    rows = cot.shape[0]
    nt = active.shape[0]
    load_weights(refs[: nw // 2], where_split, full, sem)
    turns = [turn_of(where, n) for n in (2, 3, 0, 1)]
    for t in turns[:2]:
        load(active_in.at[t], active.at[t], sem_a.at[t])
    load_weights(refs[nw // 2 :], where_split, full, sem, 0, nw // 2)
    for t in turns[2:]:
        load(active_in.at[t], active.at[t], sem_a.at[t])
    load(normed_in, normed_ref, sem_b.at[0])
    load(cot_in, cot, sem_b.at[1])
    gain1, shift1, outer_bias, gain, shift = (rows_in[n : n + 1, :] for n in range(1, 6))
    vec_ref[...] = jnp.zeros_like(vec_ref)
    for n, t in enumerate(turns):
        wait(active.at[t], sem_a.at[t])
        wait(full.at[t], sem.at[t])
        part = dot_t(active[t], full[t]).astype(BF).astype(F32)
        second[...] = part if n == 0 else second[...] + part
    wait(normed_ref, sem_b.at[0])
    wait(cot, sem_b.at[1])

    @blocks(rows, 128)
    def _(span):
        first = normed_ref[span, :] * gain1 + shift1
        normed, scale = norm_stats(second[span, :] + outer_bias + first)
        out_v[span, :] = (normed * gain + shift).astype(BF)
        incoming = cot[span, :].astype(F32)
        pull = norm_pull(incoming, normed, scale, gain)
        second[span, :] = pull
        ffn[span, :] = pull.astype(BF)
        vec_ref[0:1, :] += jnp.sum(incoming * normed, axis=0, keepdims=True)
        vec_ref[1:2, :] += jnp.sum(incoming, axis=0, keepdims=True)
        vec_ref[2:3, :] += jnp.sum(pull, axis=0, keepdims=True)

    load(out_v, out_part, sem_out.at[2])
    load(second, second_out, sem_out.at[3])
    load(ffn, ffn_out, sem_out.at[4])
    turned[...] = ffn[...].T
    each_grad(where_split, outs, lambda t: dot(turned[...], active[t]).astype(BF))(held, sem_out)()
    wait(out_v, sem_out.at[2])
    wait(second, sem_out.at[3])
    wait(ffn, sem_out.at[4])


def middle_kernel(nw, ng, slope_in, second_in, ffn_in, low_in, normed_in, scale_in, rows_in, where, where_split, *rest):
    refs, inner_refs, attn_refs, rest = rest[:nw], rest[nw : 2 * nw], rest[2 * nw : 3 * nw], rest[3 * nw :]
    outs, rest = rest[:ng], rest[ng:]
    attn_in_out, attn_low_out, ctx_grad_out, vec_ref, inner_vec = rest[:5]
    full, inner_full, attn_full, slope, normed_ref, scale_ref, low, second, attn_in, ffn = rest[5:15]
    turned, pulled, ctx_grad, held, sem, sem_a, sem_b, sem_out = rest[15:]
    rows = low.shape[0]
    nt = slope.shape[0]
    load(ffn_in, ffn, sem_b.at[0])
    load_weights(refs, where_split, full, sem.at[0])
    for t in [turn_of(where, n) for n in (2, 3, 0, 1)]:
        load(slope_in.at[t], slope.at[t], sem_a.at[t])
    load(low_in, low, sem_b.at[1])
    load_weights(inner_refs, where_split, inner_full, sem.at[1])
    load(second_in, second, sem_b.at[2])
    load(normed_in, normed_ref, sem_b.at[3])
    load(scale_in, scale_ref, sem_b.at[4])
    load_weights(attn_refs, where, attn_full, sem.at[2], 512)
    gain1 = rows_in[1:2, :]
    vec_ref[...] = jnp.zeros_like(vec_ref)
    wait(ffn, sem_b.at[0])
    for t in [turn_of(where, n) for n in (2, 3, 0, 1)]:
        wait(full.at[t], sem.at[0, t])
        wait(slope.at[t], sem_a.at[t])
        grad = (dot(ffn[...], full[t]) * slope[t].astype(F32)).astype(BF)
        pulled[t] = grad
        inner_vec[t] = jnp.sum(grad.astype(F32), axis=0, keepdims=True)
    wait(low, sem_b.at[1])
    turned[...] = low[...].T
    done = each_grad(where_split, outs, lambda t: dot(turned[...], pulled[t]).astype(BF))(held, sem_out)
    for t in range(nt):
        wait(inner_full.at[t], sem.at[1, t])
        part = dot_t(pulled[t], inner_full[t])
        attn_in[...] = part if t == 0 else attn_in[...] + part
    wait(second, sem_b.at[2])
    wait(normed_ref, sem_b.at[3])
    wait(scale_ref, sem_b.at[4])

    @blocks(rows, 128)
    def _(span):
        incoming = attn_in[span, :] + second[span, :]
        normed = normed_ref[span, :]
        grad = norm_pull(incoming, normed, scale_ref[span, 0:1], gain1)
        attn_in[span, :] = grad
        ffn[span, :] = grad.astype(BF)
        vec_ref[0:1, :] += jnp.sum(incoming * normed, axis=0, keepdims=True)
        vec_ref[1:2, :] += jnp.sum(incoming, axis=0, keepdims=True)
        vec_ref[2:3, :] += jnp.sum(grad, axis=0, keepdims=True)

    load(attn_in, attn_in_out, sem_out.at[2])
    load(ffn, attn_low_out, sem_out.at[3])
    low_half = lane_masks(rows)
    for t in range(nt):
        wait(attn_full.at[t], sem.at[2, t])
        got = dot(ffn[...], attn_full[t])
        ctx_grad[t, :, 0:128] = pick(~low_half, got[:, :128]).astype(BF)
        ctx_grad[t, :, 128:256] = got[:, 128:].astype(BF)
        load(ctx_grad.at[t], ctx_grad_out.at[t], sem_out.at[4])
    done()
    wait(attn_in, sem_out.at[2])
    wait(ffn, sem_out.at[3])
    wait(ctx_grad, sem_out.at[4])


def attend_pull(acts, probs, ctx_grad, back, t):
    rows = acts.shape[1]
    low_half = lane_masks(LEN)
    factor = HEAD_DIM ** (-0.5)
    h = HEAD_DIM
    for s in range(rows // LEN):
        span = slice(s * LEN, (s + 1) * LEN)
        q01, k01, v01 = acts[t, span, 0:128], acts[t, span, 128:256], acts[t, span, 256:384]
        qv2, k2 = acts[t, span, 384:512], acts[t, span, 512:640]
        g2, g01 = ctx_grad[t, span, 0:128], ctx_grad[t, span, 128:256]
        heads = (
            (pick(low_half, g01), k01, v01),
            (pick(~low_half, g01), k01, v01),
            (g2, k2, qv2),
        )
        queries, scores = [], []
        for n, (grad, key, value) in enumerate(heads):
            wide = probs[t, s, n].astype(F32)
            pulled = dot_t(grad, value)
            delta = jnp.sum(pulled * wide, axis=-1, keepdims=True)
            scores.append((wide * (pulled - delta)).astype(BF))
            queries.append(dot(scores[n], key) * factor)
        q01t, g01t, qv2t, g2t = q01.T, g01.T, qv2.T, g2.T
        keys01 = jnp.concatenate([dot(q01t[:h], scores[0]), dot(q01t[h:], scores[1])], axis=0) * factor
        values01 = jnp.concatenate([dot(g01t[:h], probs[t, s, 0]), dot(g01t[h:], probs[t, s, 1])], axis=0)
        both2 = jnp.concatenate([dot(qv2t[:h], scores[2]) * factor, dot(g2t[h:], probs[t, s, 2])], axis=0)
        kv2 = both2.astype(BF).T
        back[t, span, 0:128] = jnp.where(low_half, queries[0], queries[1]).astype(BF)
        back[t, span, 128:256] = keys01.astype(BF).T
        back[t, span, 256:384] = values01.astype(BF).T
        back[t, span, 384:512] = jnp.where(low_half, queries[2].astype(BF), kv2)
        back[t, span, 512:640] = pick(low_half, kv2)


def attend_back_kernel(nw, ng, x_ref, attn_low, acts_in, probs_in, ctx_in, ctx_grad_in, attn_in, *rest):
    second_vec, first_vec, inner_vec, where, where_split, *rest = rest
    refs, outs, (input_a, input_b, vectors, packs) = rest[:nw], rest[nw : nw + ng], rest[nw + ng : nw + ng + 4]
    full, total, acts, probs, ctx, ctx_grad, back, turned_x, turned_a, held, vec_ref = rest[nw + ng + 4 : -3]
    sem, sem_in, sem_out = rest[-3:]
    nt = acts.shape[0]
    for n in range(nt):
        t = turn_of(where, n) if ng > 1 else n
        load(acts_in.at[t], acts.at[t], sem_in.at[t])
        load(ctx_grad_in.at[t], ctx_grad.at[t], sem_in.at[t])
        load(probs_in.at[t], probs.at[t], sem_in.at[t])
        load(ctx_in.at[t], ctx.at[t], sem_in.at[t])
    load_weights(refs, where, full, sem)
    load(attn_in, total, sem_in.at[nt])
    turned_x[...] = x_ref[...].T
    turned_a[...] = attn_low[...].T

    def make(t):
        for held_in in (acts, ctx_grad, probs, ctx):
            wait(held_in.at[t], sem_in.at[t])
        attend_pull(acts, probs, ctx_grad, back, t)
        vec_ref[t] = jnp.sum(back[t].astype(F32), axis=0, keepdims=True)
        from_x = dot(turned_x[...], back[t])
        from_out = dot(turned_a[...], ctx[t])
        return jnp.concatenate(
            [from_x[:, :512], from_x[:, 512:] + from_out[:, :128], from_out[:, 128:]], axis=1
        ).astype(BF)

    done = each_grad(where_split, outs, make)(held, sem_out)
    wait(total, sem_in.at[nt])
    for t in range(nt):
        wait(full.at[t], sem.at[t])
        total[...] += dot_t(back[t], full[t, :, 0:640])
    half = total.shape[0] // 2
    input_a[...] = total[:half, :].astype(BF)
    input_b[...] = total[half:, :].astype(BF)
    vectors[...] = jnp.zeros_like(vectors)
    for at, ref in ((0, second_vec), (3, first_vec)):
        vectors[at : at + 3, :] = ref[0:3, :]
    for n in range(nt):
        vectors[6 + n : 7 + n, :] = inner_vec[n]
        sums, h = vec_ref[n], HEAD_DIM
        vectors[6 + nt + n : 7 + nt + n, 0 : 6 * h] = jnp.concatenate(
            [sums[:, : 2 * h], sums[:, 6 * h : 7 * h], sums[:, 4 * h : 6 * h], sums[:, 7 * h : 8 * h]], axis=1
        )
    sums = vectors[...]
    packs[...] = jnp.concatenate([sums, sums - sums.astype(BF).astype(F32)]).astype(BF)
    done()


def place_kernel(order, one, two, three, four, out, held, sem, sem_out):
    rows = one.shape[0]
    parts = (one, two, three, four)
    for n, part in enumerate(parts):
        load(part, held.at[n], sem.at[n])
    for n in range(4):
        wait(held.at[n], sem.at[n])
        spot = pl.ds(pl.multiple_of(order[n] * rows, rows), rows)
        pltpu.make_async_copy(held.at[n], out.at[spot], sem_out.at[n]).start()
    for n in range(4):
        wait(held.at[n], sem_out.at[n])


def widen_kernel(order, *rest):
    parts, (out, held, wide, sem, sem_out) = rest[:4], rest[-5:]
    half = parts[0].shape[0]
    for n, part in enumerate(parts):
        load(part, held.at[n], sem.at[n])
    for n in range(4):
        wait(held.at[n], sem.at[n])
        wide[n] = held[n].astype(F32)
        spot = pl.ds(pl.multiple_of((order[n // 2] * 2 + n % 2) * half, half), half)
        load(wide.at[n], out.at[spot], sem_out.at[n])
    for n in range(4):
        wait(wide.at[n], sem_out.at[n])


def interleave(q, k, v, o):
    h = HEAD_DIM
    return jnp.concatenate(
        [
            q[..., : 2 * h], k[..., : 2 * h], v[..., : 2 * h],
            q[..., 2 * h :], v[..., 2 * h :], k[..., 2 * h :], o[..., 2 * h :],
            o[..., : 2 * h],
        ],
        axis=-1,
    )


def interleave_kernel(q_in, k_in, v_in, o_in, out, q, k, v, o, sem):
    for n, (ref, held) in enumerate(((q_in, q), (k_in, k), (v_in, v), (o_in, o))):
        load(ref, held, sem.at[n])
    for n, held in enumerate((q, k, v, o)):
        wait(held, sem.at[n])
    out[...] = interleave(q[...].astype(F32), k[...].astype(F32), v[...].astype(F32), o[...].astype(F32).T).astype(BF)


def part_kernel(total, moved, q, k, v, o):
    grad = total[...] + moved[0 : total.shape[0], :].astype(F32)
    h = HEAD_DIM
    part = lambda *spans: jnp.concatenate([grad[:, a * h : b * h] for a, b in spans], axis=1)
    q[...] = part((0, 2), (6, 7))
    k[...] = part((2, 4), (8, 9))
    v[...] = part((4, 6), (7, 8))
    o[...] = part((10, 12), (9, 10)).T


def body(
    plan,
    inputs,
    segments,
    query_weight,
    key_weight,
    value_weight,
    query_bias,
    value_bias,
    out_weight,
    out_bias,
    first_gain,
    first_shift,
    inner_weight,
    inner_bias,
    outer_weight,
    outer_bias,
    second_gain,
    second_shift,
    cotangent,
):
    nt, ndp = plan.nt, plan.ndp
    width = inputs.shape[1]
    local, hidden = query_weight.shape[1], inner_weight.shape[1]
    rows = inputs.shape[0] // nt
    nseq = rows // LEN
    me = lax.axis_index("tensor")
    mine = lambda a, n: lax.dynamic_slice_in_dim(a, me * n, n, 0)
    x = mine(inputs, rows)
    cot = mine(cotangent, rows)
    seg_row = mine(segments, nseq)

    nw = 8 if plan.pieces else 1
    if plan.pieces:
        where, where_split = plan.tables(False), plan.tables(True)
    else:
        where = where_split = jnp.zeros((1, 1), jnp.int32)
    params = jnp.concatenate(
        [
            v.reshape(1, width)
            for v in (out_bias, first_gain, first_shift, outer_bias, second_gain, second_shift, out_bias, out_bias)
        ]
    )
    limit = 56
    LOW = 24 if rows <= 512 else 56
    weights = pltpu.VMEM((nt, width, hidden), BF)
    acted = pltpu.VMEM((nt, rows, hidden), BF)
    dma = pltpu.SemaphoreType.DMA
    any_w = [anywhere()] * nw
    shards = (
        call(
            interleave_kernel,
            [query_weight, key_weight, value_weight, out_weight],
            [anywhere()] * 4,
            [shape((query_weight.shape[0], 4 * local), BF)],
            [vmem()],
            [*[pltpu.VMEM(query_weight.shape, BF)] * 3, pltpu.VMEM(out_weight.shape, BF), dma((4,))],
            limit,
            1,
        )[0],
        inner_weight,
        outer_weight.T,
    )

    def attend(x, bias, attn_w):
        return call(
            functools.partial(attend_kernel, nw),
            [x, seg_row, bias, params, where, *attn_w],
            [vmem()] * 4 + [smem()] + any_w,
            [
                shape((nt, rows, 640), BF),
                shape((nt, nseq, 3, LEN, LEN), BF),
                shape((nt, rows, 256), BF),
                shape((rows, width), F32),
                shape((rows, 128), F32),
                shape((rows, width), BF),
            ],
            [anywhere()] * 3 + [vmem()] * 3,
            [
                weights,
                pltpu.VMEM((nseq, LEN, LEN), F32),
                pltpu.VMEM((nt, rows, 640), BF),
                pltpu.VMEM((nt, nseq, 3, LEN, LEN), BF),
                pltpu.VMEM((nt, rows, 256), BF),
                dma((nt,)),
                dma((3,)),
            ],
            limit,
            13,
        )

    def inner(low, inner_b, inner_w):
        return call(
            functools.partial(inner_kernel, nw),
            [low, inner_b, where_split, *inner_w],
            [vmem()] * 2 + [smem()] + any_w,
            [shape((nt, rows, hidden), BF)] * 2,
            [anywhere()] * 2,
            [weights, pltpu.VMEM((rows, hidden), F32), acted, acted, dma((nt,)), dma((2,))],
            limit,
            13,
        )

    if plan.pieces:
        slot = (plan.nz, width // ndp, hidden)
        grads = [shape((4, *slot), BF)] + [shape(slot, BF)] * 4
    else:
        grads = [shape((nt, width, hidden), BF)]
    ng = len(grads)
    wide, thin = pltpu.VMEM((rows, width), F32), pltpu.VMEM((rows, width), BF)

    def outer(active, normed, outer_w):
        return call(
            functools.partial(outer_kernel, nw, ng),
            [active, normed, cot, params, where, where_split, *outer_w],
            [anywhere()] * 3 + [vmem()] + [smem()] * 2 + any_w,
            [
                *grads,
                shape((rows, width), BF),
                shape((rows, width), F32),
                shape((rows, width), BF),
                shape((8, width), F32),
            ],
            [anywhere()] * (ng + 3) + [vmem()],
            [
                weights, acted, wide, thin, wide, thin, thin, pltpu.VMEM((width, rows), BF), weights,
                dma((nt,)), dma((nt,)), dma((2,)), dma((5,)),
            ],
            limit,
            14,
        )

    def middle(slope, second, ffn, low, normed, scale, outer_w, inner_w, attn_w):
        return call(
            functools.partial(middle_kernel, nw, ng),
            [slope, second, ffn, low, normed, scale, params, where, where_split, *outer_w, *inner_w, *attn_w],
            [anywhere()] * 6 + [vmem()] + [smem()] * 2 + any_w * 3,
            [
                *grads,
                shape((rows, width), F32),
                shape((rows, width), BF),
                shape((nt, rows, 256), BF),
                shape((8, width), F32),
                shape((nt, 1, hidden), F32),
            ],
            [anywhere()] * (ng + 3) + [vmem()] * 2,
            [
                weights, weights, pltpu.VMEM((nt, width, 256), BF), acted, wide,
                pltpu.VMEM((rows, 128), F32), thin, wide, wide, thin,
                pltpu.VMEM((width, rows), BF), acted, pltpu.VMEM((nt, rows, 256), BF), weights,
                dma((3, nt)), dma((nt,)), dma((5,)), dma((5,)),
            ],
            limit,
            0.1,
        )

    def attend_back(attn_low, acts, probs, ctx, ctx_grad, attn_in, vecs, attn_w):
        return call(
            functools.partial(attend_back_kernel, nw, ng),
            [x, attn_low, acts, probs, ctx, ctx_grad, attn_in, *vecs, where, where_split, *attn_w],
            [vmem()] * 2 + [anywhere()] * 5 + [vmem()] * 3 + [smem()] * 2 + any_w,
            [*grads, *[shape((rows // 2, width), BF)] * 2, shape((16, hidden), F32), shape((32, hidden), BF)],
            [anywhere()] * ng + [vmem()] * 4,
            [
                weights,
                pltpu.VMEM((rows, width), F32),
                pltpu.VMEM((nt, rows, 640), BF),
                pltpu.VMEM((nt, nseq, 3, LEN, LEN), BF),
                pltpu.VMEM((nt, rows, 256), BF),
                pltpu.VMEM((nt, rows, 256), BF),
                pltpu.VMEM((nt, rows, 640), BF),
                pltpu.VMEM((width, rows), BF),
                pltpu.VMEM((width, rows), BF),
                weights,
                pltpu.VMEM((nt, 1, 640), F32),
                dma((nt,)),
                dma((nt + 1,)),
                dma((2,)),
            ],
            limit,
            0.1,
        )

    def place(parts):
        order = jnp.stack([me, me ^ 2, me ^ 1, me ^ 3]).astype(jnp.int32)
        return call(
            place_kernel,
            [order, *parts],
            [smem()] + [anywhere()] * 4,
            [shape((nt * rows, width), BF)],
            [anywhere()],
            [pltpu.VMEM((4, rows, width), BF), dma((4,)), dma((4,))],
            limit,
            0.1,
        )[0]

    def widen(parts, flip, half=None):
        order = jnp.stack([me ^ flip, me ^ flip ^ 1]).astype(jnp.int32)
        more = [] if half is None else [half]
        return call(
            widen_kernel,
            [order, *parts, *more],
            [smem()] + [anywhere()] * (4 + len(more)),
            [shape((nt * rows, width), F32)],
            [anywhere()],
            [pltpu.VMEM((4, rows // 2, width), BF), pltpu.VMEM((4, rows // 2, width), F32), dma((4,)), dma((4,))],
            limit,
            0.1,
            {5: 0} if more else {},
        )[0]

    def small_parts():
        every = lax.all_gather(jnp.concatenate([query_bias, value_bias, inner_bias]), "tensor", axis=0)
        q_b, v_b = every[:, None, :local], every[:, None, local : 2 * local]
        none = jnp.zeros_like(q_b)
        return interleave(q_b, none, v_b, none), every[:, None, 2 * local :]

    bias, inner_b = small_parts()
    if plan.pieces:
        turn, one_way, other_way, core = plan.turn, plan.first(), plan.second(), plan.core()

        beside = plan.beside()

        def spread(own):
            return [turn(own, one_way), turn(own, other_way)]

        def cores(parts):
            return [turn(v, core) for v in parts]

        near = plan.near(shards[0])
        near, bias, inner_b, x, cot, seg_row, where, where_split, params = tie(
            (near, bias, inner_b, x, cot, seg_row, where, where_split, params)
        )
        own1 = jnp.stack([shards[0], *near])
        two1 = spread(own1)
        a2 = turn(tie(shards[1], own1), plan.step(False))
        own1_c = turn(own1, core)
        two1, a2, own1_c = tie((two1, a2, own1_c))
        both1 = turn(two1[0], other_way)
        cores1 = cores(two1)
        pair2 = jnp.stack([shards[1], a2])
        b2 = turn(pair2, plan.step(True))
        both1, cores1, b2 = tie((both1, cores1, b2))
        own2 = jnp.concatenate([pair2, b2])
        two2 = spread(own2)
        a3 = turn(tie(shards[2], own2), plan.step(False))
        own2_c = turn(own2, core)
        attn_w = [own1, *two1, both1, own1_c, *cores1, turn(both1, core)]
        acts, probs, ctx, normed, scale, low = attend(x, bias, attn_w)
        two2, a3, own2_c, low = tie((two2, a3, own2_c, low))
        both2 = turn(two2[0], other_way)
        cores2 = cores(two2)
        pair3 = jnp.stack([shards[2], a3])
        b3 = turn(pair3, plan.step(True))
        both2, cores2, b3 = tie((both2, cores2, b3))
        own3 = jnp.concatenate([pair3, b3])
        two3 = spread(own3)
        own3_c = turn(own3, core)
        inner_w = [own2, *two2, both2, own2_c, *cores2, turn(both2, core)]
        active, slope = inner(low, inner_b, inner_w)
        two3, own3_c, active = tie((two3, own3_c, active))
        both3 = turn(two3[0], other_way)
        cores3 = cores(two3)
        both3, cores3 = tie((both3, cores3))
        outer_w = [own3, *two3, both3, own3_c, *cores3, turn(both3, core)]
        keep3, *send3, layer_part, second, ffn, second_vec = outer(active, normed, outer_w)

        got3 = cores(send3)
        layer_x = turn(layer_part, beside)
        keep2, *send2, attn_in, attn_low, ctx_grad, first_vec, inner_vec = middle(
            slope, second, tie((ffn, send3))[0], low, normed, scale, outer_w, inner_w, attn_w
        )
        got3, layer_x, send2, ctx_grad = tie((got3, layer_x, send2, ctx_grad))
        away3 = plan.scatter_a(keep3, got3)
        got3a = turn(away3, one_way)
        got2 = cores(send2)
        layer_c = cores([layer_part, layer_x])
        got2, layer_c, ctx_grad = tie((got2, layer_c, ctx_grad))
        away2 = plan.scatter_a(keep2, got2)
        got2a = turn(away2, one_way)
        keep1, *send1, input_a, input_b, vectors, packs = attend_back(
            attn_low, acts, probs, ctx, tie((ctx_grad, away2))[0], attn_in, (second_vec, first_vec, inner_vec), attn_w
        )
        got1 = cores(send1)
        packed = 2 * vectors.shape[0]
        input_low = [input_a, input_b]
        got3a, got2a, got1, input_low, packs = tie((got3a, got2a, got1, input_low, packs))
        flat = (-1, hidden)
        away1 = plan.scatter_a(keep1, got1)
        away1 = jnp.concatenate([away1.reshape(flat), packs])
        got1a = turn(away1, one_way)
        left3 = tie((keep3, away1))[0][:2].astype(F32) + jnp.stack(got3[:2]).astype(F32) + got3a.astype(F32)
        half3 = turn(left3[:, 2:].astype(BF), plan.step(True))
        left = tie((keep2, left3))[0]
        away2 = plan.scatter_b(left, got2, got2a)
        got2b = turn(away2, other_way)
        input_c = cores(input_low)
        layer_out = place(tie(([layer_part, layer_x, *layer_c], away2))[0])
        half_grad = widen(tie(([*input_low, *input_c], layer_out))[0], 0)
        half3, got2b, half_grad, got1a = tie((half3, got2b, half_grad, got1a))
        vectors = vectors + unpack(got1a[-packed:])
        got1a = got1a[:-packed].reshape(2, *slot)
        away = plan.scatter_b(keep1, got1, got1a)
        away = jnp.concatenate([away.reshape(flat), pack(vectors)])
        got1b = turn(away, other_way)
        input_x = turn(tie((input_low[0], away))[0], beside)
        half3, got2b, away = tie((half3, got2b, away))
        left3 = left3[:, :2] + half3.astype(F32)
        quarter3 = turn(left3[:, 1].astype(BF), plan.step(False))
        left2 = plan.scatter_left(keep2, got2, got2a, got2b)
        half2 = plan.half_z(left2)
        quarter3, got1b, input_x = tie((quarter3, got1b, input_x))
        left3 = left3[:, 0] + quarter3.astype(F32)
        last3 = turn(left3[1].astype(BF), other_way)
        vectors = vectors + unpack(got1b[-packed:])
        got1b = got1b[:-packed].reshape(slot)
        left1 = plan.scatter_left(keep1, got1, got1a, got1b)
        away = jnp.concatenate([left1[2:].astype(BF).reshape(flat), pack(vectors)])
        half1 = turn(away, plan.step(True))
        input_y = turn(tie((input_low[1], left2))[0], beside)
        last3, half2, away = tie((last3, half2, away))
        left2 = left2[:2] + half2.astype(F32)
        quarter2 = plan.last_z(left2[1])
        outer_grad = left3[0] + last3.astype(F32)
        half1, outer_grad, input_y = tie((half1, outer_grad, input_y))
        vectors = vectors + unpack(half1[-packed:])
        half1 = half1[:-packed].reshape(2, -1, hidden)
        away = (left1[1] + half1[1].astype(F32)).astype(BF)
        away = jnp.concatenate([away, pack(vectors)])
        quarter1 = turn(away, plan.step(False))
        input_x = [input_x, input_y]
        input_xc = cores(input_x)
        input_grad = widen([*input_x, *input_xc], 2, half_grad)
        quarter1, quarter2, input_grad = tie((quarter1, quarter2, input_grad))
        inner_grad = left2[0] + quarter2.astype(F32)
        vectors = vectors + unpack(quarter1[-packed:])
        vectors = vectors + turn(vectors, core)
        attn_grads = call(
            part_kernel,
            [left1[0] + half1[0].astype(F32), quarter1],
            [vmem()] * 2,
            [shape((width // ndp, local), F32)] * 3 + [shape((local, width // ndp), F32)],
            [vmem()] * 4,
            [],
            16,
            1,
        )
    else:
        attn_w, inner_w, outer_w = (
            [lax.all_gather(lax.all_gather(s, "dp", axis=0, tiled=True), "tensor", axis=0)]
            for s in shards
        )
        acts, probs, ctx, normed, scale, low = attend(x, bias, attn_w)
        active, slope = inner(low, inner_b, inner_w)
        outer_g, layer_part, second, ffn, second_vec = outer(active, normed, outer_w)
        inner_g, attn_in, attn_low, ctx_grad, first_vec, inner_vec = middle(
            slope, second, ffn, low, normed, scale, outer_w, inner_w, attn_w
        )
        attn_g, input_a, input_b, vectors, _ = attend_back(
            attn_low, acts, probs, ctx, ctx_grad, attn_in, (second_vec, first_vec, inner_vec), attn_w
        )
        outer_grad, inner_grad, attn_g = (
            lax.psum_scatter(
                lax.psum_scatter(g, "tensor", scatter_dimension=0, tiled=False),
                "dp",
                scatter_dimension=0,
                tiled=True,
            ).astype(F32)
            for g in (outer_g, inner_g, attn_g)
        )
        layer_out = lax.all_gather(layer_part, "tensor", axis=0, tiled=True)
        input_low = jnp.concatenate([input_a, input_b])
        input_grad = lax.all_gather(input_low, "tensor", axis=0, tiled=True).astype(F32)

    if not plan.pieces:
        vectors = lax.psum(vectors, AXES)
    gain2, shift2, bias2, gain1, shift1, bias1 = (vectors[n] for n in range(6))
    inner_bias_grad = lax.dynamic_index_in_dim(vectors, 6 + me, 0, keepdims=False)
    mine_vec = lax.dynamic_index_in_dim(vectors, 6 + nt + me, 0, keepdims=False)
    query_bias_grad, value_bias_grad = mine_vec[:local], mine_vec[local : 2 * local]
    h = HEAD_DIM
    if not plan.pieces:
        part = lambda *spans: jnp.concatenate([attn_g[:, a * h : b * h] for a, b in spans], axis=1)
        attn_grads = part((0, 2), (6, 7)), part((2, 4), (8, 9)), part((4, 6), (7, 8)), part((10, 12), (9, 10)).T
    return (
        layer_out,
        input_grad,
        *attn_grads[:3],
        query_bias_grad,
        value_bias_grad,
        attn_grads[3],
        bias1,
        gain1,
        shift1,
        inner_grad,
        inner_bias_grad,
        outer_grad.T,
        bias2,
        gain2,
        shift2,
    )


def solution(mesh):
    in_specs = (
        P("dp", None),
        P("dp", None),
        P("dp", "tensor"),
        P("dp", "tensor"),
        P("dp", "tensor"),
        P("tensor"),
        P("tensor"),
        P("tensor", "dp"),
        P(),
        P(),
        P(),
        P("dp", "tensor"),
        P("tensor"),
        P("tensor", "dp"),
        P(),
        P(),
        P(),
        P("dp", None),
    )
    out_specs = (
        P("dp", None),
        P("dp", None),
        P("dp", "tensor"),
        P("dp", "tensor"),
        P("dp", "tensor"),
        P("tensor"),
        P("tensor"),
        P("tensor", "dp"),
        P(),
        P(),
        P(),
        P("dp", "tensor"),
        P("tensor"),
        P("tensor", "dp"),
        P(),
        P(),
        P(),
    )
    return jax.shard_map(
        functools.partial(body, Plan(mesh)),
        mesh=mesh,
        in_specs=in_specs,
        out_specs=out_specs,
        check_vma=False,
    )
```

```python
import functools
import math

import jax
import jax.numpy as jnp
from jax import lax
from jax.experimental import pallas as pl
from jax.experimental.pallas import tpu as pltpu
from jax.sharding import PartitionSpec as P

HEAD_DIM = 64
LEN = 256
EPS = 1e-06
BF = jnp.bfloat16
F32 = jnp.float32
AXES = ("dp", "tensor")
MIB = 1 << 20
SCALE = 0.6


def dot(left, right):
    return lax.dot_general(left, right, (((1,), (0,)), ((), ())), preferred_element_type=F32)


def dot_t(left, right):
    return lax.dot_general(left, right, (((1,), (1,)), ((), ())), preferred_element_type=F32)


def t_dot(left, right):
    return lax.dot_general(left, right, (((0,), (0,)), ((), ())), preferred_element_type=F32)


def vmem():
    return pl.BlockSpec(memory_space=pltpu.VMEM)


def smem():
    return pl.BlockSpec(memory_space=pltpu.SMEM)


def anywhere():
    return pl.BlockSpec(memory_space=pl.ANY)


def call(body, ins, in_specs, outs, out_specs, scratch, limit, cost, aliases={}):
    return pl.pallas_call(
        body,
        out_shape=outs,
        in_specs=in_specs,
        out_specs=out_specs,
        scratch_shapes=scratch,
        input_output_aliases=aliases,
        compiler_params=pltpu.CompilerParams(vmem_limit_bytes=limit * MIB),
        cost_estimate=pl.CostEstimate(flops=int(cost * SCALE * 1e9), bytes_accessed=1000, transcendentals=0),
    )(*ins)


def shape(dims, dtype):
    return jax.ShapeDtypeStruct(dims, dtype)


class Plan:
    def __init__(self, mesh):
        self.ndp, self.nt = mesh.shape["dp"], mesh.shape["tensor"]
        self.pieces = self.nt == 4 and self.ndp == 8
        self.nz = self.ndp // 2

    def pairs(self, move):
        found = []
        for d in range(self.ndp):
            for t in range(self.nt):
                z, y, x, c = move(d >> 1, d & 1, t >> 1, t & 1)
                found.append((d * self.nt + t, (z * 2 + y) * self.nt + x * 2 + c))
        return found

    def first(self):
        return self.pairs(lambda z, y, x, c: (z, y, x ^ 1, c) if c == 0 else (z, y ^ 1, x, c))

    def second(self):
        return self.pairs(lambda z, y, x, c: (z, y, x ^ 1, c) if c == 1 else (z, y ^ 1, x, c))

    def core(self):
        return self.pairs(lambda z, y, x, c: (z, y, x, c ^ 1))

    def along(self, j):
        return self.pairs(lambda z, y, x, c: (z ^ j, y, x, c))

    def step(self, last):
        return self.pairs(lambda z, y, x, c: (z ^ (1 if (c == 0) != last else 2), y, x, c))

    def tables(self, split):
        d, t = lax.axis_index("dp"), lax.axis_index("tensor")
        z, y, x, c = d >> 1, d & 1, t >> 1, t & 1
        s = jnp.arange(2)[:, None, None]
        r = jnp.arange(4)[None, :, None]
        j = jnp.arange(self.nz)[None, None, :]
        a, b = r & 1, r >> 1
        core = c ^ s
        dx, dy = jnp.where(core == 0, a, b), jnp.where(core == 0, b, a)
        if split:
            j = jnp.where(core == 0, j, (j & 1) * 2 + (j >> 1))
        where_t = jnp.broadcast_to((x ^ dx) * 2 + core, (2, 4, self.nz))
        where_d = jnp.broadcast_to((z ^ j) * 2 + (y ^ dy), (2, 4, self.nz))
        return jnp.stack([where_t.reshape(-1), where_d.reshape(-1)]).astype(jnp.int32)

    def turn(self, values, pairs):
        return lax.ppermute(values, AXES, pairs)

    def near(self, shard):
        return [self.turn(shard, self.along(j)) for j in range(1, self.nz)]

    def beside(self):
        return self.pairs(lambda z, y, x, c: (z, y, x ^ 1, c))

    def scatter_a(self, keep, got):
        return (keep[2:].astype(F32) + jnp.stack(got[2:]).astype(F32)).astype(BF)

    def scatter_b(self, keep, got, got_a):
        return (keep[1].astype(F32) + got[1].astype(F32) + got_a[1].astype(F32)).astype(BF)

    def scatter_left(self, keep, got, got_a, got_b):
        return keep[0].astype(F32) + got[0].astype(F32) + got_a[0].astype(F32) + got_b.astype(F32)

    def half_z(self, left):
        return self.turn(left[2:].astype(BF), self.step(True))

    def last_z(self, values):
        return self.turn(values.astype(BF), self.step(False))


def load_weights(refs, where, full, sem, start=0, before=0):
    columns = pl.ds(start, full.shape[2])
    if not refs:
        return
    if len(refs) == 1:
        for t in range(full.shape[0]):
            pltpu.make_async_copy(refs[0].at[t, :, columns], full.at[t], sem.at[t]).start()
        return
    nz, rows, _ = refs[0].shape
    for r, ref in enumerate(refs):
        for j in range(nz):
            n = (before + r) * nz + j
            t, d = where[0, n], where[1, n]
            spot = pl.ds(pl.multiple_of(d * rows, rows), rows)
            pltpu.make_async_copy(ref.at[j, :, columns], full.at[t, spot], sem.at[t]).start()


def load(ref, held, sem):
    pltpu.make_async_copy(ref, held, sem).start()


def wait(held, sem):
    pltpu.make_async_copy(held, held, sem).wait()


def blocks(rows, block):
    def over(run):
        @pl.loop(0, rows // block)
        def _(i):
            run(pl.ds(pl.multiple_of(i * block, block), block))

    return over


def pack(vectors):
    high = vectors.astype(BF)
    return jnp.concatenate([high, (vectors - high.astype(F32)).astype(BF)])


def unpack(rows):
    half = rows.shape[0] // 2
    return rows[:half].astype(F32) + rows[half:].astype(F32)


def tie(values, *after):
    if after:
        return lax.optimization_barrier((values, *after))[0]
    return lax.optimization_barrier(values)


def lane_masks(rows):
    lane = lax.broadcasted_iota(jnp.int32, (rows, 128), 1)
    return lane < HEAD_DIM


def pick(mask, values):
    return jnp.where(mask, values, jnp.zeros_like(values))


def norm_stats(hidden):
    center = hidden - jnp.mean(hidden, axis=-1, keepdims=True)
    scale = lax.rsqrt(jnp.mean(center * center, axis=-1, keepdims=True) + EPS)
    return center * scale, scale


def norm_pull(incoming, normed, scale, gain):
    scaled = incoming * gain
    return scale * (
        scaled
        - jnp.mean(scaled, axis=-1, keepdims=True)
        - normed * jnp.mean(scaled * normed, axis=-1, keepdims=True)
    )


def attend_kernel(nw, x_ref, seg_row, bias, params, where, *rest):
    refs, rest = rest[:nw], rest[nw:]
    acts_out, probs_out, ctx_out, normed_ref, scale_ref, low_ref = rest[:6]
    full, keep, acts, probs, ctx, sem, sem_out = rest[6:]
    rows = x_ref.shape[0]
    nt = acts.shape[0]
    load_weights(refs, where, full, sem)
    nseq = rows // LEN
    for s in range(nseq):
        own = seg_row[s : s + 1, :].astype(F32)
        same = jnp.broadcast_to(own, (8, LEN)).T[:, 0:1] == own
        keep[s] = jnp.where(same, 0.0, -1e30).astype(F32)
    low_half = lane_masks(LEN)
    ones = jnp.ones((LEN, 128), BF)

    normed_ref[...] = x_ref[...].astype(F32) + params[0:1, :]

    @pl.loop(0, nt)
    def _(t):
        wait(full.at[t], sem.at[t])
        x = x_ref[...]
        acts[t, :, 0:512] = (dot(x, full[t, :, 0:512]) + bias[t, :, 0:512]).astype(BF)
        last = dot(x, full[t, :, 512:640]).astype(BF)
        acts[t, :, 512:640] = pick(lane_masks(rows), last)

        for s in range(nseq):
            span = slice(s * LEN, (s + 1) * LEN)
            q01, k01, v01 = acts[t, span, 0:128], acts[t, span, 128:256], acts[t, span, 256:384]
            qv2, k2 = acts[t, span, 384:512], acts[t, span, 512:640]
            heads = (
                (pick(low_half, q01), k01, v01),
                (pick(~low_half, q01), k01, v01),
                (pick(low_half, qv2), k2, qv2),
            )
            done = []
            for h, (query, key, value) in enumerate(heads):
                scores = dot_t(query, key) * HEAD_DIM ** (-0.5) + keep[s]
                top = jnp.max(scores, axis=-1, keepdims=True)
                expo = jnp.exp(scores - top)
                low = expo.astype(BF)
                mixed = dot(low, jnp.concatenate([value, ones], axis=1))
                inverse = 1.0 / mixed[:, 128:]
                probs[t, s, h] = (expo * jnp.concatenate([inverse, inverse], axis=1)).astype(BF)
                done.append(mixed[:, :128] * inverse)
            ctx[t, span, 0:128] = pick(~low_half, done[2]).astype(BF)
            ctx[t, span, 128:256] = jnp.where(low_half, done[0], done[1]).astype(BF)
        pltpu.make_async_copy(acts.at[t], acts_out.at[t], sem_out.at[0]).start()
        pltpu.make_async_copy(probs.at[t], probs_out.at[t], sem_out.at[1]).start()
        pltpu.make_async_copy(ctx.at[t], ctx_out.at[t], sem_out.at[2]).start()
        part = dot_t(ctx[t], full[t, :, 512:768]).astype(BF)
        normed_ref[...] += part.astype(F32)

    @blocks(rows, 128)
    def _(span):
        normed, scale = norm_stats(normed_ref[span, :])
        normed_ref[span, :] = normed
        scale_ref[span, :] = jnp.broadcast_to(scale, (128, 128))
        low_ref[span, :] = (normed * params[1:2, :] + params[2:3, :]).astype(BF)

    wait(acts, sem_out.at[0])
    wait(probs, sem_out.at[1])
    wait(ctx, sem_out.at[2])


TAIL_STEP = 0.43 / math.sqrt(2.0)
TAIL = (
    0.12125730288161489,
    0.12218773837809233,
    0.1024754485844625,
    0.12342253549698744,
    -0.04286343715820851,
    0.19185342214732998,
    -0.15518700012679373,
    0.036854031729008835,
)


def normal_parts(values):
    t = 1.0 / (1.0 + TAIL_STEP * jnp.abs(values))
    bell = jnp.exp2(values * values * (-0.5 * math.log2(math.e)))
    poly = TAIL[-1]
    for c in TAIL[-2::-1]:
        poly = c + t * poly
    tail = t * poly * bell
    return jnp.where(values >= 0, 1.0 - tail, tail), bell


def inner_kernel(nw, low_ref, bias, where, *rest):
    refs, rest = rest[:nw], rest[nw:]
    active_out, slope_out, full, inner_ref, active, slope, sem, sem_out = rest
    rows = low_ref.shape[0]
    nt = active.shape[0]
    load_weights(refs, where, full, sem)

    @pl.loop(0, nt)
    def _(t):
        wait(full.at[t], sem.at[t])
        inner_ref[...] = dot(low_ref[...], full[t]) + bias[t]

        @blocks(rows, 64)
        def _(span):
            inner = inner_ref[span, :]
            phi, bell = normal_parts(inner)
            active[t, span, :] = (inner * phi).astype(BF)
            slope[t, span, :] = (phi + inner * bell * (1.0 / math.sqrt(2.0 * math.pi))).astype(BF)

        pltpu.make_async_copy(active.at[t], active_out.at[t], sem_out.at[0]).start()
        pltpu.make_async_copy(slope.at[t], slope_out.at[t], sem_out.at[1]).start()

    wait(active, sem_out.at[0])
    wait(slope, sem_out.at[1])


def turn_of(where, n):
    return 2 * (n % 2) + ((where[0, 0] % 2) ^ (1 - n // 2))


def store_grads(where, side, held, outs, sem):
    nz, rows = outs[0].shape[0], outs[0].shape[1]
    for r in range(4):
        for j in range(nz):
            n = (side * 4 + r) * nz + j
            t, d = where[0, n], where[1, n]
            spot = pl.ds(pl.multiple_of(d * rows, rows), rows)
            pltpu.make_async_copy(
                held.at[t // 2, spot], outs[(r & 1) * 2 + (r >> 1)].at[j], sem
            ).start()


def each_grad(where, outs, make):
    def over(held, sems):
        nt = held.shape[0]
        if len(outs) == 1:
            for n in range(nt):
                held[n] = make(n)
                load(held.at[n], outs[0].at[n], sems.at[0])
            return lambda: wait(held, sems.at[0])
        keep, send = outs[0], outs[1:]
        for n in range(nt):
            held[n] = make(turn_of(where, n))
            if n == 1:
                store_grads(where, 1, held.at[0:2], send, sems.at[0])
            if n == 3:
                store_grads(where, 0, held.at[2:4], [keep.at[r] for r in range(4)], sems.at[1])
        return lambda: [wait(held.at[2 * n : 2 * n + 2], sems.at[n]) for n in range(2)]

    return over


def outer_kernel(nw, ng, active_in, normed_in, cot_in, rows_in, where, where_split, *rest):
    refs, outs, rest = rest[:nw], rest[nw : nw + ng], rest[nw + ng :]
    out_part, second_out, ffn_out, vec_ref, full, active, normed_ref, cot, second, out_v, ffn = rest[:11]
    turned, held, sem, sem_a, sem_b, sem_out = rest[11:]
    rows = cot.shape[0]
    nt = active.shape[0]
    load_weights(refs[: nw // 2], where_split, full, sem)
    turns = [turn_of(where, n) for n in (2, 3, 0, 1)]
    for t in turns[:2]:
        load(active_in.at[t], active.at[t], sem_a.at[t])
    load_weights(refs[nw // 2 :], where_split, full, sem, 0, nw // 2)
    for t in turns[2:]:
        load(active_in.at[t], active.at[t], sem_a.at[t])
    load(normed_in, normed_ref, sem_b.at[0])
    load(cot_in, cot, sem_b.at[1])
    gain1, shift1, outer_bias, gain, shift = (rows_in[n : n + 1, :] for n in range(1, 6))
    vec_ref[...] = jnp.zeros_like(vec_ref)
    for n, t in enumerate(turns):
        wait(active.at[t], sem_a.at[t])
        wait(full.at[t], sem.at[t])
        part = dot_t(active[t], full[t]).astype(BF).astype(F32)
        second[...] = part if n == 0 else second[...] + part
    wait(normed_ref, sem_b.at[0])
    wait(cot, sem_b.at[1])

    @blocks(rows, 128)
    def _(span):
        first = normed_ref[span, :] * gain1 + shift1
        normed, scale = norm_stats(second[span, :] + outer_bias + first)
        out_v[span, :] = (normed * gain + shift).astype(BF)
        incoming = cot[span, :].astype(F32)
        pull = norm_pull(incoming, normed, scale, gain)
        second[span, :] = pull
        ffn[span, :] = pull.astype(BF)
        vec_ref[0:1, :] += jnp.sum(incoming * normed, axis=0, keepdims=True)
        vec_ref[1:2, :] += jnp.sum(incoming, axis=0, keepdims=True)
        vec_ref[2:3, :] += jnp.sum(pull, axis=0, keepdims=True)

    load(out_v, out_part, sem_out.at[2])
    load(second, second_out, sem_out.at[3])
    load(ffn, ffn_out, sem_out.at[4])
    turned[...] = ffn[...].T
    each_grad(where_split, outs, lambda t: dot(turned[...], active[t]).astype(BF))(held, sem_out)()
    wait(out_v, sem_out.at[2])
    wait(second, sem_out.at[3])
    wait(ffn, sem_out.at[4])


def middle_kernel(nw, ng, slope_in, second_in, ffn_in, low_in, normed_in, scale_in, rows_in, where, where_split, *rest):
    refs, inner_refs, attn_refs, rest = rest[:nw], rest[nw : 2 * nw], rest[2 * nw : 3 * nw], rest[3 * nw :]
    outs, rest = rest[:ng], rest[ng:]
    attn_in_out, attn_low_out, ctx_grad_out, vec_ref, inner_vec = rest[:5]
    full, inner_full, attn_full, slope, normed_ref, scale_ref, low, second, attn_in, ffn = rest[5:15]
    turned, pulled, ctx_grad, held, sem, sem_a, sem_b, sem_out = rest[15:]
    rows = low.shape[0]
    nt = slope.shape[0]
    load(ffn_in, ffn, sem_b.at[0])
    turns = [turn_of(where, n) for n in (2, 3, 0, 1)]
    load_weights(refs[: nw // 2], where_split, full, sem.at[0])
    for t in turns[:2]:
        load(slope_in.at[t], slope.at[t], sem_a.at[t])
    load_weights(refs[nw // 2 :], where_split, full, sem.at[0], 0, nw // 2)
    for t in turns[2:]:
        load(slope_in.at[t], slope.at[t], sem_a.at[t])
    load(low_in, low, sem_b.at[1])
    load_weights(inner_refs, where_split, inner_full, sem.at[1])
    load(second_in, second, sem_b.at[2])
    load(normed_in, normed_ref, sem_b.at[3])
    load(scale_in, scale_ref, sem_b.at[4])
    load_weights(attn_refs, where, attn_full, sem.at[2], 512)
    gain1 = rows_in[1:2, :]
    vec_ref[...] = jnp.zeros_like(vec_ref)
    wait(ffn, sem_b.at[0])
    for t in turns:
        wait(full.at[t], sem.at[0, t])
        wait(slope.at[t], sem_a.at[t])
        grad = (dot(ffn[...], full[t]) * slope[t].astype(F32)).astype(BF)
        pulled[t] = grad
        inner_vec[t] = jnp.sum(grad.astype(F32), axis=0, keepdims=True)
    wait(low, sem_b.at[1])
    turned[...] = low[...].T
    done = each_grad(where_split, outs, lambda t: dot(turned[...], pulled[t]).astype(BF))(held, sem_out)
    for t in range(nt):
        wait(inner_full.at[t], sem.at[1, t])
        part = dot_t(pulled[t], inner_full[t])
        attn_in[...] = part if t == 0 else attn_in[...] + part
    wait(second, sem_b.at[2])
    wait(normed_ref, sem_b.at[3])
    wait(scale_ref, sem_b.at[4])

    @blocks(rows, 128)
    def _(span):
        incoming = attn_in[span, :] + second[span, :]
        normed = normed_ref[span, :]
        grad = norm_pull(incoming, normed, scale_ref[span, 0:1], gain1)
        attn_in[span, :] = grad
        ffn[span, :] = grad.astype(BF)
        vec_ref[0:1, :] += jnp.sum(incoming * normed, axis=0, keepdims=True)
        vec_ref[1:2, :] += jnp.sum(incoming, axis=0, keepdims=True)
        vec_ref[2:3, :] += jnp.sum(grad, axis=0, keepdims=True)

    load(attn_in, attn_in_out, sem_out.at[2])
    load(ffn, attn_low_out, sem_out.at[3])
    low_half = lane_masks(rows)
    for t in range(nt):
        wait(attn_full.at[t], sem.at[2, t])
        got = dot(ffn[...], attn_full[t])
        ctx_grad[t, :, 0:128] = pick(~low_half, got[:, :128]).astype(BF)
        ctx_grad[t, :, 128:256] = got[:, 128:].astype(BF)
        load(ctx_grad.at[t], ctx_grad_out.at[t], sem_out.at[4])
    done()
    wait(attn_in, sem_out.at[2])
    wait(ffn, sem_out.at[3])
    wait(ctx_grad, sem_out.at[4])


def attend_pull(acts, probs, ctx_grad, back, t):
    rows = acts.shape[1]
    low_half = lane_masks(LEN)
    factor = HEAD_DIM ** (-0.5)
    h = HEAD_DIM
    for s in range(rows // LEN):
        span = slice(s * LEN, (s + 1) * LEN)
        q01, k01, v01 = acts[t, span, 0:128], acts[t, span, 128:256], acts[t, span, 256:384]
        qv2, k2 = acts[t, span, 384:512], acts[t, span, 512:640]
        g2, g01 = ctx_grad[t, span, 0:128], ctx_grad[t, span, 128:256]
        heads = (
            (pick(low_half, g01), k01, v01),
            (pick(~low_half, g01), k01, v01),
            (g2, k2, qv2),
        )
        queries, scores = [], []
        for n, (grad, key, value) in enumerate(heads):
            wide = probs[t, s, n].astype(F32)
            pulled = dot_t(grad, value)
            delta = jnp.sum(pulled * wide, axis=-1, keepdims=True)
            scores.append((wide * (pulled - delta)).astype(BF))
            queries.append(dot(scores[n], key) * factor)
        q01t, g01t, qv2t, g2t = q01.T, g01.T, qv2.T, g2.T
        keys01 = jnp.concatenate([dot(q01t[:h], scores[0]), dot(q01t[h:], scores[1])], axis=0) * factor
        values01 = jnp.concatenate([dot(g01t[:h], probs[t, s, 0]), dot(g01t[h:], probs[t, s, 1])], axis=0)
        both2 = jnp.concatenate([dot(qv2t[:h], scores[2]) * factor, dot(g2t[h:], probs[t, s, 2])], axis=0)
        kv2 = both2.astype(BF).T
        back[t, span, 0:128] = jnp.where(low_half, queries[0], queries[1]).astype(BF)
        back[t, span, 128:256] = keys01.astype(BF).T
        back[t, span, 256:384] = values01.astype(BF).T
        back[t, span, 384:512] = jnp.where(low_half, queries[2].astype(BF), kv2)
        back[t, span, 512:640] = pick(low_half, kv2)


def attend_back_kernel(nw, ng, x_ref, attn_low, acts_in, probs_in, ctx_in, ctx_grad_in, attn_in, *rest):
    second_vec, first_vec, inner_vec, where, where_split, *rest = rest
    refs, outs, (input_a, input_b, vectors, packs) = rest[:nw], rest[nw : nw + ng], rest[nw + ng : nw + ng + 4]
    full, total, acts, probs, ctx, ctx_grad, back, turned_x, turned_a, held, vec_ref = rest[nw + ng + 4 : -3]
    sem, sem_in, sem_out = rest[-3:]
    nt = acts.shape[0]
    for n in range(nt):
        t = turn_of(where, n) if ng > 1 else n
        load(acts_in.at[t], acts.at[t], sem_in.at[t])
        load(ctx_grad_in.at[t], ctx_grad.at[t], sem_in.at[t])
        load(probs_in.at[t], probs.at[t], sem_in.at[t])
        load(ctx_in.at[t], ctx.at[t], sem_in.at[t])
    load_weights(refs, where, full, sem)
    load(attn_in, total, sem_in.at[nt])
    turned_x[...] = x_ref[...].T
    turned_a[...] = attn_low[...].T

    def make(t):
        for held_in in (acts, ctx_grad, probs, ctx):
            wait(held_in.at[t], sem_in.at[t])
        attend_pull(acts, probs, ctx_grad, back, t)
        vec_ref[t] = jnp.sum(back[t].astype(F32), axis=0, keepdims=True)
        from_x = dot(turned_x[...], back[t])
        from_out = dot(turned_a[...], ctx[t])
        return jnp.concatenate(
            [from_x[:, :512], from_x[:, 512:] + from_out[:, :128], from_out[:, 128:]], axis=1
        ).astype(BF)

    done = each_grad(where_split, outs, make)(held, sem_out)
    wait(total, sem_in.at[nt])
    for t in range(nt):
        wait(full.at[t], sem.at[t])
        total[...] += dot_t(back[t], full[t, :, 0:640])
    half = total.shape[0] // 2
    input_a[...] = total[:half, :].astype(BF)
    input_b[...] = total[half:, :].astype(BF)
    vectors[...] = jnp.zeros_like(vectors)
    for at, ref in ((0, second_vec), (3, first_vec)):
        vectors[at : at + 3, :] = ref[0:3, :]
    for n in range(nt):
        vectors[6 + n : 7 + n, :] = inner_vec[n]
        sums, h = vec_ref[n], HEAD_DIM
        vectors[6 + nt + n : 7 + nt + n, 0 : 6 * h] = jnp.concatenate(
            [sums[:, : 2 * h], sums[:, 6 * h : 7 * h], sums[:, 4 * h : 6 * h], sums[:, 7 * h : 8 * h]], axis=1
        )
    sums = vectors[...]
    packs[...] = jnp.concatenate([sums, sums - sums.astype(BF).astype(F32)]).astype(BF)
    done()


def place_kernel(order, one, two, three, four, out, held, sem, sem_out):
    rows = one.shape[0]
    parts = (one, two, three, four)
    for n, part in enumerate(parts):
        load(part, held.at[n], sem.at[n])
    for n in range(4):
        wait(held.at[n], sem.at[n])
        spot = pl.ds(pl.multiple_of(order[n] * rows, rows), rows)
        pltpu.make_async_copy(held.at[n], out.at[spot], sem_out.at[n]).start()
    for n in range(4):
        wait(held.at[n], sem_out.at[n])


def widen_kernel(order, *rest):
    parts, (out, held, wide, sem, sem_out) = rest[:4], rest[-5:]
    half = parts[0].shape[0]
    for n, part in enumerate(parts):
        load(part, held.at[n], sem.at[n])
    for n in range(4):
        wait(held.at[n], sem.at[n])
        wide[n] = held[n].astype(F32)
        spot = pl.ds(pl.multiple_of((order[n // 2] * 2 + n % 2) * half, half), half)
        load(wide.at[n], out.at[spot], sem_out.at[n])
    for n in range(4):
        wait(wide.at[n], sem_out.at[n])


def interleave(q, k, v, o):
    h = HEAD_DIM
    return jnp.concatenate(
        [
            q[..., : 2 * h], k[..., : 2 * h], v[..., : 2 * h],
            q[..., 2 * h :], v[..., 2 * h :], k[..., 2 * h :], o[..., 2 * h :],
            o[..., : 2 * h],
        ],
        axis=-1,
    )


def interleave_kernel(q_in, k_in, v_in, o_in, out, q, k, v, o, sem):
    for n, (ref, held) in enumerate(((q_in, q), (k_in, k), (v_in, v), (o_in, o))):
        load(ref, held, sem.at[n])
    for n, held in enumerate((q, k, v, o)):
        wait(held, sem.at[n])
    out[...] = interleave(q[...].astype(F32), k[...].astype(F32), v[...].astype(F32), o[...].astype(F32).T).astype(BF)


def part_kernel(total, moved, q, k, v, o):
    grad = total[...] + moved[0 : total.shape[0], :].astype(F32)
    h = HEAD_DIM
    part = lambda *spans: jnp.concatenate([grad[:, a * h : b * h] for a, b in spans], axis=1)
    q[...] = part((0, 2), (6, 7))
    k[...] = part((2, 4), (8, 9))
    v[...] = part((4, 6), (7, 8))
    o[...] = part((10, 12), (9, 10)).T


def body(
    plan,
    inputs,
    segments,
    query_weight,
    key_weight,
    value_weight,
    query_bias,
    value_bias,
    out_weight,
    out_bias,
    first_gain,
    first_shift,
    inner_weight,
    inner_bias,
    outer_weight,
    outer_bias,
    second_gain,
    second_shift,
    cotangent,
):
    nt, ndp = plan.nt, plan.ndp
    width = inputs.shape[1]
    local, hidden = query_weight.shape[1], inner_weight.shape[1]
    rows = inputs.shape[0] // nt
    nseq = rows // LEN
    me = lax.axis_index("tensor")
    mine = lambda a, n: lax.dynamic_slice_in_dim(a, me * n, n, 0)
    x = mine(inputs, rows)
    cot = mine(cotangent, rows)
    seg_row = mine(segments, nseq)

    nw = 8 if plan.pieces else 1
    if plan.pieces:
        where, where_split = plan.tables(False), plan.tables(True)
    else:
        where = where_split = jnp.zeros((1, 1), jnp.int32)
    params = jnp.concatenate(
        [
            v.reshape(1, width)
            for v in (out_bias, first_gain, first_shift, outer_bias, second_gain, second_shift, out_bias, out_bias)
        ]
    )
    limit = 56
    LOW = 24 if rows <= 512 else 56
    weights = pltpu.VMEM((nt, width, hidden), BF)
    acted = pltpu.VMEM((nt, rows, hidden), BF)
    dma = pltpu.SemaphoreType.DMA
    any_w = [anywhere()] * nw
    shards = (
        call(
            interleave_kernel,
            [query_weight, key_weight, value_weight, out_weight],
            [anywhere()] * 4,
            [shape((query_weight.shape[0], 4 * local), BF)],
            [vmem()],
            [*[pltpu.VMEM(query_weight.shape, BF)] * 3, pltpu.VMEM(out_weight.shape, BF), dma((4,))],
            limit,
            1,
        )[0],
        inner_weight,
        outer_weight.T,
    )

    def attend(x, bias, attn_w):
        return call(
            functools.partial(attend_kernel, nw),
            [x, seg_row, bias, params, where, *attn_w],
            [vmem()] * 4 + [smem()] + any_w,
            [
                shape((nt, rows, 640), BF),
                shape((nt, nseq, 3, LEN, LEN), BF),
                shape((nt, rows, 256), BF),
                shape((rows, width), F32),
                shape((rows, 128), F32),
                shape((rows, width), BF),
            ],
            [anywhere()] * 3 + [vmem()] * 3,
            [
                weights,
                pltpu.VMEM((nseq, LEN, LEN), F32),
                pltpu.VMEM((nt, rows, 640), BF),
                pltpu.VMEM((nt, nseq, 3, LEN, LEN), BF),
                pltpu.VMEM((nt, rows, 256), BF),
                dma((nt,)),
                dma((3,)),
            ],
            limit,
            13,
        )

    def inner(low, inner_b, inner_w):
        return call(
            functools.partial(inner_kernel, nw),
            [low, inner_b, where_split, *inner_w],
            [vmem()] * 2 + [smem()] + any_w,
            [shape((nt, rows, hidden), BF)] * 2,
            [anywhere()] * 2,
            [weights, pltpu.VMEM((rows, hidden), F32), acted, acted, dma((nt,)), dma((2,))],
            limit,
            13,
        )

    if plan.pieces:
        slot = (plan.nz, width // ndp, hidden)
        grads = [shape((4, *slot), BF)] + [shape(slot, BF)] * 4
    else:
        grads = [shape((nt, width, hidden), BF)]
    ng = len(grads)
    wide, thin = pltpu.VMEM((rows, width), F32), pltpu.VMEM((rows, width), BF)

    def outer(active, normed, outer_w):
        return call(
            functools.partial(outer_kernel, nw, ng),
            [active, normed, cot, params, where, where_split, *outer_w],
            [anywhere()] * 3 + [vmem()] + [smem()] * 2 + any_w,
            [
                *grads,
                shape((rows, width), BF),
                shape((rows, width), F32),
                shape((rows, width), BF),
                shape((8, width), F32),
            ],
            [anywhere()] * (ng + 3) + [vmem()],
            [
                weights, acted, wide, thin, wide, thin, thin, pltpu.VMEM((width, rows), BF), weights,
                dma((nt,)), dma((nt,)), dma((2,)), dma((5,)),
            ],
            limit,
            14,
        )

    def middle(slope, second, ffn, low, normed, scale, outer_w, inner_w, attn_w):
        return call(
            functools.partial(middle_kernel, nw, ng),
            [slope, second, ffn, low, normed, scale, params, where, where_split, *outer_w, *inner_w, *attn_w],
            [anywhere()] * 6 + [vmem()] + [smem()] * 2 + any_w * 3,
            [
                *grads,
                shape((rows, width), F32),
                shape((rows, width), BF),
                shape((nt, rows, 256), BF),
                shape((8, width), F32),
                shape((nt, 1, hidden), F32),
            ],
            [anywhere()] * (ng + 3) + [vmem()] * 2,
            [
                weights, weights, pltpu.VMEM((nt, width, 256), BF), acted, wide,
                pltpu.VMEM((rows, 128), F32), thin, wide, wide, thin,
                pltpu.VMEM((width, rows), BF), acted, pltpu.VMEM((nt, rows, 256), BF), weights,
                dma((3, nt)), dma((nt,)), dma((5,)), dma((5,)),
            ],
            limit,
            0.1,
        )

    def attend_back(attn_low, acts, probs, ctx, ctx_grad, attn_in, vecs, attn_w):
        return call(
            functools.partial(attend_back_kernel, nw, ng),
            [x, attn_low, acts, probs, ctx, ctx_grad, attn_in, *vecs, where, where_split, *attn_w],
            [vmem()] * 2 + [anywhere()] * 5 + [vmem()] * 3 + [smem()] * 2 + any_w,
            [*grads, *[shape((rows // 2, width), BF)] * 2, shape((16, hidden), F32), shape((32, hidden), BF)],
            [anywhere()] * ng + [vmem()] * 4,
            [
                weights,
                pltpu.VMEM((rows, width), F32),
                pltpu.VMEM((nt, rows, 640), BF),
                pltpu.VMEM((nt, nseq, 3, LEN, LEN), BF),
                pltpu.VMEM((nt, rows, 256), BF),
                pltpu.VMEM((nt, rows, 256), BF),
                pltpu.VMEM((nt, rows, 640), BF),
                pltpu.VMEM((width, rows), BF),
                pltpu.VMEM((width, rows), BF),
                weights,
                pltpu.VMEM((nt, 1, 640), F32),
                dma((nt,)),
                dma((nt + 1,)),
                dma((2,)),
            ],
            limit,
            0.1,
        )

    def place(parts):
        order = jnp.stack([me, me ^ 2, me ^ 1, me ^ 3]).astype(jnp.int32)
        return call(
            place_kernel,
            [order, *parts],
            [smem()] + [anywhere()] * 4,
            [shape((nt * rows, width), BF)],
            [anywhere()],
            [pltpu.VMEM((4, rows, width), BF), dma((4,)), dma((4,))],
            limit,
            0.1,
        )[0]

    def widen(parts, flip, half=None):
        order = jnp.stack([me ^ flip, me ^ flip ^ 1]).astype(jnp.int32)
        more = [] if half is None else [half]
        return call(
            widen_kernel,
            [order, *parts, *more],
            [smem()] + [anywhere()] * (4 + len(more)),
            [shape((nt * rows, width), F32)],
            [anywhere()],
            [pltpu.VMEM((4, rows // 2, width), BF), pltpu.VMEM((4, rows // 2, width), F32), dma((4,)), dma((4,))],
            limit,
            0.1,
            {5: 0} if more else {},
        )[0]

    def small_parts():
        every = lax.all_gather(jnp.concatenate([query_bias, value_bias, inner_bias]), "tensor", axis=0)
        q_b, v_b = every[:, None, :local], every[:, None, local : 2 * local]
        none = jnp.zeros_like(q_b)
        return interleave(q_b, none, v_b, none), every[:, None, 2 * local :]

    bias, inner_b = small_parts()
    if plan.pieces:
        turn, one_way, other_way, core = plan.turn, plan.first(), plan.second(), plan.core()

        beside = plan.beside()

        def spread(own):
            return [turn(own, one_way), turn(own, other_way)]

        def cores(parts):
            return [turn(v, core) for v in parts]

        near = plan.near(shards[0])
        near, bias, inner_b, x, cot, seg_row, where, where_split, params = tie(
            (near, bias, inner_b, x, cot, seg_row, where, where_split, params)
        )
        own1 = jnp.stack([shards[0], *near])
        two1 = spread(own1)
        a2 = turn(tie(shards[1], own1), plan.step(False))
        own1_c = turn(own1, core)
        two1, a2, own1_c = tie((two1, a2, own1_c))
        both1 = turn(two1[0], other_way)
        cores1 = cores(two1)
        pair2 = jnp.stack([shards[1], a2])
        b2 = turn(pair2, plan.step(True))
        both1, cores1, b2 = tie((both1, cores1, b2))
        own2 = jnp.concatenate([pair2, b2])
        two2 = spread(own2)
        a3 = turn(tie(shards[2], own2), plan.step(False))
        own2_c = turn(own2, core)
        attn_w = [own1, *two1, both1, own1_c, *cores1, turn(both1, core)]
        acts, probs, ctx, normed, scale, low = attend(x, bias, attn_w)
        two2, a3, own2_c, low = tie((two2, a3, own2_c, low))
        both2 = turn(two2[0], other_way)
        cores2 = cores(two2)
        pair3 = jnp.stack([shards[2], a3])
        b3 = turn(pair3, plan.step(True))
        both2, cores2, b3 = tie((both2, cores2, b3))
        own3 = jnp.concatenate([pair3, b3])
        two3 = spread(own3)
        own3_c = turn(own3, core)
        inner_w = [own2, *two2, both2, own2_c, *cores2, turn(both2, core)]
        active, slope = inner(low, inner_b, inner_w)
        two3, own3_c, active = tie((two3, own3_c, active))
        both3 = turn(two3[0], other_way)
        cores3 = cores(two3)
        both3, cores3 = tie((both3, cores3))
        outer_w = [own3, *two3, both3, own3_c, *cores3, turn(both3, core)]
        keep3, *send3, layer_part, second, ffn, second_vec = outer(active, normed, outer_w)

        got3 = cores(send3)
        layer_x = turn(layer_part, beside)
        keep2, *send2, attn_in, attn_low, ctx_grad, first_vec, inner_vec = middle(
            slope, second, tie((ffn, send3))[0], low, normed, scale, outer_w, inner_w, attn_w
        )
        got3, layer_x, send2, ctx_grad = tie((got3, layer_x, send2, ctx_grad))
        away3 = plan.scatter_a(keep3, got3)
        got3a = turn(away3, one_way)
        got2 = cores(send2)
        layer_c = cores([layer_part, layer_x])
        got2, layer_c, ctx_grad = tie((got2, layer_c, ctx_grad))
        away2 = plan.scatter_a(keep2, got2)
        got2a = turn(away2, one_way)
        keep1, *send1, input_a, input_b, vectors, packs = attend_back(
            attn_low, acts, probs, ctx, tie((ctx_grad, away2))[0], attn_in, (second_vec, first_vec, inner_vec), attn_w
        )
        got1 = cores(send1)
        packed = 2 * vectors.shape[0]
        input_low = [input_a, input_b]
        got3a, got2a, got1, input_low, packs = tie((got3a, got2a, got1, input_low, packs))
        flat = (-1, hidden)
        away1 = plan.scatter_a(keep1, got1)
        away1 = jnp.concatenate([away1.reshape(flat), packs])
        got1a = turn(away1, one_way)
        left3 = tie((keep3, away1))[0][:2].astype(F32) + jnp.stack(got3[:2]).astype(F32) + got3a.astype(F32)
        half3 = turn(left3[:, 2:].astype(BF), plan.step(True))
        left = tie((keep2, left3))[0]
        away2 = plan.scatter_b(left, got2, got2a)
        got2b = turn(away2, other_way)
        input_c = cores(input_low)
        layer_out = place(tie(([layer_part, layer_x, *layer_c], away2))[0])
        half_grad = widen(tie(([*input_low, *input_c], layer_out))[0], 0)
        half3, got2b, half_grad, got1a = tie((half3, got2b, half_grad, got1a))
        vectors = vectors + unpack(got1a[-packed:])
        got1a = got1a[:-packed].reshape(2, *slot)
        away = plan.scatter_b(keep1, got1, got1a)
        away = jnp.concatenate([away.reshape(flat), pack(vectors)])
        got1b = turn(away, other_way)
        input_x = turn(tie((input_low[0], away))[0], beside)
        half3, got2b, away = tie((half3, got2b, away))
        left3 = left3[:, :2] + half3.astype(F32)
        quarter3 = turn(left3[:, 1].astype(BF), plan.step(False))
        left2 = plan.scatter_left(keep2, got2, got2a, got2b)
        half2 = plan.half_z(left2)
        quarter3, got1b, input_x = tie((quarter3, got1b, input_x))
        left3 = left3[:, 0] + quarter3.astype(F32)
        last3 = turn(left3[1].astype(BF), other_way)
        vectors = vectors + unpack(got1b[-packed:])
        got1b = got1b[:-packed].reshape(slot)
        left1 = plan.scatter_left(keep1, got1, got1a, got1b)
        away = jnp.concatenate([left1[2:].astype(BF).reshape(flat), pack(vectors)])
        half1 = turn(away, plan.step(True))
        input_y = turn(tie((input_low[1], left2))[0], beside)
        last3, half2, away = tie((last3, half2, away))
        left2 = left2[:2] + half2.astype(F32)
        quarter2 = plan.last_z(left2[1])
        outer_grad = left3[0] + last3.astype(F32)
        half1, outer_grad, input_y = tie((half1, outer_grad, input_y))
        vectors = vectors + unpack(half1[-packed:])
        half1 = half1[:-packed].reshape(2, -1, hidden)
        away = (left1[1] + half1[1].astype(F32)).astype(BF)
        away = jnp.concatenate([away, pack(vectors)])
        quarter1 = turn(away, plan.step(False))
        input_x = [input_x, input_y]
        input_xc = cores(input_x)
        input_grad = widen([*input_x, *input_xc], 2, half_grad)
        quarter1, quarter2, input_grad = tie((quarter1, quarter2, input_grad))
        inner_grad = left2[0] + quarter2.astype(F32)
        vectors = vectors + unpack(quarter1[-packed:])
        vectors = vectors + turn(vectors, core)
        attn_grads = call(
            part_kernel,
            [left1[0] + half1[0].astype(F32), quarter1],
            [vmem()] * 2,
            [shape((width // ndp, local), F32)] * 3 + [shape((local, width // ndp), F32)],
            [vmem()] * 4,
            [],
            16,
            1,
        )
    else:
        attn_w, inner_w, outer_w = (
            [lax.all_gather(lax.all_gather(s, "dp", axis=0, tiled=True), "tensor", axis=0)]
            for s in shards
        )
        acts, probs, ctx, normed, scale, low = attend(x, bias, attn_w)
        active, slope = inner(low, inner_b, inner_w)
        outer_g, layer_part, second, ffn, second_vec = outer(active, normed, outer_w)
        inner_g, attn_in, attn_low, ctx_grad, first_vec, inner_vec = middle(
            slope, second, ffn, low, normed, scale, outer_w, inner_w, attn_w
        )
        attn_g, input_a, input_b, vectors, _ = attend_back(
            attn_low, acts, probs, ctx, ctx_grad, attn_in, (second_vec, first_vec, inner_vec), attn_w
        )
        outer_grad, inner_grad, attn_g = (
            lax.psum_scatter(
                lax.psum_scatter(g, "tensor", scatter_dimension=0, tiled=False),
                "dp",
                scatter_dimension=0,
                tiled=True,
            ).astype(F32)
            for g in (outer_g, inner_g, attn_g)
        )
        layer_out = lax.all_gather(layer_part, "tensor", axis=0, tiled=True)
        input_low = jnp.concatenate([input_a, input_b])
        input_grad = lax.all_gather(input_low, "tensor", axis=0, tiled=True).astype(F32)

    if not plan.pieces:
        vectors = lax.psum(vectors, AXES)
    gain2, shift2, bias2, gain1, shift1, bias1 = (vectors[n] for n in range(6))
    inner_bias_grad = lax.dynamic_index_in_dim(vectors, 6 + me, 0, keepdims=False)
    mine_vec = lax.dynamic_index_in_dim(vectors, 6 + nt + me, 0, keepdims=False)
    query_bias_grad, value_bias_grad = mine_vec[:local], mine_vec[local : 2 * local]
    h = HEAD_DIM
    if not plan.pieces:
        part = lambda *spans: jnp.concatenate([attn_g[:, a * h : b * h] for a, b in spans], axis=1)
        attn_grads = part((0, 2), (6, 7)), part((2, 4), (8, 9)), part((4, 6), (7, 8)), part((10, 12), (9, 10)).T
    return (
        layer_out,
        input_grad,
        *attn_grads[:3],
        query_bias_grad,
        value_bias_grad,
        attn_grads[3],
        bias1,
        gain1,
        shift1,
        inner_grad,
        inner_bias_grad,
        outer_grad.T,
        bias2,
        gain2,
        shift2,
    )


def solution(mesh):
    in_specs = (
        P("dp", None),
        P("dp", None),
        P("dp", "tensor"),
        P("dp", "tensor"),
        P("dp", "tensor"),
        P("tensor"),
        P("tensor"),
        P("tensor", "dp"),
        P(),
        P(),
        P(),
        P("dp", "tensor"),
        P("tensor"),
        P("tensor", "dp"),
        P(),
        P(),
        P(),
        P("dp", None),
    )
    out_specs = (
        P("dp", None),
        P("dp", None),
        P("dp", "tensor"),
        P("dp", "tensor"),
        P("dp", "tensor"),
        P("tensor"),
        P("tensor"),
        P("tensor", "dp"),
        P(),
        P(),
        P(),
        P("dp", "tensor"),
        P("tensor"),
        P("tensor", "dp"),
        P(),
        P(),
        P(),
    )
    return jax.shard_map(
        functools.partial(body, Plan(mesh)),
        mesh=mesh,
        in_specs=in_specs,
        out_specs=out_specs,
        check_vma=False,
    )
```
